32 devices in a mesh: dp: 8 (over z, x), tensor: 4 (over y, core).
Axes of the slice: x: 2, y: 2, z: 4, core: 2. Of those that a mesh axis runs over, the one named last changes fastest.
Arguments:
- query_stream: bfloat16 [4, 8192, 512], P(None, 'dp'), may hold values from -6 to 6
- context_stream: bfloat16 [4, 8192, 512], P(None, 'dp'), may hold values from -6 to 6
- encoder_out: bfloat16 [4, 8192, 512], P(None, 'dp'), may hold values from -6 to 6
- query_masks: int32 [4, 4096, 128], P(None, 'dp'), may hold values from 0 to 1, as said below
- source_segments: int32 [4, 8, 1024], P(None, 'dp'), may hold values from 0 to 15, never falling along the last dimension, each value on 1 to 128 neighbouring positions
- out_grad: bfloat16 [4, 8192, 512], P(None, ('dp', 'tensor')), may hold values from -6 to 6
- self_query: bfloat16 [512, 512], P('dp', 'tensor'), may hold values from -0.25 to 0.25
- self_key_value: bfloat16 [2, 512, 512], P(None, 'dp', 'tensor'), may hold values from -0.25 to 0.25
- self_output: bfloat16 [512, 512], P('tensor', 'dp'), may hold values from -1.5 to 1.5
- cross_query: bfloat16 [512, 512], P('dp', 'tensor'), may hold values from -0.25 to 0.25
- cross_key_value: bfloat16 [2, 512, 512], P(None, 'dp', 'tensor'), may hold values from -0.25 to 0.25
- cross_output: bfloat16 [512, 512], P('tensor', 'dp'), may hold values from -2 to 2
- ffn_in: bfloat16 [512, 2048], P('dp'), may hold values from -0.25 to 0.25
- ffn_out: bfloat16 [2048, 512], P('dp'), may hold values from -0.1875 to 0.1875
- norm_gain: bfloat16 [3, 512], P(None, 'dp'), may hold values from 0.5 to 1.5
- norm_bias: bfloat16 [3, 512], P(None, 'dp'), may hold values from -3 to 3
Outputs:
- block_out: bfloat16 [4, 8192, 512], P(None, ('dp', 'tensor'))
- stream_grad: bfloat16 [4, 8192, 512], P(None, ('dp', 'tensor'))
- context_grad: bfloat16 [4, 8192, 512], P(None, ('dp', 'tensor'))
- encoder_grad: bfloat16 [4, 8192, 512], P(None, ('dp', 'tensor'))
- grad_self_query: float32 [512, 512], P('dp', 'tensor')
- grad_self_key_value: float32 [2, 512, 512], P(None, 'dp', 'tensor')
- grad_self_output: float32 [512, 512], P('tensor', 'dp')
- grad_cross_query: float32 [512, 512], P('dp', 'tensor')
- grad_cross_key_value: float32 [2, 512, 512], P(None, 'dp', 'tensor')
- grad_cross_output: float32 [512, 512], P('tensor', 'dp')
- grad_ffn_in: float32 [512, 2048], P('dp')
- grad_ffn_out: float32 [2048, 512], P('dp')
- grad_norm_gain: float32 [3, 512], P(None, 'dp')
- grad_norm_bias: float32 [3, 512], P(None, 'dp')
The draws below stay inside these ranges and needn't reach their ends.
Inputs may be any that keep to these rules, and one draw needn't show every extreme that they name: `query_masks`: token t of a micro-batch owns entries t * 64 to t * 64 + 63 of the flattened array, one for each position of its slot; the entry of its own position is 0 and at least one entry is 1. `source_segments`: along a row the numbers never fall, and every slot number has 1 to 128 encoder tokens, one exactly 128.
All inputs are finite; a program needn't handle non-finite values.
Results may differ from the reference program's by a relative error of at most 0.034.
Values may be sent and summed in bfloat16 or wider, within the bound.
A program may use at most 192 MiB of HBM per device.

```python
import math
import jax
import jax.numpy as jnp
import numpy as np
from jax import lax

D = 512
HEADS = 8
FF = 2048
HEAD_DIM = 64
SLOT = 64
ROW_LEN = 1024
ENC_LEN = 1024
MICRO = 4
MB_ROWS = 8
MB_TOKENS = 8192
MB_ENC = 8192
TOTAL_TOKENS = 32768
SLOTS = 16
SEG_MOST = 128
MASK_ROWS = 4096


def draw_query_masks(key, part):
    tokens = MICRO * MB_TOKENS
    first_key, second_key = jax.random.split(key)
    coins = jax.random.randint(first_key, (tokens, SLOT), 0, 2)
    offset = jax.random.randint(second_key, (tokens, 1), 1, SLOT)
    place = (jnp.arange(tokens, dtype=jnp.int32) % SLOT)[:, None]
    column = jnp.arange(SLOT, dtype=jnp.int32)[None, :]
    coins = jnp.where(column == place, 0, coins)
    coins = jnp.where(column == (place + offset) % SLOT, 1, coins)
    return coins.reshape(MICRO, MASK_ROWS, 128).astype(jnp.int32)


def steps_of(own_key, extent, cuts, smallest, high):
    factor_of, own = 1.0, jax.random.fold_in(own_key, 6)
    for dim, blocks in cuts:
        steps = jnp.exp(jax.random.uniform(jax.random.fold_in(own, dim), (blocks,), jnp.float32, smallest / len(cuts), high / len(cuts)))
        factor_of = factor_of * jnp.repeat(steps, extent[dim] // blocks).reshape([-1 if axis == dim else 1 for axis in range(len(extent))])
    return factor_of


def length_profile(amount, total, reach, slope):
    portions = [(1 << 20) // math.isqrt(grade ** slope) + 1 for grade in range(2, amount + 1)]
    spare, holding = total - reach - (amount - 1), [1] * (amount - 1)
    while spare > 0:
        candidates = [i for i in range(amount - 1) if holding[i] < reach]
        whole, left = sum([portions[i] for i in candidates]), spare
        for i in candidates:
            extra = min(reach - holding[i], max(1, left * portions[i] // whole), spare)
            holding[i] = holding[i] + extra
            spare = spare - extra
    return np.array([reach] + holding)


def uneven_parts(own_key, amount, total, most, skew):
    if amount == 2:
        one = jax.random.randint(own_key, (), max(1, total - most), min(most, total - 1) + 1)
        return jnp.stack([one, total - one])
    sizes = jnp.asarray(length_profile(amount, total, most, skew), jnp.int32)
    pairs = (amount - 1) // 2
    donor, receiver = sizes[1:1 + 2 * pairs:2], sizes[2:2 + 2 * pairs:2]
    room = jnp.minimum(donor - 1, most - receiver)
    moved = jax.random.randint(jax.random.fold_in(own_key, 1), (pairs,), 0, 1 << 20) % (room + 1)
    sizes = sizes.at[1:1 + 2 * pairs:2].set(donor - moved).at[2:2 + 2 * pairs:2].set(receiver + moved)
    return sizes[jax.random.permutation(jax.random.fold_in(own_key, 2), amount)]


def gaussian(key, shape, width, most, cuts=(), kind=jnp.bfloat16):
    level = steps_of(key, shape, cuts, -0.22, 0.18) if cuts else 1.0
    values = jax.random.normal(key, shape, jnp.float32) * width * level
    return jnp.minimum(jnp.maximum(values, -most), most).astype(kind)


def setup_inputs(seed: int = 0) -> dict:
    keys = jax.random.split(jax.random.key(seed), 17)
    query_stream = gaussian(keys[0], (MICRO, MB_TOKENS, D), 1.0, 6.0, ((1, 8),))
    context_stream = gaussian(keys[1], (MICRO, MB_TOKENS, D), 1.0, 6.0, ((1, 8),))
    encoder_out = gaussian(keys[2], (MICRO, MB_ENC, D), 1.0, 6.0, ((1, 8),))
    query_masks = draw_query_masks(jax.random.fold_in(keys[16], 71), 0)
    source_segments = jax.vmap(lambda own: jnp.searchsorted(jnp.cumsum(uneven_parts(own, SLOTS, ENC_LEN, SEG_MOST, 0)), jnp.arange(ENC_LEN), side="right"))(jax.random.split(keys[4], MICRO * MB_ROWS)).reshape((MICRO, MB_ROWS, ENC_LEN)).astype(jnp.int32)
    out_grad = gaussian(keys[5], (MICRO, MB_TOKENS, D), 1.0, 6.0, ((1, 32),))
    self_query = gaussian(keys[6], (D, D), D ** -0.5, 0.25, ((0, 8), (1, 4)))
    self_key_value = gaussian(keys[7], (2, D, D), D ** -0.5, 0.25, ((1, 8), (2, 4)))
    self_output = gaussian(keys[8], (D, D), (D * 2 // SLOT) ** -0.5, 1.5, ((0, 4), (1, 8)))
    cross_query = gaussian(keys[9], (D, D), D ** -0.5, 0.25, ((0, 8), (1, 4)))
    cross_key_value = gaussian(keys[10], (2, D, D), D ** -0.5, 0.25, ((1, 8), (2, 4)))
    cross_output = gaussian(keys[11], (D, D), (D * SLOTS // ENC_LEN) ** -0.5, 2.0, ((0, 4), (1, 8)))
    ffn_in = gaussian(keys[12], (D, FF), D ** -0.5, 0.25, ((0, 8),))
    ffn_out = gaussian(keys[13], (FF, D), (FF // 2) ** -0.5, 0.1875, ((0, 8),))
    norm_gain = jnp.clip(1.0 + 0.1 * jax.random.normal(keys[14], (3, D), jnp.float32), 0.5, 1.5).astype(jnp.bfloat16)
    norm_bias = gaussian(keys[15], (3, D), 0.3, 3.0, ((1, 8),))
    return dict(query_stream=query_stream, context_stream=context_stream, encoder_out=encoder_out, query_masks=query_masks, source_segments=source_segments, out_grad=out_grad, self_query=self_query, self_key_value=self_key_value, self_output=self_output, cross_query=cross_query, cross_key_value=cross_key_value, cross_output=cross_output, ffn_in=ffn_in, ffn_out=ffn_out, norm_gain=norm_gain, norm_bias=norm_bias)


epsilon = 1e-05
neg_fill = -1e+30
exact = lax.Precision.HIGHEST
gelu_coef = 0.7978845608028654
gelu_cube = 0.044715

@jax.custom_vjp
def low(v):
    return lax.optimization_barrier(v.astype(jnp.bfloat16)).astype(jnp.float32)

@jax.custom_vjp
def low_back(v):
    return v

def low_keep(v):
    return (low(v), None)

def low_pass(kept, grad):
    return (grad,)

def back_keep(v):
    return (v, None)

def back_low(kept, grad):
    return (low(grad),)
low.defvjp(low_keep, low_pass)
low_back.defvjp(back_keep, back_low)

def smooth_gate(value):
    return 0.5 * value * (1.0 + jnp.tanh(gelu_coef * (value + gelu_cube * value * value * value)))

def layer_norm(value, gain, bias):
    center = lax.optimization_barrier(jnp.mean(value, axis=-1, keepdims=True))
    shifted = value - center
    factor = lax.rsqrt(lax.optimization_barrier(jnp.mean(shifted * shifted, axis=-1, keepdims=True)) + epsilon)
    return shifted * factor * gain + bias

def split_heads(value):
    return value.reshape(value.shape[0], value.shape[1], HEADS, HEAD_DIM)

def attention(queries, key_rows, value_rows, allowed):
    scores = low_back(jnp.einsum('gqhe,gkhe->ghqk', queries, key_rows, precision=exact) * HEAD_DIM ** (-0.5))
    scores = jnp.where(allowed[:, None], scores, neg_fill)
    row_top = lax.optimization_barrier(jnp.max(scores, axis=-1, keepdims=True))
    summed = lax.optimization_barrier(jnp.sum(jnp.exp(scores - row_top), axis=-1, keepdims=True))
    probs = low(jnp.exp(scores - (row_top + jnp.log(summed))))
    return jnp.einsum('ghqk,gkhe->gqhe', probs, value_rows, precision=exact)

def project(value, weight):
    return jnp.einsum('gtd,de->gte', value, weight, precision=exact)

def layer_rows(params, stream, context, source, bits, segments):
    w_query, w_pair, w_out, c_query, c_pair, c_out, f_in, f_out, gains, biases = params
    group_size, length, model_width = stream.shape
    position = jnp.arange(length, dtype=jnp.int32)
    slot_of = position // SLOT
    seen = jnp.tile(bits, (1, 1, length // SLOT)) == 1
    allowed_self = seen & (slot_of[:, None] == slot_of[None, :])[None]
    allowed_cross = segments[:, None, :] == slot_of[None, :, None]
    query_self = low(low_back(project(stream, w_query)))
    key_self = low(low_back(project(context, w_pair[0])))
    value_self = low(low_back(project(context, w_pair[1])))
    mixed = attention(split_heads(query_self), split_heads(key_self), split_heads(value_self), allowed_self)
    mixed = low(low_back(mixed.reshape(group_size, length, model_width)))
    attn_self = low_back(project(mixed, w_out))
    first = layer_norm(stream + attn_self, gains[0], biases[0])
    query_cross = low(low_back(project(low(first), c_query)))
    key_cross = low(low_back(project(source, c_pair[0])))
    value_cross = low(low_back(project(source, c_pair[1])))
    mixed_cross = attention(split_heads(query_cross), split_heads(key_cross), split_heads(value_cross), allowed_cross)
    mixed_cross = low(low_back(mixed_cross.reshape(group_size, length, model_width)))
    attn_cross = low_back(project(mixed_cross, c_out))
    second = layer_norm(first + attn_cross, gains[1], biases[1])
    inner = low_back(project(low(second), f_in))
    hidden = low(smooth_gate(inner))
    ffn_value = low_back(project(hidden, f_out))
    return layer_norm(second + ffn_value, gains[2], biases[2])

def reference(query_stream, context_stream, encoder_out, query_masks, source_segments, out_grad, self_query, self_key_value, self_output, cross_query, cross_key_value, cross_output, ffn_in, ffn_out, norm_gain, norm_bias):
    all_rows = MICRO * MB_ROWS
    group_size = 2
    steps_count = all_rows // group_size

    def split_rows(value, length):
        return value.astype(jnp.float32).reshape(steps_count, group_size, length, D)
    streams = split_rows(query_stream, ROW_LEN)
    contexts = split_rows(context_stream, ROW_LEN)
    sources = split_rows(encoder_out, ENC_LEN)
    cotangents = split_rows(out_grad, ROW_LEN)
    bit_rows = query_masks.reshape(steps_count, group_size, ROW_LEN, SLOT)
    segment_rows = source_segments.reshape(steps_count, group_size, ENC_LEN)
    params = tuple((item.astype(jnp.float32) for item in (self_query, self_key_value, self_output, cross_query, cross_key_value, cross_output, ffn_in, ffn_out, norm_gain, norm_bias)))

    def step(totals, block_items):
        stream, context, source, cotangent, bits, segments = block_items

        def forward(weights, stream_in, context_in, source_in):
            return layer_rows(weights, stream_in, context_in, source_in, bits, segments)
        result, pullback = jax.vjp(forward, params, stream, context, source)
        weight_grads, d_stream, d_context, d_source = pullback(cotangent)
        totals = jax.tree.map(lambda left, right: left + right, totals, weight_grads)
        return (totals, (result, d_stream, d_context, d_source))
    zeros = jax.tree.map(lambda item: jnp.zeros(item.shape, jnp.float32), params)
    totals, (results, d_streams, d_contexts, d_sources) = lax.scan(step, zeros, (streams, contexts, sources, cotangents, bit_rows, segment_rows))
    grad_scale = float(TOTAL_TOKENS) ** (-0.5)
    totals = tuple((item * grad_scale for item in totals))
    block_out = results.reshape(MICRO, MB_TOKENS, D).astype(jnp.bfloat16)
    stream_grad = d_streams.reshape(MICRO, MB_TOKENS, D).astype(jnp.bfloat16)
    context_grad = d_contexts.reshape(MICRO, MB_TOKENS, D).astype(jnp.bfloat16)
    encoder_grad = d_sources.reshape(MICRO, MB_ENC, D).astype(jnp.bfloat16)
    return (block_out, stream_grad, context_grad, encoder_grad, totals[0], totals[1], totals[2], totals[3], totals[4], totals[5], totals[6], totals[7], totals[8], totals[9])
```

```python
import functools

import jax
import jax.numpy as jnp
from jax import lax
from jax.experimental import pallas as pl
from jax.experimental.pallas import tpu as pltpu
from jax.sharding import PartitionSpec as P

HEAD_DIM = 64
SLOT = 64
SEG_MOST = 128
QUAD = 4 * HEAD_DIM
PAIR = 2 * HEAD_DIM
NZ, NX, NY, NC = 4, 2, 2, 2
SELF, CROSS, UP, DOWN = 0, 4, 8, 12
BF16 = jnp.bfloat16
F32 = jnp.float32
MESH = pl.DeviceIdType.MESH

epsilon = 1e-05
neg_fill = -1e30
gelu_coef = 0.7978845608028654
gelu_cube = 0.044715
VMEM_LIMIT = 65400 * 1024


def mm(left, right):
    return jnp.dot(left, right, preferred_element_type=F32)


def mm_nt(left, right):
    return lax.dot_general(left, right, (((1,), (1,)), ((), ())), preferred_element_type=F32)


def mm_tn(left, right):
    return lax.dot_general(left, right, (((0,), (0,)), ((), ())), preferred_element_type=F32)


def norm_forward(value, gain, bias):
    center = jnp.mean(value, axis=-1, keepdims=True)
    shifted = value - center
    factor = lax.rsqrt(jnp.mean(shifted * shifted, axis=-1, keepdims=True) + epsilon)
    normed = shifted * factor
    return normed * gain + bias, normed, factor


def norm_backward(incoming, normed, factor, gain):
    scaled = incoming * gain
    inside = (
        scaled
        - jnp.mean(scaled, axis=-1, keepdims=True)
        - normed * jnp.mean(scaled * normed, axis=-1, keepdims=True)
    )
    return (
        factor * inside,
        jnp.sum(incoming * normed, axis=0, keepdims=True),
        jnp.sum(incoming, axis=0, keepdims=True),
    )


def columns(r, kind):
    parts = [r.w[kind, t // NC, t % NC].reshape(-1, 128) for t in range(NY * NC)]
    return jnp.concatenate(parts, axis=1)


def ffn_columns(r, j):
    parts = [r.w[UP + k, j // NC, j % NC].reshape(-1, 128) for k in range(4)]
    return jnp.concatenate(parts, axis=1)


def ffn_rows(r, j):
    parts = []
    for t in range(NY * NC):
        rows = [r.w[DOWN + k, t // NC, t % NC, j, b] for b in range(NX) for k in range(4)]
        parts.append(jnp.concatenate(rows, axis=0))
    return jnp.concatenate(parts, axis=1)


def grad_place(r, kind):
    if kind >= UP:
        return r.g_ffn, kind - UP
    return r.w, kind + UP


def store_columns(r, value, kind):
    ref, at = grad_place(r, kind)
    for t in range(NY * NC):
        ref[at, t // NC, t % NC] = value[:, t * 128 : (t + 1) * 128].reshape(NZ, NX, -1, 128)


def head_marks():
    lane = lax.broadcasted_iota(jnp.int32, (1, QUAD), 1) // HEAD_DIM
    return [jnp.where(lane == h, 1.0, 0.0).astype(BF16) for h in range(4)]


def spread_heads(rows, marks):
    return jnp.concatenate([rows * mark for mark in marks], axis=0)


def fold_pairs(weights, rows):
    first = lax.broadcasted_iota(jnp.int32, (SLOT, PAIR), 1) < HEAD_DIM
    parts = []
    for p in range(2):
        cut = slice(p * PAIR, (p + 1) * PAIR)
        full = mm_tn(weights[:, cut], rows[:, cut])
        parts.append(jnp.where(first, full[:SLOT], full[SLOT:]))
    return jnp.concatenate(parts, axis=1)


def soft_keys(scores, allowed):
    scores = jnp.where(allowed, scores, neg_fill)
    top = jnp.max(scores, axis=0, keepdims=True)
    raised = jnp.exp(scores - top)
    return (raised * (1.0 / jnp.sum(raised, axis=0, keepdims=True))).astype(BF16)


def attend_back(probs, keys, values, queries, d_mixed, marks):
    d_spread = spread_heads(d_mixed, marks)
    d_probs = mm_nt(values, d_spread)
    wide = probs.astype(F32)
    inner = jnp.sum(wide * d_probs, axis=0, keepdims=True)
    d_scores = (wide * (d_probs - inner)).astype(BF16)
    d_values = mm(probs, d_spread).astype(BF16)
    d_keys = mm(d_scores, spread_heads(queries, marks)).astype(BF16)
    d_queries = (fold_pairs(d_scores, keys) * HEAD_DIM ** (-0.5)).astype(BF16)
    return d_queries, d_keys, d_values


class Refs:
    pass


def frame_rows(share):
    return (share // SLOT) * SEG_MOST + 16


def window_rows():
    return SEG_MOST + 16


def window_table(starts, share, enc_len):
    frame, wide = frame_rows(share), window_rows()
    base = jnp.minimum(starts[:, :1] // 16 * 16, enc_len - frame)
    begin = starts[:, :-1] - base
    at = jnp.minimum(begin // 16 * 16, frame - wide)
    low = begin - at
    high = low + starts[:, 1:] - starts[:, :-1]
    return jnp.concatenate(
        [base // 16, (enc_len - frame - base) // 16, at // 16, low, high, (frame - wide - at) // 16],
        axis=1,
    )


def frame_start(r, m):
    return r.table[m, 0] * 16


def slot_window(r, m, s):
    at = r.table[m, 2 + s] * 16
    return at, r.table[m, 2 + r.slots + s], r.table[m, 2 + 2 * r.slots + s]


def slot_shift(r, m, s):
    return r.table[m, 2 + 3 * r.slots + s] * 16


def forward_self(r, m):
    marks = head_marks()
    stream, context = r.stream[m], r.context[m]
    queries = (mm(stream, columns(r, SELF + 0)) * HEAD_DIM ** (-0.5)).astype(BF16)
    keys = mm(context, columns(r, SELF + 1)).astype(BF16)
    values = mm(context, columns(r, SELF + 2)).astype(BF16)
    r.q_self[m], r.k_self[m], r.v_self[m] = queries, keys, values
    row = lax.broadcasted_iota(jnp.int32, (SLOT, QUAD), 0)
    lane = lax.broadcasted_iota(jnp.int32, (SLOT, QUAD), 1) % SLOT
    place = jnp.where(lane == 2 * (row % 32) + row // 32, 1.0, 0.0).astype(BF16)
    mixed = []
    for s in range(r.slots):
        rows = slice(s * SLOT, (s + 1) * SLOT)
        bits = r.masks[m, s * 32 : (s + 1) * 32].astype(F32)
        bits = jnp.concatenate([bits[:, :SLOT], bits[:, SLOT:]], axis=0).astype(BF16)
        allowed = mm_tn(bits, place) > 0.5
        halves = []
        for g in range(r.quads):
            cut = slice(g * QUAD, (g + 1) * QUAD)
            scores = mm_nt(keys[rows, cut], spread_heads(queries[rows, cut], marks))
            probs = soft_keys(scores, allowed)
            r.p_self[m, s, g] = probs
            halves.append(fold_pairs(probs, values[rows, cut]).astype(BF16))
        mixed.append(jnp.concatenate(halves, axis=1))
    mixed = jnp.concatenate(mixed, axis=0)
    r.mixed_self[m] = mixed
    attn = mm_nt(mixed, columns(r, SELF + 3))
    first, normed, factor = norm_forward(
        stream.astype(F32) + attn, r.norms[0:1, :], r.norms[3:4, :]
    )
    r.residual[m], r.factor[m, :, 0:1] = first, factor
    r.normed1[m] = normed.astype(BF16)
    r.first_low[m] = first.astype(BF16)


def forward_cross(r, m):
    marks = head_marks()
    base = frame_start(r, m)
    source = r.big1[m, pl.ds(base, r.frame), :]
    r.source[m] = source
    r.k_cross[m] = mm(source, columns(r, CROSS + 1)).astype(BF16)
    r.v_cross[m] = mm(source, columns(r, CROSS + 2)).astype(BF16)
    queries = (mm(r.first_low[m], columns(r, CROSS + 0)) * HEAD_DIM ** (-0.5)).astype(BF16)
    r.q_cross[m] = queries
    wide = window_rows()
    row = lax.broadcasted_iota(jnp.int32, (wide, QUAD), 0)
    mixed = []
    for s in range(r.slots):
        rows = slice(s * SLOT, (s + 1) * SLOT)
        at, low, high = slot_window(r, m, s)
        allowed = (row >= low) & (row < high)
        halves = []
        for g in range(r.quads):
            cut = slice(g * QUAD, (g + 1) * QUAD)
            keys = r.k_cross[m, pl.ds(at, wide), cut]
            values = r.v_cross[m, pl.ds(at, wide), cut]
            scores = mm_nt(keys, spread_heads(queries[rows, cut], marks))
            probs = soft_keys(scores, allowed)
            r.p_cross[m, s, g] = probs
            halves.append(fold_pairs(probs, values).astype(BF16))
        mixed.append(jnp.concatenate(halves, axis=1))
    mixed = jnp.concatenate(mixed, axis=0)
    r.mixed_cross[m] = mixed
    attn = mm_nt(mixed, columns(r, CROSS + 3))
    second, normed, factor = norm_forward(
        r.residual[m] + attn, r.norms[1:2, :], r.norms[4:5, :]
    )
    r.residual[m], r.factor[m, :, 1:2] = second, factor
    r.normed2[m] = normed.astype(BF16)
    r.second_low[m] = second.astype(BF16)


def feed_forward(r, m):
    second = r.residual[m]
    low = r.second_low[m]
    rows = pl.ds(pl.multiple_of(m * r.share, r.share), r.share)
    total = second
    for j in range(4):
        inner = mm(low, ffn_columns(r, j))
        square = inner * inner
        bent = jnp.tanh(gelu_coef * inner * (1.0 + gelu_cube * square))
        half = 0.5 * (1.0 + bent)
        hidden = (inner * half).astype(BF16)
        r.big1[j, rows, :] = hidden
        slope = half + 0.5 * inner * (1.0 - bent * bent) * gelu_coef * (
            1.0 + 3.0 * gelu_cube * square
        )
        r.shifted[j * r.share : (j + 1) * r.share, :] = slope.astype(BF16)
        total = total + mm(hidden, ffn_rows(r, j))
    result, normed, factor = norm_forward(total, r.norms[2:3, :], r.norms[5:6, :])
    r.d_first[m] = result.astype(BF16)
    d_third, gain, bias = norm_backward(
        r.cotangent[m].astype(F32), normed, factor, r.norms[2:3, :]
    )
    r.sums[2:3, :] += gain
    r.sums[5:6, :] += bias
    d_low = d_third.astype(BF16)
    r.d_third[m] = d_low
    d_second = d_third
    for j in range(4):
        slope = r.shifted[j * r.share : (j + 1) * r.share, :].astype(F32)
        d_inner = (mm_nt(d_low, ffn_rows(r, j)) * slope).astype(BF16)
        r.big2[j, rows, :] = d_inner
        d_second = d_second + mm_nt(d_inner, ffn_columns(r, j))
    d_cross, gain, bias = norm_backward(d_second, r.normed2[m].astype(F32), r.factor[m, :, 1:2], r.norms[1:2, :])
    r.sums[1:2, :] += gain
    r.sums[4:5, :] += bias
    r.residual[m] = d_cross
    r.d_second[m] = d_cross.astype(BF16)


def tokens(ref):
    value = ref[...]
    return value.reshape(-1, value.shape[-1])


def ffn_grads(r, j):
    up = mm_tn(tokens(r.second_low), r.big2[j]).astype(BF16)
    for k in range(4):
        r.g_ffn[k, j // NC, j % NC] = up[:, k * 128 : (k + 1) * 128].reshape(NZ, NX, -1, 128)
    down = mm_tn(tokens(r.d_third), r.big1[j]).astype(BF16)
    for t in range(NY * NC):
        for i in range(2):
            for b in range(NX):
                for n in range(2):
                    r.g_ffn[4 + 2 * i + n, t // NC, t % NC, j, b] = down[
                        t * 128 + i * 64 : t * 128 + (i + 1) * 64,
                        b * 256 + n * 128 : b * 256 + (n + 1) * 128,
                    ]


def clear_pads(r):
    for s in range(r.slots):
        r.big2[s] = jnp.zeros(r.big2.shape[1:], BF16)
    r.shifted[...] = jnp.zeros(r.shifted.shape, BF16)


def backward_cross(r, m):
    marks = head_marks()
    wide = window_rows()
    reach = r.frame - wide
    d_mixed = mm(r.d_second[m], columns(r, CROSS + 3)).astype(BF16)
    queries = r.q_cross[m]
    d_queries = []
    windows = [slot_window(r, m, s) for s in range(r.slots)]
    for g in range(r.quads):
        cut = slice(g * QUAD, (g + 1) * QUAD)
        column = []
        for s in range(r.slots):
            rows = slice(s * SLOT, (s + 1) * SLOT)
            at = windows[s][0]
            d_q, d_k, d_v = attend_back(
                r.p_cross[m, s, g],
                r.k_cross[m, pl.ds(at, wide), cut],
                r.v_cross[m, pl.ds(at, wide), cut],
                queries[rows, cut],
                d_mixed[rows, cut],
                marks,
            )
            r.big2[s, reach : reach + wide, :QUAD] = d_k
            r.big2[s, reach : reach + wide, QUAD:] = d_v
            column.append(d_q)
        d_queries.append(jnp.concatenate(column, axis=0))
        total = None
        for s in range(r.slots):
            piece = r.big2[s, pl.ds(slot_shift(r, m, s), r.frame), :]
            total = piece if total is None else total + piece
        r.k_cross[m, :, cut] = total[:, :QUAD]
        r.v_cross[m, :, cut] = total[:, QUAD:]
    d_queries = jnp.concatenate(d_queries, axis=1)
    r.q_cross[m] = d_queries
    d_first = r.residual[m] + mm_nt(d_queries, columns(r, CROSS + 0))
    d_attn, gain, bias = norm_backward(d_first, r.normed1[m].astype(F32), r.factor[m, :, 0:1], r.norms[0:1, :])
    r.sums[0:1, :] += gain
    r.sums[3:4, :] += bias
    r.residual[m] = d_attn
    r.d_first[m] = d_attn.astype(BF16)
    source_term = mm_nt(r.k_cross[m], columns(r, CROSS + 1)) + mm_nt(
        r.v_cross[m], columns(r, CROSS + 2)
    )
    edge = r.enc_len - r.frame
    r.shifted[edge : edge + r.frame, :] = source_term.astype(BF16)
    r.big1[m] = r.shifted[pl.ds(r.table[m, 1] * 16, r.enc_len), :]


def cross_grads(r):
    store_columns(r, mm_tn(tokens(r.first_low), tokens(r.q_cross)).astype(BF16), CROSS)
    store_columns(r, mm_tn(tokens(r.source), tokens(r.k_cross)).astype(BF16), CROSS + 1)
    store_columns(r, mm_tn(tokens(r.source), tokens(r.v_cross)).astype(BF16), CROSS + 2)
    store_columns(r, mm_tn(tokens(r.d_second), tokens(r.mixed_cross)).astype(BF16), CROSS + 3)


def backward_self(r, m):
    marks = head_marks()
    d_mixed = mm(r.d_first[m], columns(r, SELF + 3)).astype(BF16)
    queries, keys, values = r.q_self[m], r.k_self[m], r.v_self[m]
    out = []
    for s in range(r.slots):
        rows = slice(s * SLOT, (s + 1) * SLOT)
        halves = []
        for g in range(r.quads):
            cut = slice(g * QUAD, (g + 1) * QUAD)
            halves.append(
                attend_back(
                    r.p_self[m, s, g],
                    keys[rows, cut],
                    values[rows, cut],
                    queries[rows, cut],
                    d_mixed[rows, cut],
                    marks,
                )
            )
        out.append([jnp.concatenate([half[i] for half in halves], axis=1) for i in range(3)])
    d_q, d_k, d_v = [jnp.concatenate([item[i] for item in out], axis=0) for i in range(3)]
    r.q_self[m], r.k_self[m], r.v_self[m] = d_q, d_k, d_v
    r.cotangent[m] = (r.residual[m] + mm_nt(d_q, columns(r, SELF + 0))).astype(BF16)
    r.second_low[m] = (
        mm_nt(d_k, columns(r, SELF + 1)) + mm_nt(d_v, columns(r, SELF + 2))
    ).astype(BF16)


def self_grads(r):
    store_columns(r, mm_tn(tokens(r.stream), tokens(r.q_self)).astype(BF16), SELF)
    store_columns(r, mm_tn(tokens(r.context), tokens(r.k_self)).astype(BF16), SELF + 1)
    store_columns(r, mm_tn(tokens(r.context), tokens(r.v_self)).astype(BF16), SELF + 2)


def output_grads(r):
    store_columns(r, mm_tn(tokens(r.d_first), tokens(r.mixed_self)).astype(BF16), SELF + 3)


class Place:
    def __init__(self, groups):
        d, t = lax.axis_index("dp"), lax.axis_index("tensor")
        high, self.low = lax.div(d, groups), lax.rem(d, groups)
        self.groups = groups
        self.a, self.b = lax.div(high, NX), lax.rem(high, NX)
        self.y, self.c = lax.div(t, NC), lax.rem(t, NC)
        self.t = t

    def device(self, a=None, b=None, y=None, c=None):
        a, b = self.a if a is None else a, self.b if b is None else b
        y, c = self.y if y is None else y, self.c if c is None else c
        return ((a * NX + b) * self.groups + self.low, y * NC + c)

    def up(self, k):
        return lax.rem(self.a + k, NZ)

    def peer(self, axis, k=0):
        if axis == "z":
            return self.device(a=self.up(k))
        if axis == "x":
            return self.device(b=1 - self.b)
        if axis == "y":
            return self.device(y=1 - self.y)
        if axis == "core":
            return self.device(c=1 - self.c)
        return self.device(y=1 - self.y, c=1 - self.c)


class Link:
    def __init__(self, r):
        self.r = r
        self.used = 0
        self.all = []

    def slot(self):
        self.used += 1
        return self.used - 1

    def send(self, key, source, target, device):
        return pltpu.make_async_remote_copy(
            src_ref=source,
            dst_ref=target,
            send_sem=self.r.send_sems.at[key],
            recv_sem=self.r.recv_sems.at[key],
            device_id=device,
            device_id_type=MESH,
        )


class Stages:
    def __init__(self, link, counts):
        self.link = link
        self.keys = [[link.slot() for _ in range(n)] for n in counts]
        link.all.append(self)

    def start(self, stage):
        for copy in self.copies(stage):
            copy.start()

    def wait(self, stage):
        for copy in self.copies(stage):
            copy.wait_recv()

    def drain(self):
        for stage in range(len(self.keys)):
            for copy in self.copies(stage):
                copy.wait_send()


class Gather(Stages):
    def __init__(self, link, place, first, count, order):
        super().__init__(link, (NZ - 1, 1, 1, 1))
        self.p, self.kinds, self.order = place, pl.ds(first, count), order

    def copies(self, stage):
        p, w, send = self.p, self.link.r.w, self.link.send
        keys = self.keys[stage]
        if stage == 0:
            ref = w.at[self.kinds, p.y, p.c, p.a, p.b]
            return [send(keys[k - 1], ref, ref, p.peer("z", k)) for k in range(1, NZ)]
        if stage == 1:
            ref = w.at[self.kinds, p.y, p.c, :, p.b]
            return [send(keys[0], ref, ref, p.peer(self.order[0]))]
        if stage == 2:
            if self.order == "xy":
                ref = w.at[self.kinds, p.y, p.c]
            else:
                ref = w.at[self.kinds, :, p.c, :, p.b]
            return [send(keys[0], ref, ref, p.peer(self.order[1]))]
        ref = w.at[self.kinds, :, p.c]
        return [send(keys[0], ref, ref, p.peer("core"))]


class GatherNorms(Stages):
    def __init__(self, link, place):
        super().__init__(link, (NZ - 1, 1))
        self.p = place

    def copies(self, stage):
        p, pack, send = self.p, self.link.r.pack, self.link.send
        keys = self.keys[stage]
        if stage == 0:
            ref = pack.at[p.a, p.b]
            return [send(keys[k - 1], ref, ref, p.peer("z", k)) for k in range(1, NZ)]
        ref = pack.at[:, p.b]
        return [send(keys[0], ref, ref, p.peer("x"))]


class Scatter(Stages):
    def __init__(self, link, place, first, count, order, boxes):
        super().__init__(link, (1, 1, 1, NZ - 1))
        self.p, self.count, self.order, self.boxes = place, count, order, boxes
        self.ref, at = grad_place(link.r, first)
        self.first = at
        self.kinds = pl.ds(at, count)

    def parts(self, stage):
        p = self.p
        every = slice(None)
        if stage == 0:
            return (every, 1 - p.c), (every, p.c)
        if stage == 1:
            if self.order == "xy":
                return (every, p.c, every, 1 - p.b), (every, p.c, every, p.b)
            return (1 - p.y, p.c), (p.y, p.c)
        if self.order == "xy":
            return (1 - p.y, p.c, every, p.b), (p.y, p.c, every, p.b)
        return (p.y, p.c, every, 1 - p.b), (p.y, p.c, every, p.b)

    def copies(self, stage):
        p, send, keys = self.p, self.link.send, self.keys[stage]
        if stage < 3:
            axis = "core" if stage == 0 else self.order[stage - 1]
            source = self.ref.at[(self.kinds, *self.parts(stage)[0])]
            return [send(keys[0], source, self.boxes[stage], p.peer(axis))]
        return [
            send(
                keys[k - 1],
                self.ref.at[self.kinds, p.y, p.c, p.up(k), p.b],
                self.boxes[3].at[k - 1],
                p.peer("z", k),
            )
            for k in range(1, NZ)
        ]

    def add(self, stage):
        self.wait(stage)
        keep = self.parts(stage)[1]
        for k in range(self.count):
            at = (self.first + k, *keep)
            self.ref[at] = self.ref[at] + self.boxes[stage][k]

    def step(self, stage):
        self.add(stage)
        self.start(stage + 1)

    def total(self, k):
        p = self.p
        own = self.ref[self.first + k, p.y, p.c, p.a, p.b].astype(F32)
        box = self.boxes[3]
        return own + box[0, k].astype(F32) + box[1, k].astype(F32) + box[2, k].astype(F32)


def scatter_boxes(name, count, order):
    second = (NY, NZ) if order == "xy" else (NZ, NX)
    tile = (64, 128)
    return [
        (name + "0", pltpu.VMEM((count, NY, NZ, NX, *tile), BF16)),
        (name + "1", pltpu.VMEM((count, *second, *tile), BF16)),
        (name + "2", pltpu.VMEM((count, NZ, *tile), BF16)),
        (name + "3", pltpu.VMEM((NZ - 1, count, *tile), BF16)),
    ]


SCATTERS = {
    "up": (UP, 4, "xy"),
    "down": (DOWN, 4, "xy"),
    "cross": (CROSS, 4, "xy"),
    "mix": (SELF + 3, 1, "xy"),
    "query": (SELF, 1, "xy"),
    "pair": (SELF + 1, 2, "yx"),
}


class ScatterNorms(Stages):
    def __init__(self, link, place):
        super().__init__(link, (1, 1, 1, NZ - 1))
        self.p = place

    def copies(self, stage):
        p, r, send, keys = self.p, self.link.r, self.link.send, self.keys[stage]
        if stage == 0:
            return [send(keys[0], r.g_norm, r.n_box0, p.peer("core"))]
        if stage == 1:
            return [send(keys[0], r.n_sum, r.n_box1, p.peer("y"))]
        if stage == 2:
            return [send(keys[0], r.n_all.at[:, 1 - p.b], r.n_box2, p.peer("x"))]
        return [
            send(keys[k - 1], r.n_half.at[p.up(k)], r.n_box3.at[k - 1], p.peer("z", k))
            for k in range(1, NZ)
        ]

    def step(self, stage):
        p, r = self.p, self.link.r
        self.wait(stage)
        if stage == 0:
            r.n_sum[...] = r.g_norm[...] + r.n_box0[...]
        elif stage == 1:
            r.n_all[...] = r.n_sum[...] + r.n_box1[...]
        else:
            r.n_half[...] = r.n_all[:, p.b] + r.n_box2[...]
        self.start(stage + 1)

    def total(self):
        r = self.link.r
        return r.n_half[self.p.a] + ((r.n_box3[0] + r.n_box3[1]) + r.n_box3[2])


class ScatterEncoder(Stages):
    def __init__(self, link, place, share):
        super().__init__(link, (NY, 1))
        self.p, self.share = place, share
        self.boxes = (link.r.d_third, link.r.second_low)

    def rows(self, y, c):
        at = pl.multiple_of((y * NC + c) * self.share, self.share)
        return self.link.r.big1.at[:, pl.ds(at, self.share), :]

    def copies(self, stage):
        p, r, send, keys = self.p, self.link.r, self.link.send, self.keys[stage]
        if stage == 0:
            return [
                send(keys[y], self.rows(y, 1 - p.c), self.boxes[y], p.peer("core"))
                for y in range(NY)
            ]
        return [send(keys[0], self.rows(1 - p.y, p.c), r.e_box1, p.peer("y"))]

    def step(self):
        self.wait(0)
        for y in range(NY):
            ref = self.rows(y, self.p.c)
            for m in range(ref.shape[0]):
                ref[m] = ref[m] + self.boxes[y][m]
        self.start(1)

    def finish(self):
        self.wait(1)
        ref = self.rows(self.p.y, self.p.c)
        for m in range(ref.shape[0]):
            ref[m] = ref[m] + self.link.r.e_box1[m]
        return ref


class ShareFfn(Stages):
    def __init__(self, link, place, box):
        super().__init__(link, (3,))
        self.p, self.box = place, box

    def copies(self, stage):
        p, send, keys = self.p, self.link.send, self.keys[0]
        ref = self.box.at[p.t]
        axes = ("core", "y", "both")
        return [send(keys[i], ref, ref, p.peer(axes[i])) for i in range(3)]


def each(count, body, ticks=None):
    def step(i, carry):
        for k, tick in (ticks or {}).items():
            pl.when(i == k)(tick)
        body(i)
        return carry

    lax.fori_loop(0, count, step, 0)


SEMS = 115


def layer_kernel(names, groups, scale, *refs):
    r = Refs()
    for name, ref in zip(names, refs):
        setattr(r, name, ref)
    micro, r.share = r.stream.shape[0], r.stream.shape[1]
    r.slots = r.share // SLOT
    r.quads = r.stream.shape[2] // QUAD
    r.enc_len = r.encoder.shape[1]
    r.frame = frame_rows(r.share)
    p = Place(groups)
    link = Link(r)

    mine = pl.ds(pl.multiple_of(p.t * r.share, r.share), r.share)
    half = pl.ds(pl.multiple_of(p.t * (r.share // 2), r.share // 2), r.share // 2)
    pairs = [
        (r.self_query, r.w.at[SELF, p.y, p.c, p.a, p.b]),
        (r.self_key_value, r.w.at[pl.ds(SELF + 1, 2), p.y, p.c, p.a, p.b]),
        (r.cross_query, r.w.at[CROSS, p.y, p.c, p.a, p.b]),
        (r.cross_key_value, r.w.at[pl.ds(CROSS + 1, 2), p.y, p.c, p.a, p.b]),
    ]
    for k in range(4):
        up = pl.ds(pl.multiple_of(p.t * 512 + k * 128, 128), 128)
        pairs.append((r.ffn_in.at[:, up], r.w.at[UP + k, p.y, p.c, p.a, p.b]))
        down = pl.ds(pl.multiple_of(p.t * 128, 128), 128)
        pairs.append(
            (r.ffn_out.at[pl.ds(k * 64, 64), down], r.w.at[DOWN + k, p.y, p.c, p.a, p.b])
        )
    weights = len(pairs)
    pairs += [
        (r.stream_hbm.at[:, mine, :], r.stream),
        (r.context_hbm.at[:, mine, :], r.context),
        (r.masks_hbm.at[:, half, :], r.masks),
        (r.encoder, r.big1),
        (r.out_grad, r.cotangent),
    ]
    copies = [
        pltpu.make_async_copy(source, target, r.sems.at[i])
        for i, (source, target) in enumerate(pairs)
    ]
    for copy in copies:
        copy.start()
    partners = [p.peer("z", k) for k in range(1, NZ)]
    partners += [p.peer(axis) for axis in ("x", "y", "core", "both")]
    barrier = pltpu.get_barrier_semaphore()
    for device in partners:
        pl.semaphore_signal(barrier, inc=1, device_id=device, device_id_type=MESH)
    r.w[SELF + 3, p.y, p.c, p.a, p.b] = r.self_output[...].astype(F32).T.astype(BF16)
    r.w[CROSS + 3, p.y, p.c, p.a, p.b] = r.cross_output[...].astype(F32).T.astype(BF16)
    r.pack[p.a, p.b, 0:3, :64] = r.norm_gain[...].astype(F32)
    r.pack[p.a, p.b, 3:6, :64] = r.norm_bias[...].astype(F32)
    for copy in copies[:weights]:
        copy.wait()
    pl.semaphore_wait(barrier, len(partners))

    first = [Gather(link, p, SELF + k, 1, "xy" if k % 2 == 0 else "yx") for k in range(4)]
    rest = [Gather(link, p, CROSS + 2 * k, 2, "xy" if k % 2 == 0 else "yx") for k in range(6)]
    cross, up, down = rest[:2], rest[2:4], rest[4:]
    norms = GatherNorms(link, p)

    def start(items, stage):
        for item in items:
            item.start(stage)

    def move(items, stage):
        for item in items:
            item.wait(stage)
            item.start(stage + 1)

    def wait(items, stage):
        for item in items:
            item.wait(stage)

    start(first, 0)
    norms.start(0)
    move(first, 0)
    start(cross, 0)
    r.sums[...] = jnp.zeros(r.sums.shape, F32)
    move(first, 1)
    norms.wait(0)
    norms.start(1)
    move(first, 2)
    for copy in copies[weights:]:
        copy.wait()
    norms.wait(1)
    r.norms[...] = jnp.concatenate(
        [r.pack[d // NX, d % NX, :, :64] for d in range(NZ * NX)], axis=1
    )
    wait(first, 3)

    def self_tick0():
        move(cross, 0)
        start(up, 0)

    def self_tick1():
        move(cross, 1)
        move(up, 0)
        start(down, 0)

    def self_tick2():
        move(cross, 2)
        move(up, 1)
        move(down, 0)

    def self_tick3():
        move(up, 2)
        move(down, 1)

    each(
        micro,
        functools.partial(forward_self, r),
        {0: self_tick0, 1: self_tick1, 2: self_tick2, 3: self_tick3},
    )
    wait(cross, 3)
    each(micro, functools.partial(forward_cross, r), {1: lambda: move(down, 2)})
    wait(up, 3)
    wait(down, 3)
    for item in link.all:
        item.drain()
    link.all = []
    each(micro, functools.partial(feed_forward, r))
    out = [pltpu.make_async_copy(r.d_first, r.block_out, r.sems.at[0])]
    out[0].start()
    each(4, functools.partial(ffn_grads, r))

    sums = {}
    for name, (kind, count, order) in SCATTERS.items():
        boxes = [getattr(r, "box_" + name + str(i)) for i in range(4)]
        sums[name] = Scatter(link, p, kind, count, order, boxes)
    norm_sums = ScatterNorms(link, p)
    rows = ScatterEncoder(link, p, r.share)
    share_up, share_down = ShareFfn(link, p, r.all_up), ShareFfn(link, p, r.all_down)

    sums["up"].start(0)
    sums["down"].start(0)
    clear_pads(r)
    out[0].wait()

    def cross_tick1():
        sums["up"].step(0)
        sums["down"].step(0)

    each(
        micro,
        functools.partial(backward_cross, r),
        {1: cross_tick1, 3: lambda: sums["up"].step(1)},
    )
    rows.start(0)
    for d in range(NZ * NX):
        r.g_norm[d // NX, d % NX] = jnp.zeros(r.g_norm.shape[2:], F32)
        r.g_norm[d // NX, d % NX, :, :64] = r.sums[:, d * 64 : (d + 1) * 64]
    norm_sums.start(0)
    cross_grads(r)
    sums["cross"].start(0)
    output_grads(r)
    sums["mix"].start(0)
    rows.step()
    sums["down"].step(1)

    def share_sum(name, box, item):
        item_sum = sums[name]
        item_sum.wait(3)
        for k in range(4):
            box[p.t, k] = item_sum.total(k).astype(BF16)
        item.start(0)

    def back_tick0():
        sums["up"].step(2)
        sums["cross"].step(0)
        sums["mix"].step(0)

    def back_tick1():
        sums["down"].step(2)
        norm_sums.step(0)

    def back_tick2():
        share_sum("up", r.all_up, share_up)
        sums["mix"].step(1)
        norm_sums.step(1)

    def back_tick3():
        share_sum("down", r.all_down, share_down)
        sums["cross"].step(1)
        norm_sums.step(2)

    each(
        micro,
        functools.partial(backward_self, r),
        {0: back_tick0, 1: back_tick1, 2: back_tick2, 3: back_tick3},
    )
    out = [
        pltpu.make_async_copy(r.cotangent, r.stream_grad, r.sems.at[0]),
        pltpu.make_async_copy(r.second_low, r.context_grad, r.sems.at[1]),
    ]
    for copy in out:
        copy.start()
    self_grads(r)
    sums["query"].start(0)
    sums["pair"].start(0)
    ready = rows.finish()
    out.append(pltpu.make_async_copy(ready, r.encoder_grad, r.sems.at[2]))
    out[2].start()
    sums["cross"].step(2)
    sums["mix"].step(2)
    sums["query"].step(0)
    sums["pair"].step(0)
    sums["query"].step(1)
    sums["pair"].step(1)
    sums["query"].step(2)
    sums["pair"].step(2)
    share_up.wait(0)
    for t in range(NY * NC):
        for k in range(4):
            at = t * 512 + k * 128
            r.grad_ffn_in[:, at : at + 128] = r.all_up[t, k].astype(F32) * scale
    share_down.wait(0)
    for t in range(NY * NC):
        for n in range(2):
            block = jnp.concatenate([r.all_down[t, n], r.all_down[t, 2 + n]], axis=0)
            r.grad_ffn_out[n * 128 : (n + 1) * 128, t * 128 : (t + 1) * 128] = (
                block.astype(F32) * scale
            ).T
    norm_sums.wait(3)
    total = norm_sums.total() * scale
    r.grad_norm_gain[...] = total[0:3, :64]
    r.grad_norm_bias[...] = total[3:6, :64]
    sums["cross"].wait(3)
    r.grad_cross_query[...] = sums["cross"].total(0) * scale
    r.grad_cross_key_value[0] = sums["cross"].total(1) * scale
    r.grad_cross_key_value[1] = sums["cross"].total(2) * scale
    r.grad_cross_output[...] = (sums["cross"].total(3) * scale).T
    sums["mix"].wait(3)
    r.grad_self_output[...] = (sums["mix"].total(0) * scale).T
    sums["query"].wait(3)
    r.grad_self_query[...] = sums["query"].total(0) * scale
    sums["pair"].wait(3)
    r.grad_self_key_value[0] = sums["pair"].total(0) * scale
    r.grad_self_key_value[1] = sums["pair"].total(1) * scale
    for item in link.all:
        item.drain()
    for copy in out:
        copy.wait()


def vmem():
    return pl.BlockSpec(memory_space=pltpu.VMEM)


def hbm():
    return pl.BlockSpec(memory_space=pl.ANY)


WEIGHTS = (
    "self_query", "self_key_value", "self_output",
    "cross_query", "cross_key_value", "cross_output",
    "ffn_in", "ffn_out", "norm_gain", "norm_bias",
)


def layer(groups, scale, stream, context, encoder, masks, table, out_grad, weights):
    micro, row, width = stream.shape
    share = out_grad.shape[1]
    enc_len = encoder.shape[1]
    frame, wide = frame_rows(share), window_rows()
    slots, quads = share // SLOT, width // QUAD
    small = ("self_output", "cross_output", "norm_gain", "norm_bias")
    ins = [
        ("stream_hbm", stream, hbm()),
        ("context_hbm", context, hbm()),
        ("encoder", encoder, hbm()),
        ("masks_hbm", masks, hbm()),
        ("table", table, pl.BlockSpec(memory_space=pltpu.SMEM)),
        ("out_grad", out_grad, hbm()),
    ]
    for name, value in zip(WEIGHTS, weights):
        ins.append((name, value, vmem() if name in small else hbm()))
    part = jax.ShapeDtypeStruct((micro, share, width), BF16)
    outs = [
        ("block_out", part, hbm()),
        ("stream_grad", part, hbm()),
        ("context_grad", part, hbm()),
        ("encoder_grad", part, hbm()),
    ]
    for name, value in zip(WEIGHTS, weights):
        outs.append(("grad_" + name, jax.ShapeDtypeStruct(value.shape, F32), vmem()))
    low = pltpu.VMEM((micro, share, width), BF16)
    high = pltpu.VMEM((micro, share, width), F32)
    window = pltpu.VMEM((micro, frame, width), BF16)
    big = pltpu.VMEM((micro, enc_len, width), BF16)
    norm = pltpu.VMEM((NZ, NX, 8, 128), F32)
    scratch = [
        ("w", pltpu.VMEM((16, NY, NC, NZ, NX, 64, 128), BF16)),
        ("g_ffn", pltpu.VMEM((8, NY, NC, NZ, NX, 64, 128), BF16)),
        ("stream", low),
        ("context", low),
        ("cotangent", low),
        ("masks", pltpu.VMEM((micro, share // 2, 128), jnp.int32)),
        ("q_self", low),
        ("k_self", low),
        ("v_self", low),
        ("mixed_self", low),
        ("first_low", low),
        ("q_cross", low),
        ("k_cross", window),
        ("v_cross", window),
        ("source", window),
        ("mixed_cross", low),
        ("second_low", low),
        ("d_third", low),
        ("d_second", low),
        ("d_first", low),
        ("p_self", pltpu.VMEM((micro, slots, quads, SLOT, QUAD), BF16)),
        ("p_cross", pltpu.VMEM((micro, slots, quads, wide, QUAD), BF16)),
        ("residual", high),
        ("normed1", low),
        ("normed2", low),
        ("factor", pltpu.VMEM((micro, share, 2), F32)),
        ("big1", big),
        ("big2", big),
        ("shifted", pltpu.VMEM((2 * enc_len - frame, width), BF16)),
        ("norms", pltpu.VMEM((8, width), F32)),
        ("sums", pltpu.VMEM((8, width), F32)),
        ("pack", norm),
        ("g_norm", norm),
        ("n_sum", norm),
        ("n_all", norm),
        ("n_half", pltpu.VMEM((NZ, 8, 128), F32)),
        ("n_box0", norm),
        ("n_box1", norm),
        ("n_box2", pltpu.VMEM((NZ, 8, 128), F32)),
        ("n_box3", pltpu.VMEM((NZ - 1, 8, 128), F32)),
        ("e_box1", low),
        ("all_up", pltpu.VMEM((NY * NC, 4, 64, 128), BF16)),
        ("all_down", pltpu.VMEM((NY * NC, 4, 64, 128), BF16)),
        ("sems", pltpu.SemaphoreType.DMA((17,))),
        ("send_sems", pltpu.SemaphoreType.DMA((SEMS,))),
        ("recv_sems", pltpu.SemaphoreType.DMA((SEMS,))),
    ]
    for name, (_, count, order) in SCATTERS.items():
        scratch += scatter_boxes("box_" + name, count, order)
    names = [item[0] for item in ins + outs + scratch]
    return pl.pallas_call(
        functools.partial(layer_kernel, names, groups, scale),
        out_shape=[item[1] for item in outs],
        in_specs=[item[2] for item in ins],
        out_specs=[item[2] for item in outs],
        scratch_shapes=[item[1] for item in scratch],
        compiler_params=pltpu.CompilerParams(
            vmem_limit_bytes=VMEM_LIMIT, collective_id=0, has_side_effects=True
        ),
        cost_estimate=pl.CostEstimate(
            flops=30_000_000_000, bytes_accessed=30_000_000, transcendentals=4_000_000
        ),
    )(*[item[1] for item in ins])


GATHER_DIM = (0, 1, 1, 0, 1, 1, 0, 0, 1, 1)


def per_device(
    query_stream,
    context_stream,
    encoder_out,
    query_masks,
    source_segments,
    out_grad,
    *weights,
):
    micro, row, width = query_stream.shape
    share = out_grad.shape[1]
    slots = share // SLOT
    t = lax.axis_index("tensor")
    replicas = lax.axis_size("dp")
    scale = float(micro * row * replicas) ** (-0.5)
    groups = replicas // (NZ * NX)
    near = [[i * groups + j for j in range(groups)] for i in range(NZ * NX)]
    if groups > 1:
        weights = [
            lax.all_gather(item, "dp", axis=dim, tiled=True, axis_index_groups=near)
            for item, dim in zip(weights, GATHER_DIM)
        ]
    bounds = t * slots + jnp.arange(slots + 1, dtype=jnp.int32)
    starts = jnp.sum(
        (source_segments < bounds[None, :, None]).astype(jnp.int32), axis=-1
    )
    table = window_table(starts, share, encoder_out.shape[1])
    results = layer(
        groups, scale, query_stream, context_stream, encoder_out, query_masks, table,
        out_grad, weights,
    )
    grads = results[4:]
    if groups > 1:
        grads = [
            lax.psum_scatter(
                item, "dp", scatter_dimension=dim, tiled=True, axis_index_groups=near
            )
            for item, dim in zip(grads, GATHER_DIM)
        ]
    return (*results[:4], *grads)


def solution(mesh):
    in_specs = (
        P(None, "dp", None),
        P(None, "dp", None),
        P(None, "dp", None),
        P(None, "dp", None),
        P(None, "dp", None),
        P(None, ("dp", "tensor"), None),
        P("dp", "tensor"),
        P(None, "dp", "tensor"),
        P("tensor", "dp"),
        P("dp", "tensor"),
        P(None, "dp", "tensor"),
        P("tensor", "dp"),
        P("dp", None),
        P("dp", None),
        P(None, "dp"),
        P(None, "dp"),
    )
    out_specs = (
        P(None, ("dp", "tensor"), None),
        P(None, ("dp", "tensor"), None),
        P(None, ("dp", "tensor"), None),
        P(None, ("dp", "tensor"), None),
        P("dp", "tensor"),
        P(None, "dp", "tensor"),
        P("tensor", "dp"),
        P("dp", "tensor"),
        P(None, "dp", "tensor"),
        P("tensor", "dp"),
        P("dp", None),
        P("dp", None),
        P(None, "dp"),
        P(None, "dp"),
    )
    return jax.shard_map(
        per_device, mesh=mesh, in_specs=in_specs, out_specs=out_specs, check_vma=False
    )
```

```python
import functools

import jax
import jax.numpy as jnp
from jax import lax
from jax.experimental import pallas as pl
from jax.experimental.pallas import tpu as pltpu
from jax.sharding import PartitionSpec as P

HEAD_DIM = 64
SLOT = 64
SEG_MOST = 128
QUAD = 4 * HEAD_DIM
PAIR = 2 * HEAD_DIM
NZ, NX, NY, NC = 4, 2, 2, 2
PIECE = 2
SELF, CROSS, FEED, KINDS = 0, 4, 8, 16
BF16 = jnp.bfloat16
F32 = jnp.float32
MESH = pl.DeviceIdType.MESH
DP, TENSOR = "dp", "tensor"

epsilon = 1e-05
neg_fill = -1e30
gelu_coef = 0.7978845608028654
gelu_cube = 0.044715
VMEM_LIMIT = 65400 * 1024


def mm(left, right):
    return jnp.dot(left, right, preferred_element_type=F32)


def mm_nt(left, right):
    return lax.dot_general(left, right, (((1,), (1,)), ((), ())), preferred_element_type=F32)


def mm_tn(left, right):
    return lax.dot_general(left, right, (((0,), (0,)), ((), ())), preferred_element_type=F32)


def norm_forward(value, gain, bias):
    center = jnp.mean(value, axis=-1, keepdims=True)
    shifted = value - center
    factor = lax.rsqrt(jnp.mean(shifted * shifted, axis=-1, keepdims=True) + epsilon)
    normed = shifted * factor
    return normed * gain + bias, normed, factor


def norm_backward(incoming, normed, factor, gain):
    scaled = incoming * gain
    inside = (
        scaled
        - jnp.mean(scaled, axis=-1, keepdims=True)
        - normed * jnp.mean(scaled * normed, axis=-1, keepdims=True)
    )
    return (
        factor * inside,
        jnp.sum(incoming * normed, axis=0, keepdims=True),
        jnp.sum(incoming, axis=0, keepdims=True),
    )


def columns(r, kind):
    parts = [r.w[kind, t // NC, t % NC].reshape(-1, 128) for t in range(NY * NC)]
    return jnp.concatenate(parts, axis=1)


def grad_place(r, kind):
    if kind >= FEED:
        return r.g_ffn, kind - FEED
    return r.w, kind + FEED


def store_columns(ref, at, value):
    for t in range(NY * NC):
        ref[at, t // NC, t % NC] = value[:, t * 128 : (t + 1) * 128].reshape(NZ, NX, -1, 128)


def head_marks():
    lane = lax.broadcasted_iota(jnp.int32, (1, QUAD), 1) // HEAD_DIM
    return [jnp.where(lane == h, 1.0, 0.0).astype(BF16) for h in range(4)]


def spread_heads(rows, marks):
    return jnp.concatenate([rows * mark for mark in marks], axis=0)


def fold_pairs(weights, rows):
    first = lax.broadcasted_iota(jnp.int32, (SLOT, PAIR), 1) < HEAD_DIM
    parts = []
    for p in range(2):
        cut = slice(p * PAIR, (p + 1) * PAIR)
        full = mm_tn(weights[:, cut], rows[:, cut])
        parts.append(jnp.where(first, full[:SLOT], full[SLOT:]))
    return jnp.concatenate(parts, axis=1)


def soft_keys(scores, allowed):
    scores = jnp.where(allowed, scores, neg_fill)
    top = jnp.max(scores, axis=0, keepdims=True)
    raised = jnp.exp(scores - top)
    return (raised * (1.0 / jnp.sum(raised, axis=0, keepdims=True))).astype(BF16)


def attend_back(items, marks):
    d_spread = [spread_heads(item[4], marks) for item in items]
    d_probs = [mm_nt(item[2], spread) for item, spread in zip(items, d_spread)]
    d_values = [mm(item[0], spread).astype(BF16) for item, spread in zip(items, d_spread)]
    d_scores = []
    for item, d_prob in zip(items, d_probs):
        wide = item[0].astype(F32)
        inner = jnp.sum(wide * d_prob, axis=0, keepdims=True)
        d_scores.append((wide * (d_prob - inner)).astype(BF16))
    d_keys = [
        mm(d_score, spread_heads(item[3], marks)).astype(BF16)
        for item, d_score in zip(items, d_scores)
    ]
    d_queries = [
        (fold_pairs(d_score, item[1]) * HEAD_DIM ** (-0.5)).astype(BF16)
        for item, d_score in zip(items, d_scores)
    ]
    return d_queries, d_keys, d_values


def cut(value, s, g):
    return value[s * SLOT : (s + 1) * SLOT, g * QUAD : (g + 1) * QUAD]


class Refs:
    pass


def frame_rows(share):
    return (share // SLOT) * SEG_MOST + 16


def window_rows():
    return SEG_MOST + 16


def window_table(starts, share, enc_len):
    frame, wide = frame_rows(share), window_rows()
    base = jnp.minimum(starts[:, :1] // 16 * 16, enc_len - frame)
    begin = starts[:, :-1] - base
    at = jnp.minimum(begin // 16 * 16, frame - wide)
    low = begin - at
    high = low + starts[:, 1:] - starts[:, :-1]
    return jnp.concatenate(
        [base // 16, (enc_len - frame - base) // 16, at // 16, low, high, (frame - wide - at) // 16],
        axis=1,
    )


def frame_start(r, m):
    return r.table[m, 0] * 16


def slot_window(r, m, s):
    at = r.table[m, 2 + s] * 16
    return at, r.table[m, 2 + r.slots + s], r.table[m, 2 + 2 * r.slots + s]


def slot_shift(r, m, s):
    return r.table[m, 2 + 3 * r.slots + s] * 16


def forward_self(r, m):
    marks = head_marks()
    stream, context = r.stream[m], r.context[m]
    queries = (mm(stream, columns(r, SELF + 0)) * HEAD_DIM ** (-0.5)).astype(BF16)
    keys = mm(context, columns(r, SELF + 1)).astype(BF16)
    values = mm(context, columns(r, SELF + 2)).astype(BF16)
    r.q_self[m], r.k_self[m], r.v_self[m] = queries, keys, values
    row = lax.broadcasted_iota(jnp.int32, (SLOT, QUAD), 0)
    lane = lax.broadcasted_iota(jnp.int32, (SLOT, QUAD), 1) % SLOT
    place = jnp.where(lane == 2 * (row % 32) + row // 32, 1.0, 0.0).astype(BF16)
    units = [(s, g) for s in range(r.slots) for g in range(r.quads)]
    allowed = []
    for s in range(r.slots):
        bits = r.masks[m, s * 32 : (s + 1) * 32].astype(F32)
        bits = jnp.concatenate([bits[:, :SLOT], bits[:, SLOT:]], axis=0).astype(BF16)
        allowed.append(mm_tn(bits, place) > 0.5)
    scores = [mm_nt(cut(keys, s, g), spread_heads(cut(queries, s, g), marks)) for s, g in units]
    probs = [soft_keys(score, allowed[s]) for score, (s, g) in zip(scores, units)]
    mixed = [fold_pairs(prob, cut(values, s, g)).astype(BF16) for prob, (s, g) in zip(probs, units)]
    for prob, one, (s, g) in zip(probs, mixed, units):
        r.p_self[m, s, g] = prob
        r.mixed_self[m, s * SLOT : (s + 1) * SLOT, g * QUAD : (g + 1) * QUAD] = one


def first_norm(r, m):
    attn = mm_nt(r.mixed_self[m], columns(r, SELF + 3))
    first, normed, factor = norm_forward(
        r.stream[m].astype(F32) + attn, r.norms[0:1, :], r.norms[3:4, :]
    )
    r.residual[m], r.factor[m, :, 0:1] = first, factor
    r.normed1[m] = normed.astype(BF16)
    r.first_low[m] = first.astype(BF16)


def forward_cross(r, m):
    marks = head_marks()
    base = frame_start(r, m)
    source = r.big1[m, pl.ds(base, r.frame), :]
    r.source[m] = source
    r.k_cross[m] = mm(source, columns(r, CROSS + 1)).astype(BF16)
    r.v_cross[m] = mm(source, columns(r, CROSS + 2)).astype(BF16)
    queries = (mm(r.first_low[m], columns(r, CROSS + 0)) * HEAD_DIM ** (-0.5)).astype(BF16)
    r.q_cross[m] = queries
    wide = window_rows()
    row = lax.broadcasted_iota(jnp.int32, (wide, QUAD), 0)
    units = [(s, g) for s in range(r.slots) for g in range(r.quads)]
    windows = [slot_window(r, m, s) for s in range(r.slots)]
    allowed = [(row >= low) & (row < high) for _, low, high in windows]

    def view(ref, s, g):
        return ref[m, pl.ds(windows[s][0], wide), g * QUAD : (g + 1) * QUAD]

    scores = [
        mm_nt(view(r.k_cross, s, g), spread_heads(cut(queries, s, g), marks)) for s, g in units
    ]
    probs = [soft_keys(score, allowed[s]) for score, (s, g) in zip(scores, units)]
    mixed = [
        fold_pairs(prob, view(r.v_cross, s, g)).astype(BF16) for prob, (s, g) in zip(probs, units)
    ]
    for prob, (s, g) in zip(probs, units):
        r.p_cross[m, s, g] = prob
    mixed = jnp.concatenate(
        [
            jnp.concatenate(mixed[s * r.quads : (s + 1) * r.quads], axis=1)
            for s in range(r.slots)
        ],
        axis=0,
    )
    r.mixed_cross[m] = mixed
    attn = mm_nt(mixed, columns(r, CROSS + 3))
    second, normed, factor = norm_forward(
        r.residual[m] + attn, r.norms[1:2, :], r.norms[4:5, :]
    )
    r.residual[m], r.factor[m, :, 1:2] = second, factor
    r.normed2[m] = normed.astype(BF16)
    r.second_low[m] = second.astype(BF16)


def tokens(ref):
    value = ref[...]
    return value.reshape(-1, value.shape[-1])


def pieces(r, i):
    return pl.ds(i * PIECE, PIECE), pl.ds(pl.multiple_of(i * PIECE * r.share, 512), PIECE * r.share)


def feed(r, i):
    j = lax.div(i, r.halves)
    some, rows = pieces(r, lax.rem(i, r.halves))
    low = tokens(r.second_low.at[some])
    up, down = columns(r, FEED + 2 * j), columns(r, FEED + 2 * j + 1)
    for at in range(0, 512, 256):
        inner = mm(low, up[:, at : at + 256])
        square = inner * inner
        bent = jnp.tanh(gelu_coef * inner * (1.0 + gelu_cube * square))
        half = 0.5 * (1.0 + bent)
        r.big1[j, rows, at : at + 256] = (inner * half).astype(BF16)
        slope = half + 0.5 * inner * (1.0 - bent * bent) * gelu_coef * (
            1.0 + 3.0 * gelu_cube * square
        )
        r.big2[j, rows, at : at + 256] = slope.astype(BF16)
    r.residual[some] += mm(r.big1[j, rows, :], down).reshape(PIECE, r.share, -1)


def third_norm(r, m):
    result, normed, factor = norm_forward(r.residual[m], r.norms[2:3, :], r.norms[5:6, :])
    r.d_first[m] = result.astype(BF16)
    d_third, gain, bias = norm_backward(
        r.cotangent[m].astype(F32), normed, factor, r.norms[2:3, :]
    )
    r.sums[2:3, :] += gain
    r.sums[5:6, :] += bias
    r.d_third[m] = d_third.astype(BF16)
    r.residual[m] = d_third


def feed_back(r, j):
    up, down = columns(r, FEED + 2 * j), columns(r, FEED + 2 * j + 1)
    for i in range(r.halves):
        some, rows = pieces(r, i)
        slope = r.big2[j, rows, :].astype(F32)
        d_inner = (mm_nt(tokens(r.d_third.at[some]), down) * slope).astype(BF16)
        r.big2[j, rows, :] = d_inner
        r.residual[some] += mm_nt(d_inner, up).reshape(PIECE, r.share, -1)


def feed_grad(r, j):
    store_columns(r.g_ffn, 2 * j, mm_tn(tokens(r.second_low), r.big2[j]).astype(BF16))
    store_columns(r.g_ffn, 2 * j + 1, mm_tn(r.big1[j], tokens(r.d_third)).astype(BF16))


def second_back(r, m):
    d_cross, gain, bias = norm_backward(
        r.residual[m], r.normed2[m].astype(F32), r.factor[m, :, 1:2], r.norms[1:2, :]
    )
    r.sums[1:2, :] += gain
    r.sums[4:5, :] += bias
    r.residual[m] = d_cross
    r.d_second[m] = d_cross.astype(BF16)


def clear_pads(r):
    for s in range(r.slots):
        r.big2[s] = jnp.zeros(r.big2.shape[1:], BF16)


def backward_cross(r, m):
    marks = head_marks()
    wide = window_rows()
    reach = r.frame - wide
    d_mixed = mm(r.d_second[m], columns(r, CROSS + 3)).astype(BF16)
    queries = r.q_cross[m]
    windows = [slot_window(r, m, s) for s in range(r.slots)]

    def view(ref, s, g):
        return ref[m, pl.ds(windows[s][0], wide), g * QUAD : (g + 1) * QUAD]

    d_queries = []
    for g in range(r.quads):
        d_q, d_k, d_v = attend_back(
            [
                (
                    r.p_cross[m, s, g],
                    view(r.k_cross, s, g),
                    view(r.v_cross, s, g),
                    cut(queries, s, g),
                    cut(d_mixed, s, g),
                )
                for s in range(r.slots)
            ],
            marks,
        )
        for s in range(r.slots):
            r.big2[s, reach : reach + wide, :QUAD] = d_k[s]
            r.big2[s, reach : reach + wide, QUAD:] = d_v[s]
        total = None
        for s in range(r.slots):
            piece = r.big2[s, pl.ds(slot_shift(r, m, s), r.frame), :]
            total = piece if total is None else total + piece
        r.k_cross[m, :, g * QUAD : (g + 1) * QUAD] = total[:, :QUAD]
        r.v_cross[m, :, g * QUAD : (g + 1) * QUAD] = total[:, QUAD:]
        d_queries.append(jnp.concatenate(d_q, axis=0))
    d_queries = jnp.concatenate(d_queries, axis=1)
    r.q_cross[m] = d_queries
    d_first = r.residual[m] + mm_nt(d_queries, columns(r, CROSS + 0))
    d_attn, gain, bias = norm_backward(d_first, r.normed1[m].astype(F32), r.factor[m, :, 0:1], r.norms[0:1, :])
    r.sums[0:1, :] += gain
    r.sums[3:4, :] += bias
    r.residual[m] = d_attn
    r.d_first[m] = d_attn.astype(BF16)
    source_term = mm_nt(r.k_cross[m], columns(r, CROSS + 1)) + mm_nt(
        r.v_cross[m], columns(r, CROSS + 2)
    )
    low, edge, half = source_term.astype(BF16), r.enc_len - r.frame, r.enc_len // 2
    shift = r.table[m, 1] * 16
    r.big2[0, reach:edge, :] = jnp.zeros((edge - reach, low.shape[1]), BF16)
    r.big2[0, edge:, :] = low
    r.big2[1, : r.frame, :] = low
    r.big1[m, :half, :] = r.big2[0, pl.ds(shift, half), :]
    r.big1[m, half:, :] = r.big2[1, pl.ds(shift + (half - edge), half), :]
    r.big2[0, edge:, :] = jnp.zeros_like(low)
    r.big2[1, : r.frame, :] = jnp.zeros_like(low)


def backward_self(r, m):
    marks = head_marks()
    d_mixed = mm(r.d_first[m], columns(r, SELF + 3)).astype(BF16)
    queries, keys, values = r.q_self[m], r.k_self[m], r.v_self[m]
    units = [(s, g) for s in range(r.slots) for g in range(r.quads)]
    parts = attend_back(
        [
            (
                r.p_self[m, s, g],
                cut(keys, s, g),
                cut(values, s, g),
                cut(queries, s, g),
                cut(d_mixed, s, g),
            )
            for s, g in units
        ],
        marks,
    )
    d_q, d_k, d_v = [
        jnp.concatenate([jnp.concatenate(part[g :: r.quads], axis=0) for g in range(r.quads)], axis=1)
        for part in parts
    ]
    r.q_self[m], r.k_self[m], r.v_self[m] = d_q, d_k, d_v
    r.cotangent[m] = (r.residual[m] + mm_nt(d_q, columns(r, SELF + 0))).astype(BF16)
    r.second_low[m] = (
        mm_nt(d_k, columns(r, SELF + 1)) + mm_nt(d_v, columns(r, SELF + 2))
    ).astype(BF16)


def weight_grad(r, kind):
    left, right = {
        SELF: (r.stream, r.q_self),
        SELF + 1: (r.context, r.k_self),
        SELF + 2: (r.context, r.v_self),
        SELF + 3: (r.d_first, r.mixed_self),
        CROSS: (r.first_low, r.q_cross),
        CROSS + 1: (r.source, r.k_cross),
        CROSS + 2: (r.source, r.v_cross),
        CROSS + 3: (r.d_second, r.mixed_cross),
    }[kind]
    store_columns(*grad_place(r, kind), mm_tn(tokens(left), tokens(right)).astype(BF16))


AXES = ("y", "core", "z", "x")
SIZES = {"y": NY, "core": NC, "z": NZ, "x": NX}


class Place:
    def __init__(self, groups):
        d, t = lax.axis_index(DP), lax.axis_index(TENSOR)
        high, self.low = lax.div(d, groups), lax.rem(d, groups)
        self.groups = groups
        self.a, self.b = lax.div(high, NX), lax.rem(high, NX)
        self.y, self.c = lax.div(t, NC), lax.rem(t, NC)
        self.t = t

    def device(self, a=None, b=None, y=None, c=None):
        a, b = self.a if a is None else a, self.b if b is None else b
        y, c = self.y if y is None else y, self.c if c is None else c
        return ((a * NX + b) * self.groups + self.low, y * NC + c)

    def up(self, k):
        return lax.rem(self.a + k, NZ)

    def peer(self, axis, k=0):
        if axis == "z":
            return self.device(a=self.up(k))
        if axis == "x":
            return self.device(b=1 - self.b)
        if axis == "y":
            return self.device(y=1 - self.y)
        if axis == "core":
            return self.device(c=1 - self.c)
        return self.device(y=1 - self.y, c=1 - self.c)

    def region(self, fixed):
        return tuple(fixed[a] if a in fixed else slice(None) for a in AXES)

    def own(self, axes):
        place = {"y": self.y, "core": self.c, "z": self.a, "x": self.b}
        return {a: place[a] for a in axes}

    def others(self, axis):
        if axis == "z":
            return [self.up(k) for k in range(1, NZ)]
        return [{"y": 1 - self.y, "core": 1 - self.c, "x": 1 - self.b}[axis]]

    def peers(self, axis):
        if axis == "z":
            return [self.peer("z", k) for k in range(1, NZ)]
        return [self.peer(axis)]


class Link:
    def __init__(self, r):
        self.r = r
        self.used = 0
        self.all = []

    def slot(self):
        self.used += 1
        return self.used - 1

    def send(self, key, source, target, device):
        return pltpu.make_async_remote_copy(
            src_ref=source,
            dst_ref=target,
            send_sem=self.r.send_sems.at[key],
            recv_sem=self.r.recv_sems.at[key],
            device_id=device,
            device_id_type=MESH,
        )


class Stages:
    def __init__(self, link, counts):
        self.link = link
        self.keys = [[link.slot() for _ in range(n)] for n in counts]
        link.all.append(self)

    def start(self, stage):
        for copy in self.copies(stage):
            copy.start()

    def wait(self, stage):
        for copy in self.copies(stage):
            copy.wait_recv()

    def last(self):
        self.wait(len(self.keys) - 1)

    def turn(self, stage):
        self.wait(stage)
        self.start(stage + 1)

    def drain(self):
        for stage in range(len(self.keys)):
            for copy in self.copies(stage):
                copy.wait_send()


class Gather(Stages):
    def __init__(self, link, place, first, count, order):
        self.axes = (*order, "core")
        super().__init__(link, [SIZES[a] - 1 for a in self.axes])
        self.p, self.kinds = place, pl.ds(first, count)

    def copies(self, stage):
        p, link = self.p, self.link
        region = p.region(p.own(self.axes[stage:]))
        ref = link.r.w.at[(self.kinds, *region)]
        peers = p.peers(self.axes[stage])
        return [link.send(key, ref, ref, peer) for key, peer in zip(self.keys[stage], peers)]


class GatherNorms(Stages):
    def __init__(self, link, place):
        super().__init__(link, (NZ - 1, 1))
        self.p = place

    def copies(self, stage):
        p, pack, send = self.p, self.link.r.pack, self.link.send
        keys = self.keys[stage]
        if stage == 0:
            ref = pack.at[p.a, p.b]
            return [send(keys[k - 1], ref, ref, p.peer("z", k)) for k in range(1, NZ)]
        ref = pack.at[:, p.b]
        return [send(keys[0], ref, ref, p.peer("x"))]


class Scatter(Stages):
    def __init__(self, link, place, first, count, order, boxes):
        self.axes = ("core", *order)
        super().__init__(link, [SIZES[a] - 1 for a in self.axes])
        self.p, self.count, self.boxes = place, count, boxes
        self.ref, self.first = grad_place(link.r, first)

    def copies(self, stage):
        p, link = self.p, self.link
        axis, kept = self.axes[stage], p.own(self.axes[:stage])
        peers, others = p.peers(axis), p.others(axis)
        out = []
        for i, key in enumerate(self.keys[stage]):
            region = p.region({**kept, axis: others[i]})
            source = self.ref.at[(pl.ds(self.first, self.count), *region)]
            out.append(link.send(key, source, self.boxes[stage].at[i], peers[i]))
        return out

    def summed(self, stage, k):
        at = (self.first + k, *self.p.region(self.p.own(self.axes[: stage + 1])))
        box = self.boxes[stage]
        if box.shape[0] == 1:
            return at, self.ref[at].astype(F32) + box[0, k].astype(F32)
        total = self.ref[at].astype(F32)
        for i in range(box.shape[0]):
            total = total + box[i, k].astype(F32)
        return at, total

    def turn(self, stage):
        if stage == len(self.keys) - 1:
            self.share.go()
            return
        self.wait(stage)
        for k in range(self.count):
            at, total = self.summed(stage, k)
            self.ref[at] = total.astype(BF16)
        self.start(stage + 1)

    def total(self, k):
        return self.summed(len(self.keys) - 1, k)[1]


def box_name(name, stage):
    return "box_%d_%d" % (name, stage)


def scatter_boxes(name, count, order):
    out, axes = [], ("core", *order)
    for i, axis in enumerate(axes):
        free = [SIZES[a] for a in AXES if a not in axes[: i + 1]]
        shape = (SIZES[axis] - 1, count, *free, 64, 128)
        out.append((box_name(name, i), pltpu.VMEM(shape, BF16)))
    return out


Q, K, V, O, C0, C1, F0, F1, F2, F3 = range(10)
SUM, ROWS = 10, 20
(
    START, SELF_FORWARD, NORM_FORWARD, CROSS_FORWARD, FEED_FORWARD, FEED_BACK,
    FEED_GRAD, NORM_BACK, CROSS_BACK, GRAD, SELF_BACK, TAIL,
) = range(12)
GATHERS = {
    Q: (SELF, 1, "zxy"),
    K: (SELF + 1, 1, "zyx"),
    V: (SELF + 2, 1, "yzx"),
    O: (SELF + 3, 1, "zxy"),
    C0: (CROSS, 2, "zxy"),
    C1: (CROSS + 2, 2, "zyx"),
    F0: (FEED, 2, "yzx"),
    F1: (FEED + 2, 2, "xzy"),
    F2: (FEED + 4, 2, "yxz"),
    F3: (FEED + 6, 2, "zyx"),
}
SCATTERS = {
    F0: (FEED, 2, "zxy"),
    F1: (FEED + 2, 2, "yxz"),
    F2: (FEED + 4, 2, "yxz"),
    F3: (FEED + 6, 2, "zxy"),
    C0: (CROSS, 2, "yxz"),
    C1: (CROSS + 2, 2, "xzy"),
    O: (SELF + 3, 1, "zyx"),
    Q: (SELF, 1, "xyz"),
    K: (SELF + 1, 1, "zyx"),
    V: (SELF + 2, 1, "xzy"),
}
LATE = 2
PLAN = {
    (START, 0): ((K, -1), (F1, -1), (F2, -1), (Q, -1), (F2, 0), (C0, -1), (K, 0), (O, -1), (Q, 0),),
    (START, 1): ((V, -1), (C1, -1), (C0, 0), (K, 1), (V, 0), (Q, 1), (F0, -1), (F0, 0), (C1, 0),),
    (START, 2): ((O, 0), (C0, 1), (V, 1), (O, 1), (F1, 0), (Q, 2), (C1, 1), (F3, -1), (V, 2), (K, 2),),
    (SELF_FORWARD, 3): ((F0, 1), (O, 2),),
    (NORM_FORWARD, 0): ((C1, 2), (F2, 1), (C0, 2),),
    (NORM_FORWARD, 1): ((F3, 0),),
    (CROSS_FORWARD, 0): ((F1, 1),),
    (CROSS_FORWARD, 2): ((F3, 1),),
    (CROSS_FORWARD, 3): ((F0, 2),),
    (FEED_FORWARD, 0): ((F1, 2),),
    (FEED_FORWARD, 2): ((F2, 2),),
    (FEED_FORWARD, 3): ((F3, 2),),
    (FEED_BACK, 2): ((SUM + F0, 0),),
    (FEED_BACK, 3): ((SUM + F1, 0),),
    (NORM_BACK, 0): ((SUM + F2, 0),),
    (CROSS_BACK, 0): ((SUM + F3, 0),),
    (CROSS_BACK, 2): ((ROWS + 0, 0),),
    (GRAD, SELF + 3): ((SUM + F2, 1), (SUM + F1, 1), (ROWS + 1, 0),),
    (SELF_BACK, 0): ((ROWS + 2, 0), (ROWS + 3, 0), (SUM + F0, 1),),
    (SELF_BACK, 1): ((SUM + O, 0),),
    (GRAD, SELF + 2): ((SUM + F2, 2), (SUM + F3, 1),),
    (GRAD, CROSS): ((SUM + V, 0), (SUM + F1, 2),),
    (GRAD, CROSS + 3): ((SUM + F0, 2), (SUM + Q, 0),),
    (TAIL, 0): ((SUM + F3, 2), (SUM + K, 0), (SUM + C0, 0), (SUM + V, 1), (SUM + C1, 0), (SUM + C1, 1), (SUM + V, 2), (SUM + Q, 1), (SUM + K, 1), (SUM + F0, 3),),
    (TAIL, 1): ((SUM + C0, 1), (SUM + F3, 3), (SUM + F1, 3), (SUM + Q, 2), (SUM + O, 1), (SUM + C0, 2), (SUM + F2, 3), (SUM + C1, 2), (SUM + O, 2), (SUM + K, 2),),
}


class ScatterNorms(Stages):
    def __init__(self, link, place):
        super().__init__(link, (1, 1, 1, NZ - 1))
        self.p = place

    def copies(self, stage):
        p, r, send, keys = self.p, self.link.r, self.link.send, self.keys[stage]
        if stage == 0:
            return [send(keys[0], r.g_norm, r.n_box0, p.peer("core"))]
        if stage == 1:
            return [send(keys[0], r.n_box0, r.n_box1, p.peer("y"))]
        if stage == 2:
            return [send(keys[0], r.n_box1.at[:, 1 - p.b], r.n_box2, p.peer("x"))]
        return [
            send(keys[k - 1], r.n_box2.at[p.up(k)], r.n_box3.at[k - 1], p.peer("z", k))
            for k in range(1, NZ)
        ]

    def step(self, stage):
        p, r = self.p, self.link.r
        self.wait(stage)
        if stage == 0:
            r.n_box0[...] = r.g_norm[...] + r.n_box0[...]
        elif stage == 1:
            r.n_box1[...] = r.n_box0[...] + r.n_box1[...]
        else:
            r.n_box2[...] = r.n_box1[:, p.b] + r.n_box2[...]
        self.start(stage + 1)

    def total(self):
        r = self.link.r
        return r.n_box2[self.p.a] + ((r.n_box3[0] + r.n_box3[1]) + r.n_box3[2])


class ScatterEncoder(Stages):
    def __init__(self, link, place, share, micro):
        super().__init__(link, (NY * micro, micro))
        self.p, self.share, self.micro = place, share, micro
        self.boxes = (link.r.d_third, link.r.second_low)

    def rows(self, m, y, c):
        at = pl.multiple_of((y * NC + c) * self.share, self.share)
        return self.link.r.big1.at[m, pl.ds(at, self.share), :]

    def one(self, stage, m):
        p, r, send = self.p, self.link.r, self.link.send
        key = self.keys[stage][0]
        if stage == 0:
            return [
                send(
                    key + NY * m + y,
                    self.rows(m, y, 1 - p.c),
                    self.boxes[y].at[m],
                    p.peer("core"),
                )
                for y in range(NY)
            ]
        return [send(key + m, self.rows(m, 1 - p.y, p.c), r.e_box1.at[m], p.peer("y"))]

    def copies(self, stage):
        return [copy for m in range(self.micro) for copy in self.one(stage, m)]

    def begin(self, m):
        for copy in self.one(0, m):
            copy.start()

    def step(self, m):
        for copy in self.one(0, m):
            copy.wait_recv()
        for y in range(NY):
            ref = self.rows(m, y, self.p.c)
            ref[...] = ref[...] + self.boxes[y][m]
        for copy in self.one(1, m):
            copy.start()

    def finish(self):
        self.wait(1)
        for m in range(self.micro):
            ref = self.rows(m, self.p.y, self.p.c)
            ref[...] = ref[...] + self.link.r.e_box1[m]


class EncoderPart:
    def __init__(self, rows, m):
        self.rows, self.m = rows, m

    def turn(self, stage):
        self.rows.step(self.m)


class ShareFfn(Stages):
    def __init__(self, link, place, box, first, item):
        super().__init__(link, (3,))
        self.p, self.box, self.first, self.item = place, box, first, item

    def copies(self, stage):
        p, send, keys = self.p, self.link.send, self.keys[0]
        ref = self.box.at[p.t, pl.ds(self.first, self.item.count)]
        axes = ("core", "y", "both")
        return [send(keys[i], ref, ref, p.peer(axes[i])) for i in range(3)]

    def go(self):
        self.item.last()
        for k in range(self.item.count):
            self.box[self.p.t, self.first + k] = self.item.total(k).astype(BF16)
        self.start(0)


def each(count, body, ticks=None):
    def step(i, carry):
        for k, tick in (ticks or {}).items():
            pl.when(i == k)(tick)
        body(i)
        return carry

    lax.fori_loop(0, count, step, 0)


SEMS = 160


def layer_kernel(names, groups, scale, *refs):
    r = Refs()
    for name, ref in zip(names, refs):
        setattr(r, name, ref)
    micro, r.share = r.stream.shape[0], r.stream.shape[1]
    r.slots = r.share // SLOT
    r.quads = r.stream.shape[2] // QUAD
    r.enc_len = r.encoder.shape[1]
    r.frame = frame_rows(r.share)
    r.halves = micro // PIECE
    p = Place(groups)
    link = Link(r)

    mine = pl.ds(pl.multiple_of(p.t * r.share, r.share), r.share)
    half = pl.ds(pl.multiple_of(p.t * (r.share // 2), r.share // 2), r.share // 2)
    pairs = [
        (r.self_query, r.w.at[SELF, p.y, p.c, p.a, p.b]),
        (r.self_key_value, r.w.at[pl.ds(SELF + 1, 2), p.y, p.c, p.a, p.b]),
        (r.cross_query, r.w.at[CROSS, p.y, p.c, p.a, p.b]),
        (r.cross_key_value, r.w.at[pl.ds(CROSS + 1, 2), p.y, p.c, p.a, p.b]),
        (r.self_output, r.w.at[SELF + 3, p.y, p.c, p.a, p.b]),
        (r.cross_output, r.w.at[CROSS + 3, p.y, p.c, p.a, p.b]),
    ]
    down = pl.ds(pl.multiple_of(p.t * 128, 128), 128)
    for j in range(4):
        pairs.append(
            (
                r.ffn_out.at[pl.ds(j * 64, 64), down],
                r.w.at[FEED + 2 * j + 1, p.y, p.c, p.a, p.b],
            )
        )
    up = pl.ds(pl.multiple_of(p.t * 512, 512), 512)
    pairs.append((r.ffn_in.at[:, up], r.own_up))
    weights = len(pairs)
    pairs += [
        (r.stream_hbm.at[:, mine, :], r.stream),
        (r.context_hbm.at[:, mine, :], r.context),
        (r.masks_hbm.at[:, half, :], r.masks),
        (r.encoder, r.big1),
        (r.out_grad, r.cotangent),
    ]
    copies = [
        pltpu.make_async_copy(source, target, r.sems.at[i])
        for i, (source, target) in enumerate(pairs)
    ]
    for copy in copies:
        copy.start()
    partners = [p.peer("z", k) for k in range(1, NZ)]
    partners += [p.peer(axis) for axis in ("x", "y", "core", "both")]
    barrier = pltpu.get_barrier_semaphore()
    for device in partners:
        pl.semaphore_signal(barrier, inc=1, device_id=device, device_id_type=MESH)
    r.pack[p.a, p.b, 0:3, :64] = r.norm_gain[...].astype(F32)
    r.pack[p.a, p.b, 3:6, :64] = r.norm_bias[...].astype(F32)
    for copy in copies[:weights]:
        copy.wait()
    for j in range(4):
        at = j * 64
        r.w[FEED + 2 * j, p.y, p.c, p.a, p.b] = jnp.concatenate(
            [r.own_up[:, at : at + 64], r.own_up[:, 256 + at : 320 + at]], axis=1
        )
    pl.semaphore_wait(barrier, len(partners))

    chains = {name: Gather(link, p, *spec) for name, spec in GATHERS.items()}
    norms = GatherNorms(link, p)

    def run(phase, step):
        for name, stage in PLAN.get((phase, step), ()):
            if stage < 0:
                chains[name].start(0)
            else:
                chains[name].turn(stage)

    def loop(phase, count, body, needs=None):
        ticks = {}
        for i in range(count):
            names = (needs or {}).get(i, ())
            if PLAN.get((phase, i)) or names:

                def tick(i=i, names=names):
                    run(phase, i)
                    for name in names:
                        chains[name].last()

                ticks[i] = tick
        each(count, functools.partial(body, r), ticks)

    r.sums[...] = jnp.zeros(r.sums.shape, F32)
    run(START, 0)
    norms.start(0)
    run(START, 1)
    norms.wait(0)
    norms.start(1)
    for copy in copies[weights:]:
        copy.wait()
    run(START, 2)
    for name in (Q, K, V):
        chains[name].last()
    loop(SELF_FORWARD, micro, forward_self)
    norms.wait(1)
    r.norms[...] = jnp.concatenate(
        [r.pack[d // NX, d % NX, :, :64] for d in range(NZ * NX)], axis=1
    )
    loop(NORM_FORWARD, micro, first_norm, {0: (O,)})
    loop(CROSS_FORWARD, micro, forward_cross, {0: (C0, C1)})
    loop(FEED_FORWARD, 4 * r.halves, feed, {j * r.halves: (F0 + j,) for j in range(4)})
    for item in link.all:
        item.drain()
    link.all = []
    each(micro, functools.partial(third_norm, r))
    out = [pltpu.make_async_copy(r.d_first, r.block_out, r.sems.at[0])]
    out[0].start()

    sums = {}
    for name, spec in SCATTERS.items():
        boxes = [getattr(r, box_name(name, i)) for i in range(1 + len(spec[2]))]
        sums[name] = Scatter(link, p, *spec, boxes)
        if name >= F0:
            sums[name].share = ShareFfn(link, p, r.all_ffn, 2 * (name - F0), sums[name])
    norm_sums = ScatterNorms(link, p)
    rows = ScatterEncoder(link, p, r.share, micro)
    chains = {SUM + name: item for name, item in sums.items()}
    for m in range(micro):
        chains[ROWS + m] = EncoderPart(rows, m)

    def feed_both(j):
        for i in range(4):
            pl.when(j == i)(functools.partial(run, FEED_BACK, i))
        feed_back(r, j)
        for i in range(4):
            pl.when(j == i)(functools.partial(run, FEED_GRAD, i))
        feed_grad(r, j)
        for i in range(4):
            pl.when(j == i)(functools.partial(sums[F0 + i].start, 0))

    each(4, feed_both)
    run(NORM_BACK, 0)
    each(micro, functools.partial(second_back, r))
    clear_pads(r)
    out[0].wait()

    def cross_back(r, m):
        backward_cross(r, m)
        rows.begin(m)

    loop(CROSS_BACK, micro, cross_back)
    for d in range(NZ * NX):
        r.g_norm[d // NX, d % NX] = jnp.zeros(r.g_norm.shape[2:], F32)
        r.g_norm[d // NX, d % NX, :, :64] = r.sums[:, d * 64 : (d + 1) * 64]
    norm_sums.start(0)

    def grad(kind):
        run(GRAD, kind)
        weight_grad(r, kind)

    def cross_grads(pair):
        for k in (2 * pair, 2 * pair + 1):
            grad(CROSS + k)
        sums[C0 + pair].start(0)

    for pair in range(2 - LATE):
        cross_grads(pair)
    norm_sums.step(0)
    grad(SELF + 3)
    sums[O].start(0)
    norm_sums.step(1)
    loop(SELF_BACK, micro, backward_self)
    out = [
        pltpu.make_async_copy(r.cotangent, r.stream_grad, r.sems.at[0]),
        pltpu.make_async_copy(r.second_low, r.context_grad, r.sems.at[1]),
    ]
    for copy in out:
        copy.start()
    norm_sums.step(2)
    for name, kind in ((V, SELF + 2), (Q, SELF), (K, SELF + 1)):
        grad(kind)
        sums[name].start(0)
    for pair in range(2 - LATE, 2):
        cross_grads(pair)
    run(TAIL, 0)
    rows.finish()
    mine = pl.ds(pl.multiple_of(p.t * r.share, r.share), r.share)
    out.append(pltpu.make_async_copy(r.big1.at[:, mine, :], r.encoder_grad, r.sems.at[2]))
    out[2].start()
    run(TAIL, 1)
    for j in range(4):
        sums[F0 + j].share.wait(0)
    for t in range(NY * NC):
        halves = [
            r.all_ffn[t, 2 * j, :, h * 64 : (h + 1) * 64] for h in range(2) for j in range(4)
        ]
        r.grad_ffn_in[:, t * 512 : (t + 1) * 512] = (
            jnp.concatenate(halves, axis=1).astype(F32) * scale
        )
        for j in range(4):
            r.grad_ffn_out[j * 64 : (j + 1) * 64, t * 128 : (t + 1) * 128] = (
                r.all_ffn[t, 2 * j + 1].astype(F32) * scale
            )
    norm_sums.wait(3)
    total = norm_sums.total() * scale
    r.grad_norm_gain[...] = total[0:3, :64]
    r.grad_norm_bias[...] = total[3:6, :64]
    for name in (C0, C1, O, Q, K, V):
        sums[name].last()
    r.grad_cross_query[...] = sums[C0].total(0) * scale
    r.grad_cross_key_value[0] = sums[C0].total(1) * scale
    r.grad_cross_key_value[1] = sums[C1].total(0) * scale
    r.grad_cross_output[...] = sums[C1].total(1) * scale
    r.grad_self_output[...] = sums[O].total(0) * scale
    r.grad_self_query[...] = sums[Q].total(0) * scale
    r.grad_self_key_value[0] = sums[K].total(0) * scale
    r.grad_self_key_value[1] = sums[V].total(0) * scale
    for item in link.all:
        item.drain()
    for copy in out:
        copy.wait()


def vmem():
    return pl.BlockSpec(memory_space=pltpu.VMEM)


def hbm():
    return pl.BlockSpec(memory_space=pl.ANY)


WEIGHTS = (
    "self_query", "self_key_value", "self_output",
    "cross_query", "cross_key_value", "cross_output",
    "ffn_in", "ffn_out", "norm_gain", "norm_bias",
)


def layer(groups, scale, stream, context, encoder, masks, table, out_grad, weights):
    micro, row, width = stream.shape
    share = out_grad.shape[1]
    enc_len = encoder.shape[1]
    frame, wide = frame_rows(share), window_rows()
    slots, quads = share // SLOT, width // QUAD
    small = ("norm_gain", "norm_bias")
    ins = [
        ("stream_hbm", stream, hbm()),
        ("context_hbm", context, hbm()),
        ("encoder", encoder, hbm()),
        ("masks_hbm", masks, hbm()),
        ("table", table, pl.BlockSpec(memory_space=pltpu.SMEM)),
        ("out_grad", out_grad, hbm()),
    ]
    for name, value in zip(WEIGHTS, weights):
        ins.append((name, value, vmem() if name in small else hbm()))
    part = jax.ShapeDtypeStruct((micro, share, width), BF16)
    outs = [
        ("block_out", part, hbm()),
        ("stream_grad", part, hbm()),
        ("context_grad", part, hbm()),
        ("encoder_grad", part, hbm()),
    ]
    for name, value in zip(WEIGHTS, weights):
        outs.append(("grad_" + name, jax.ShapeDtypeStruct(value.shape, F32), vmem()))
    low = pltpu.VMEM((micro, share, width), BF16)
    high = pltpu.VMEM((micro, share, width), F32)
    window = pltpu.VMEM((micro, frame, width), BF16)
    big = pltpu.VMEM((micro, enc_len, width), BF16)
    norm = pltpu.VMEM((NZ, NX, 8, 128), F32)
    scratch = [
        ("w", pltpu.VMEM((KINDS, NY, NC, NZ, NX, 64, 128), BF16)),
        ("g_ffn", pltpu.VMEM((8, NY, NC, NZ, NX, 64, 128), BF16)),
        ("stream", low),
        ("context", low),
        ("cotangent", low),
        ("masks", pltpu.VMEM((micro, share // 2, 128), jnp.int32)),
        ("q_self", low),
        ("k_self", low),
        ("v_self", low),
        ("mixed_self", low),
        ("first_low", low),
        ("q_cross", low),
        ("k_cross", window),
        ("v_cross", window),
        ("source", window),
        ("mixed_cross", low),
        ("second_low", low),
        ("d_third", low),
        ("d_second", low),
        ("d_first", low),
        ("p_self", pltpu.VMEM((micro, slots, quads, SLOT, QUAD), BF16)),
        ("p_cross", pltpu.VMEM((micro, slots, quads, wide, QUAD), BF16)),
        ("residual", high),
        ("normed1", low),
        ("normed2", low),
        ("factor", pltpu.VMEM((micro, share, 2), F32)),
        ("big1", big),
        ("big2", big),
        ("own_up", pltpu.VMEM((64, 512), BF16)),
        ("norms", pltpu.VMEM((8, width), F32)),
        ("sums", pltpu.VMEM((8, width), F32)),
        ("pack", norm),
        ("g_norm", norm),
        ("n_box0", norm),
        ("n_box1", norm),
        ("n_box2", pltpu.VMEM((NZ, 8, 128), F32)),
        ("n_box3", pltpu.VMEM((NZ - 1, 8, 128), F32)),
        ("e_box1", low),
        ("all_ffn", pltpu.VMEM((NY * NC, 8, 64, 128), BF16)),
        ("sems", pltpu.SemaphoreType.DMA((19,))),
        ("send_sems", pltpu.SemaphoreType.DMA((SEMS,))),
        ("recv_sems", pltpu.SemaphoreType.DMA((SEMS,))),
    ]
    for name, (_, count, order) in SCATTERS.items():
        scratch += scatter_boxes(name, count, order)
    names = [item[0] for item in ins + outs + scratch]
    return pl.pallas_call(
        functools.partial(layer_kernel, names, groups, scale),
        out_shape=[item[1] for item in outs],
        in_specs=[item[2] for item in ins],
        out_specs=[item[2] for item in outs],
        scratch_shapes=[item[1] for item in scratch],
        compiler_params=pltpu.CompilerParams(
            vmem_limit_bytes=VMEM_LIMIT, collective_id=0, has_side_effects=True
        ),
        cost_estimate=pl.CostEstimate(
            flops=30_000_000_000, bytes_accessed=30_000_000, transcendentals=4_000_000
        ),
    )(*[item[1] for item in ins])


def copy_kernel(count, *refs):
    given, results, held = (refs[i * count : (i + 1) * count] for i in range(3))
    sems = refs[3 * count]
    loads = [pltpu.make_async_copy(a, b, sems.at[0, i]) for i, (a, b) in enumerate(zip(given, held))]
    stores = [
        pltpu.make_async_copy(a, b, sems.at[1, i]) for i, (a, b) in enumerate(zip(held, results))
    ]
    for load in loads:
        load.start()
    for load, store in zip(loads, stores):
        load.wait()
        store.start()
    for store in stores:
        store.wait()


def copy_all(values):
    count = len(values)
    return pl.pallas_call(
        functools.partial(copy_kernel, count),
        out_shape=[jax.ShapeDtypeStruct(v.shape, v.dtype) for v in values],
        in_specs=[hbm()] * count,
        out_specs=[hbm()] * count,
        scratch_shapes=[pltpu.VMEM(v.shape, v.dtype) for v in values]
        + [pltpu.SemaphoreType.DMA((2, count))],
        compiler_params=pltpu.CompilerParams(vmem_limit_bytes=VMEM_LIMIT),
    )(*values)


GATHER_DIM = (0, 1, 0, 0, 1, 0, 0, 0, 1, 1)


def per_device(
    query_stream,
    context_stream,
    encoder_out,
    query_masks,
    source_segments,
    out_grad,
    *weights,
):
    micro, row, width = query_stream.shape
    share = out_grad.shape[1]
    slots = share // SLOT
    t = lax.axis_index(TENSOR)
    replicas = lax.axis_size(DP)
    scale = float(micro * row * replicas) ** (-0.5)
    groups = replicas // (NZ * NX)
    weights = [item.T if i in (2, 5) else item for i, item in enumerate(weights)]
    near = [[i * groups + j for j in range(groups)] for i in range(NZ * NX)]
    if groups > 1:
        weights = [
            lax.all_gather(item, DP, axis=dim, tiled=True, axis_index_groups=near)
            for item, dim in zip(weights, GATHER_DIM)
        ]
    bounds = t * slots + jnp.arange(slots + 1, dtype=jnp.int32)
    starts = jnp.sum(
        (source_segments < bounds[None, :, None]).astype(jnp.int32), axis=-1
    )
    table = window_table(starts, share, encoder_out.shape[1])
    results = layer(
        groups, scale, query_stream, context_stream, encoder_out, query_masks, table,
        out_grad, weights,
    )
    results = copy_all(results)
    grads = results[4:]
    if groups > 1:
        grads = [
            lax.psum_scatter(
                item, DP, scatter_dimension=dim, tiled=True, axis_index_groups=near
            )
            for item, dim in zip(grads, GATHER_DIM)
        ]
    grads = [item.T if i in (2, 5) else item for i, item in enumerate(grads)]
    return (*results[:4], *grads)


def solution(mesh):
    in_specs = (
        P(None, DP, None),
        P(None, DP, None),
        P(None, DP, None),
        P(None, DP, None),
        P(None, DP, None),
        P(None, (DP, TENSOR), None),
        P(DP, TENSOR),
        P(None, DP, TENSOR),
        P(TENSOR, DP),
        P(DP, TENSOR),
        P(None, DP, TENSOR),
        P(TENSOR, DP),
        P(DP, None),
        P(DP, None),
        P(None, DP),
        P(None, DP),
    )
    out_specs = (
        P(None, (DP, TENSOR), None),
        P(None, (DP, TENSOR), None),
        P(None, (DP, TENSOR), None),
        P(None, (DP, TENSOR), None),
        P(DP, TENSOR),
        P(None, DP, TENSOR),
        P(TENSOR, DP),
        P(DP, TENSOR),
        P(None, DP, TENSOR),
        P(TENSOR, DP),
        P(DP, None),
        P(DP, None),
        P(None, DP),
        P(None, DP),
    )
    return jax.shard_map(
        per_device, mesh=mesh, in_specs=in_specs, out_specs=out_specs, check_vma=False
    )
```

```python
import functools

import jax
import jax.numpy as jnp
from jax import lax
from jax.experimental import pallas as pl
from jax.experimental.pallas import tpu as pltpu
from jax.sharding import PartitionSpec as P

HEAD_DIM = 64
SLOT = 64
SEG_MOST = 128
QUAD = 4 * HEAD_DIM
PAIR = 2 * HEAD_DIM
NZ, NX, NY, NC = 4, 2, 2, 2
PIECE = 2
SELF, CROSS, FEED, KINDS = 0, 4, 8, 16
BF16 = jnp.bfloat16
F32 = jnp.float32
MESH = pl.DeviceIdType.MESH
DP, TENSOR = "dp", "tensor"

epsilon = 1e-05
neg_fill = -1e30
gelu_coef = 0.7978845608028654
gelu_cube = 0.044715
VMEM_LIMIT = 65400 * 1024


def mm(left, right):
    return jnp.dot(left, right, preferred_element_type=F32)


def mm_nt(left, right):
    return lax.dot_general(left, right, (((1,), (1,)), ((), ())), preferred_element_type=F32)


def mm_tn(left, right):
    return lax.dot_general(left, right, (((0,), (0,)), ((), ())), preferred_element_type=F32)


def norm_forward(value, gain, bias):
    center = jnp.mean(value, axis=-1, keepdims=True)
    shifted = value - center
    factor = lax.rsqrt(jnp.mean(shifted * shifted, axis=-1, keepdims=True) + epsilon)
    normed = shifted * factor
    return normed * gain + bias, normed, factor


def norm_backward(incoming, normed, factor, gain):
    scaled = incoming * gain
    inside = (
        scaled
        - jnp.mean(scaled, axis=-1, keepdims=True)
        - normed * jnp.mean(scaled * normed, axis=-1, keepdims=True)
    )
    return (
        factor * inside,
        jnp.sum(incoming * normed, axis=0, keepdims=True),
        jnp.sum(incoming, axis=0, keepdims=True),
    )


def columns(r, kind):
    parts = [r.w[kind, t // NC, t % NC].reshape(-1, 128) for t in range(NY * NC)]
    return jnp.concatenate(parts, axis=1)


def grad_place(r, kind):
    if kind >= FEED:
        return r.g_ffn, kind - FEED
    return r.w, kind + FEED


def store_columns(ref, at, value):
    for t in range(NY * NC):
        ref[at, t // NC, t % NC] = value[:, t * 128 : (t + 1) * 128].reshape(NZ // 2, 2, NX, -1, 128)


def head_marks():
    lane = lax.broadcasted_iota(jnp.int32, (1, QUAD), 1) // HEAD_DIM
    return [jnp.where(lane == h, 1.0, 0.0).astype(BF16) for h in range(4)]


def spread_heads(rows, marks):
    return jnp.concatenate([rows * mark for mark in marks], axis=0)


def fold_pairs(weights, rows):
    first = lax.broadcasted_iota(jnp.int32, (SLOT, PAIR), 1) < HEAD_DIM
    parts = []
    for p in range(2):
        cut = slice(p * PAIR, (p + 1) * PAIR)
        full = mm_tn(weights[:, cut], rows[:, cut])
        parts.append(jnp.where(first, full[:SLOT], full[SLOT:]))
    return jnp.concatenate(parts, axis=1)


def soft_keys(scores, allowed):
    scores = jnp.where(allowed, scores, neg_fill)
    top = jnp.max(scores, axis=0, keepdims=True)
    raised = jnp.exp(scores - top)
    return (raised * (1.0 / jnp.sum(raised, axis=0, keepdims=True))).astype(BF16)


def attend_back(items, marks):
    d_spread = [spread_heads(item[4], marks) for item in items]
    d_probs = [mm_nt(item[2], spread) for item, spread in zip(items, d_spread)]
    d_values = [mm(item[0], spread).astype(BF16) for item, spread in zip(items, d_spread)]
    d_scores = []
    for item, d_prob in zip(items, d_probs):
        wide = item[0].astype(F32)
        inner = jnp.sum(wide * d_prob, axis=0, keepdims=True)
        d_scores.append((wide * (d_prob - inner)).astype(BF16))
    d_keys = [
        mm(d_score, spread_heads(item[3], marks)).astype(BF16)
        for item, d_score in zip(items, d_scores)
    ]
    d_queries = [
        (fold_pairs(d_score, item[1]) * HEAD_DIM ** (-0.5)).astype(BF16)
        for item, d_score in zip(items, d_scores)
    ]
    return d_queries, d_keys, d_values


def cut(value, s, g):
    return value[s * SLOT : (s + 1) * SLOT, g * QUAD : (g + 1) * QUAD]


class Refs:
    pass


def frame_rows(share):
    return (share // SLOT) * SEG_MOST + 16


def window_rows():
    return SEG_MOST + 16


def window_table(starts, share, enc_len):
    frame, wide = frame_rows(share), window_rows()
    base = jnp.minimum(starts[:, :1] // 16 * 16, enc_len - frame)
    begin = starts[:, :-1] - base
    at = jnp.minimum(begin // 16 * 16, frame - wide)
    low = begin - at
    high = low + starts[:, 1:] - starts[:, :-1]
    return jnp.concatenate(
        [base // 16, (enc_len - frame - base) // 16, at // 16, low, high, (frame - wide - at) // 16],
        axis=1,
    )


def frame_start(r, m):
    return r.table[m, 0] * 16


def slot_window(r, m, s):
    at = r.table[m, 2 + s] * 16
    return at, r.table[m, 2 + r.slots + s], r.table[m, 2 + 2 * r.slots + s]


def slot_shift(r, m, s):
    return r.table[m, 2 + 3 * r.slots + s] * 16


def forward_self(r, m):
    marks = head_marks()
    stream, context = r.stream[m], r.context[m]
    queries = (mm(stream, columns(r, SELF + 0)) * HEAD_DIM ** (-0.5)).astype(BF16)
    keys = mm(context, columns(r, SELF + 1)).astype(BF16)
    values = mm(context, columns(r, SELF + 2)).astype(BF16)
    r.q_self[m], r.k_self[m], r.v_self[m] = queries, keys, values
    row = lax.broadcasted_iota(jnp.int32, (SLOT, QUAD), 0)
    lane = lax.broadcasted_iota(jnp.int32, (SLOT, QUAD), 1) % SLOT
    place = jnp.where(lane == 2 * (row % 32) + row // 32, 1.0, 0.0).astype(BF16)
    units = [(s, g) for s in range(r.slots) for g in range(r.quads)]
    allowed = []
    for s in range(r.slots):
        bits = r.masks[m, s * 32 : (s + 1) * 32].astype(F32)
        bits = jnp.concatenate([bits[:, :SLOT], bits[:, SLOT:]], axis=0).astype(BF16)
        allowed.append(mm_tn(bits, place) > 0.5)
    scores = [mm_nt(cut(keys, s, g), spread_heads(cut(queries, s, g), marks)) for s, g in units]
    probs = [soft_keys(score, allowed[s]) for score, (s, g) in zip(scores, units)]
    mixed = [fold_pairs(prob, cut(values, s, g)).astype(BF16) for prob, (s, g) in zip(probs, units)]
    for prob, one, (s, g) in zip(probs, mixed, units):
        r.p_self[m, s, g] = prob
        r.mixed_self[m, s * SLOT : (s + 1) * SLOT, g * QUAD : (g + 1) * QUAD] = one


def first_norm(r, m):
    attn = mm_nt(r.mixed_self[m], columns(r, SELF + 3))
    first, normed, factor = norm_forward(
        r.stream[m].astype(F32) + attn, r.norms[0:1, :], r.norms[3:4, :]
    )
    r.residual[m], r.factor[m, :, 0:1] = first, factor
    r.normed1[m] = normed.astype(BF16)
    r.first_low[m] = first.astype(BF16)


def forward_cross(r, m):
    marks = head_marks()
    base = frame_start(r, m)
    source = r.big1[m, pl.ds(base, r.frame), :]
    r.source[m] = source
    r.k_cross[m] = mm(source, columns(r, CROSS + 1)).astype(BF16)
    r.v_cross[m] = mm(source, columns(r, CROSS + 2)).astype(BF16)
    queries = (mm(r.first_low[m], columns(r, CROSS + 0)) * HEAD_DIM ** (-0.5)).astype(BF16)
    r.q_cross[m] = queries
    wide = window_rows()
    row = lax.broadcasted_iota(jnp.int32, (wide, QUAD), 0)
    units = [(s, g) for s in range(r.slots) for g in range(r.quads)]
    windows = [slot_window(r, m, s) for s in range(r.slots)]
    allowed = [(row >= low) & (row < high) for _, low, high in windows]

    def view(ref, s, g):
        return ref[m, pl.ds(windows[s][0], wide), g * QUAD : (g + 1) * QUAD]

    scores = [
        mm_nt(view(r.k_cross, s, g), spread_heads(cut(queries, s, g), marks)) for s, g in units
    ]
    probs = [soft_keys(score, allowed[s]) for score, (s, g) in zip(scores, units)]
    mixed = [
        fold_pairs(prob, view(r.v_cross, s, g)).astype(BF16) for prob, (s, g) in zip(probs, units)
    ]
    for prob, (s, g) in zip(probs, units):
        r.p_cross[m, s, g] = prob
    mixed = jnp.concatenate(
        [
            jnp.concatenate(mixed[s * r.quads : (s + 1) * r.quads], axis=1)
            for s in range(r.slots)
        ],
        axis=0,
    )
    r.mixed_cross[m] = mixed
    attn = mm_nt(mixed, columns(r, CROSS + 3))
    second, normed, factor = norm_forward(
        r.residual[m] + attn, r.norms[1:2, :], r.norms[4:5, :]
    )
    r.residual[m], r.factor[m, :, 1:2] = second, factor
    r.normed2[m] = normed.astype(BF16)
    r.second_low[m] = second.astype(BF16)


def tokens(ref):
    value = ref[...]
    return value.reshape(-1, value.shape[-1])


def pieces(r, i):
    return pl.ds(i * PIECE, PIECE), pl.ds(pl.multiple_of(i * PIECE * r.share, 512), PIECE * r.share)


def feed(r, i):
    j = lax.div(i, r.halves)
    some, rows = pieces(r, lax.rem(i, r.halves))
    low = tokens(r.second_low.at[some])
    up, down = columns(r, FEED + 2 * j), columns(r, FEED + 2 * j + 1)
    for at in range(0, 512, 256):
        inner = mm(low, up[:, at : at + 256])
        square = inner * inner
        bent = jnp.tanh(gelu_coef * inner * (1.0 + gelu_cube * square))
        half = 0.5 * (1.0 + bent)
        r.big1[j, rows, at : at + 256] = (inner * half).astype(BF16)
        slope = half + 0.5 * inner * (1.0 - bent * bent) * gelu_coef * (
            1.0 + 3.0 * gelu_cube * square
        )
        r.big2[j, rows, at : at + 256] = slope.astype(BF16)
    r.residual[some] += mm(r.big1[j, rows, :], down).reshape(PIECE, r.share, -1)


def third_norm(r, m):
    result, normed, factor = norm_forward(r.residual[m], r.norms[2:3, :], r.norms[5:6, :])
    r.d_first[m] = result.astype(BF16)
    d_third, gain, bias = norm_backward(
        r.cotangent[m].astype(F32), normed, factor, r.norms[2:3, :]
    )
    r.sums[2:3, :] += gain
    r.sums[5:6, :] += bias
    r.d_third[m] = d_third.astype(BF16)
    r.residual[m] = d_third


def feed_back(r, j):
    up, down = columns(r, FEED + 2 * j), columns(r, FEED + 2 * j + 1)
    for i in range(r.halves):
        some, rows = pieces(r, i)
        slope = r.big2[j, rows, :].astype(F32)
        d_inner = (mm_nt(tokens(r.d_third.at[some]), down) * slope).astype(BF16)
        r.big2[j, rows, :] = d_inner
        r.residual[some] += mm_nt(d_inner, up).reshape(PIECE, r.share, -1)


def feed_grad(r, j):
    store_columns(r.g_ffn, 2 * j, mm_tn(tokens(r.second_low), r.big2[j]).astype(BF16))
    store_columns(r.g_ffn, 2 * j + 1, mm_tn(r.big1[j], tokens(r.d_third)).astype(BF16))


def second_back(r, m):
    d_cross, gain, bias = norm_backward(
        r.residual[m], r.normed2[m].astype(F32), r.factor[m, :, 1:2], r.norms[1:2, :]
    )
    r.sums[1:2, :] += gain
    r.sums[4:5, :] += bias
    r.residual[m] = d_cross
    r.d_second[m] = d_cross.astype(BF16)


def clear_pads(r):
    for s in range(r.slots):
        r.big2[s] = jnp.zeros(r.big2.shape[1:], BF16)


def backward_cross(r, m):
    marks = head_marks()
    wide = window_rows()
    reach = r.frame - wide
    d_mixed = mm(r.d_second[m], columns(r, CROSS + 3)).astype(BF16)
    queries = r.q_cross[m]
    windows = [slot_window(r, m, s) for s in range(r.slots)]

    def view(ref, s, g):
        return ref[m, pl.ds(windows[s][0], wide), g * QUAD : (g + 1) * QUAD]

    d_queries = []
    for g in range(r.quads):
        d_q, d_k, d_v = attend_back(
            [
                (
                    r.p_cross[m, s, g],
                    view(r.k_cross, s, g),
                    view(r.v_cross, s, g),
                    cut(queries, s, g),
                    cut(d_mixed, s, g),
                )
                for s in range(r.slots)
            ],
            marks,
        )
        for s in range(r.slots):
            r.big2[s, reach : reach + wide, :QUAD] = d_k[s]
            r.big2[s, reach : reach + wide, QUAD:] = d_v[s]
        total = None
        for s in range(r.slots):
            piece = r.big2[s, pl.ds(slot_shift(r, m, s), r.frame), :]
            total = piece if total is None else total + piece
        r.k_cross[m, :, g * QUAD : (g + 1) * QUAD] = total[:, :QUAD]
        r.v_cross[m, :, g * QUAD : (g + 1) * QUAD] = total[:, QUAD:]
        d_queries.append(jnp.concatenate(d_q, axis=0))
    d_queries = jnp.concatenate(d_queries, axis=1)
    r.q_cross[m] = d_queries
    d_first = r.residual[m] + mm_nt(d_queries, columns(r, CROSS + 0))
    d_attn, gain, bias = norm_backward(d_first, r.normed1[m].astype(F32), r.factor[m, :, 0:1], r.norms[0:1, :])
    r.sums[0:1, :] += gain
    r.sums[3:4, :] += bias
    r.residual[m] = d_attn
    r.d_first[m] = d_attn.astype(BF16)
    source_term = mm_nt(r.k_cross[m], columns(r, CROSS + 1)) + mm_nt(
        r.v_cross[m], columns(r, CROSS + 2)
    )
    low, edge, half = source_term.astype(BF16), r.enc_len - r.frame, r.enc_len // 2
    shift = r.table[m, 1] * 16
    r.big2[0, reach:edge, :] = jnp.zeros((edge - reach, low.shape[1]), BF16)
    r.big2[0, edge:, :] = low
    r.big2[1, : r.frame, :] = low
    r.big1[m, :half, :] = r.big2[0, pl.ds(shift, half), :]
    r.big1[m, half:, :] = r.big2[1, pl.ds(shift + (half - edge), half), :]
    r.big2[0, edge:, :] = jnp.zeros_like(low)
    r.big2[1, : r.frame, :] = jnp.zeros_like(low)


def backward_self(r, m):
    marks = head_marks()
    d_mixed = mm(r.d_first[m], columns(r, SELF + 3)).astype(BF16)
    queries, keys, values = r.q_self[m], r.k_self[m], r.v_self[m]
    units = [(s, g) for s in range(r.slots) for g in range(r.quads)]
    parts = attend_back(
        [
            (
                r.p_self[m, s, g],
                cut(keys, s, g),
                cut(values, s, g),
                cut(queries, s, g),
                cut(d_mixed, s, g),
            )
            for s, g in units
        ],
        marks,
    )
    d_q, d_k, d_v = [
        jnp.concatenate([jnp.concatenate(part[g :: r.quads], axis=0) for g in range(r.quads)], axis=1)
        for part in parts
    ]
    r.q_self[m], r.k_self[m], r.v_self[m] = d_q, d_k, d_v
    r.cotangent[m] = (r.residual[m] + mm_nt(d_q, columns(r, SELF + 0))).astype(BF16)
    r.second_low[m] = (
        mm_nt(d_k, columns(r, SELF + 1)) + mm_nt(d_v, columns(r, SELF + 2))
    ).astype(BF16)


def weight_grad(r, kind):
    left, right = {
        SELF: (r.stream, r.q_self),
        SELF + 1: (r.context, r.k_self),
        SELF + 2: (r.context, r.v_self),
        SELF + 3: (r.d_first, r.mixed_self),
        CROSS: (r.first_low, r.q_cross),
        CROSS + 1: (r.source, r.k_cross),
        CROSS + 2: (r.source, r.v_cross),
        CROSS + 3: (r.d_second, r.mixed_cross),
    }[kind]
    store_columns(*grad_place(r, kind), mm_tn(tokens(left), tokens(right)).astype(BF16))


AXES = ("y", "core", "p", "n", "x")
SIZES = {"y": NY, "core": NC, "z": NZ, "p": NZ // 2, "n": 2, "x": NX, "w": NX * NY}
JOINED = {"w": ("x", "y"), "z": ("p", "n")}


def plain(axes):
    return [part for axis in axes for part in JOINED.get(axis, (axis,))]


class Place:
    def __init__(self, groups):
        d, t = lax.axis_index(DP), lax.axis_index(TENSOR)
        high, self.low = lax.div(d, groups), lax.rem(d, groups)
        self.groups = groups
        self.a, self.b = lax.div(high, NX), lax.rem(high, NX)
        self.a1, self.a0 = lax.div(self.a, 2), lax.rem(self.a, 2)
        self.y, self.c = lax.div(t, NC), lax.rem(t, NC)
        self.t = t

    def device(self, a=None, b=None, y=None, c=None):
        a, b = self.a if a is None else a, self.b if b is None else b
        y, c = self.y if y is None else y, self.c if c is None else c
        return ((a * NX + b) * self.groups + self.low, y * NC + c)

    def up(self, k):
        return lax.rem(self.a + k, NZ)

    def peer(self, axis, k=0):
        if axis == "z":
            return self.device(a=self.up(k))
        if axis == "x":
            return self.device(b=1 - self.b)
        if axis == "y":
            return self.device(y=1 - self.y)
        if axis == "core":
            return self.device(c=1 - self.c)
        return self.device(y=1 - self.y, c=1 - self.c)

    def region(self, fixed):
        return tuple(fixed[a] if a in fixed else slice(None) for a in AXES)

    def own(self, axes):
        place = {"y": self.y, "core": self.c, "p": self.a1, "n": self.a0, "x": self.b}
        return {a: place[a] for a in plain(axes)}

    def others(self, axis):
        if axis == "z":
            ups = [self.up(k) for k in range(1, NZ)]
            return [{"p": lax.div(up, 2), "n": lax.rem(up, 2)} for up in ups]
        far = {axis: 1 - place for axis, place in self.own(AXES).items()}
        if axis == "w":
            x, y = far["x"], far["y"]
            return [{"x": x, "y": self.y}, {"x": self.b, "y": y}, {"x": x, "y": y}]
        return [{axis: far[axis]}]

    def peers(self, axis):
        if axis == "z":
            return [self.peer("z", k) for k in range(1, NZ)]
        if axis == "w":
            return [self.peer("x"), self.peer("y"), self.device(b=1 - self.b, y=1 - self.y)]
        if axis == "p":
            return [self.device(a=(1 - self.a1) * 2 + self.a0)]
        if axis == "n":
            return [self.device(a=self.a1 * 2 + 1 - self.a0)]
        return [self.peer(axis)]


class Link:
    def __init__(self, r):
        self.r = r
        self.used = 0
        self.all = []

    def slot(self):
        self.used += 1
        return self.used - 1

    def send(self, key, source, target, device):
        return pltpu.make_async_remote_copy(
            src_ref=source,
            dst_ref=target,
            send_sem=self.r.send_sems.at[key],
            recv_sem=self.r.recv_sems.at[key],
            device_id=device,
            device_id_type=MESH,
        )


class Stages:
    def __init__(self, link, counts):
        self.link = link
        self.keys = [[link.slot() for _ in range(n)] for n in counts]
        link.all.append(self)

    def start(self, stage):
        for copy in self.copies(stage):
            copy.start()

    def wait(self, stage):
        for copy in self.copies(stage):
            copy.wait_recv()

    def last(self):
        self.wait(len(self.keys) - 1)

    def turn(self, stage):
        self.wait(stage)
        self.start(stage + 1)

    def drain(self):
        for stage in range(len(self.keys)):
            for copy in self.copies(stage):
                copy.wait_send()


class Gather(Stages):
    def __init__(self, link, place, first, count, order):
        self.axes = (*order, "core")
        super().__init__(link, [SIZES[a] - 1 for a in self.axes])
        self.p, self.kinds = place, pl.ds(first, count)

    def copies(self, stage):
        p, link = self.p, self.link
        region = p.region(p.own(self.axes[stage:]))
        ref = link.r.w.at[(self.kinds, *region)]
        peers = p.peers(self.axes[stage])
        return [link.send(key, ref, ref, peer) for key, peer in zip(self.keys[stage], peers)]


class GatherNorms(Stages):
    def __init__(self, link, place):
        super().__init__(link, (NZ - 1, 1))
        self.p = place

    def copies(self, stage):
        p, pack, send = self.p, self.link.r.pack, self.link.send
        keys = self.keys[stage]
        if stage == 0:
            ref = pack.at[p.a, p.b]
            return [send(keys[k - 1], ref, ref, p.peer("z", k)) for k in range(1, NZ)]
        ref = pack.at[:, p.b]
        return [send(keys[0], ref, ref, p.peer("x"))]


class Scatter(Stages):
    def __init__(self, link, place, first, count, order, boxes):
        self.axes = ("core", *order)
        super().__init__(link, [SIZES[a] - 1 for a in self.axes])
        self.p, self.count, self.boxes = place, count, boxes
        self.ref, self.first = grad_place(link.r, first)

    def copies(self, stage):
        p, link = self.p, self.link
        axis, kept = self.axes[stage], p.own(self.axes[:stage])
        peers, others = p.peers(axis), p.others(axis)
        out = []
        for i, key in enumerate(self.keys[stage]):
            region = p.region({**kept, **others[i]})
            source = self.ref.at[(pl.ds(self.first, self.count), *region)]
            out.append(link.send(key, source, self.boxes[stage].at[i], peers[i]))
        return out

    def summed(self, stage, k):
        at = (self.first + k, *self.p.region(self.p.own(self.axes[: stage + 1])))
        box = self.boxes[stage]
        if box.shape[0] == 1:
            return at, self.ref[at].astype(F32) + box[0, k].astype(F32)
        total = self.ref[at].astype(F32)
        for i in range(box.shape[0]):
            total = total + box[i, k].astype(F32)
        return at, total

    def turn(self, stage):
        if stage == len(self.keys) - 1:
            self.share.go()
            return
        self.wait(stage)
        for k in range(self.count):
            at, total = self.summed(stage, k)
            self.ref[at] = total.astype(BF16)
        self.start(stage + 1)

    def total(self, k):
        return self.summed(len(self.keys) - 1, k)[1]


def box_name(name, stage):
    return "box_%d_%d" % (name, stage)


def scatter_boxes(name, count, order):
    out, axes = [], ("core", *order)
    for i, axis in enumerate(axes):
        free = [SIZES[a] for a in AXES if a not in plain(axes[: i + 1])]
        shape = (SIZES[axis] - 1, count, *free, 64, 128)
        out.append((box_name(name, i), pltpu.VMEM(shape, BF16)))
    return out


Q, K, V, O, C0, C1, F0, F1, F2, F3 = range(10)
SUM, ROWS = 10, 20
(
    START, SELF_FORWARD, NORM_FORWARD, CROSS_FORWARD, FEED_FORWARD, FEED_BACK,
    FEED_GRAD, NORM_BACK, CROSS_BACK, GRAD, SELF_BACK, TAIL,
) = range(12)
GATHERS = {
    Q: (SELF, 1, "pnw"),
    K: (SELF + 1, 1, "pxny"),
    V: (SELF + 2, 1, "yzx"),
    O: (SELF + 3, 1, "pxny"),
    C0: (CROSS, 2, "pnyx"),
    C1: (CROSS + 2, 2, "yxz"),
    F0: (FEED, 2, "zw"),
    F1: (FEED + 2, 2, "pnw"),
    F2: (FEED + 4, 2, "xypn"),
    F3: (FEED + 6, 2, "pynx"),
}
SCATTERS = {
    F0: (FEED, 2, "wz"),
    F1: (FEED + 2, 2, "zxy"),
    F2: (FEED + 4, 2, "xzy"),
    F3: (FEED + 6, 2, "yxz"),
    C0: (CROSS, 2, "yxz"),
    C1: (CROSS + 2, 2, "xzy"),
    O: (SELF + 3, 1, "xzy"),
    Q: (SELF, 1, "xnyp"),
    K: (SELF + 1, 1, "npw"),
    V: (SELF + 2, 1, "zw"),
}
LATE = 2
PLAN = {
    (START, 0): ((C0, -1), (F2, -1), (C1, -1), (Q, -1), (K, -1), (V, -1), (V, 0), (O, -1), (C1, 0), (F3, -1),),
    (START, 1): ((K, 0), (Q, 0), (F2, 0), (C0, 0), (K, 1), (O, 0), (F1, -1), (Q, 1), (F0, -1), (O, 1),),
    (START, 2): ((C0, 1), (C1, 1), (Q, 2), (V, 1), (K, 2), (C0, 2), (O, 2), (K, 3), (F3, 0), (V, 2),),
    (SELF_FORWARD, 1): ((O, 3), (F1, 0), (F0, 0),),
    (SELF_FORWARD, 2): ((F2, 1),),
    (SELF_FORWARD, 3): ((F3, 1), (C0, 3),),
    (NORM_FORWARD, 0): ((C1, 2),),
    (CROSS_FORWARD, 0): ((F1, 1),),
    (CROSS_FORWARD, 2): ((F2, 2), (F0, 1),),
    (CROSS_FORWARD, 3): ((F3, 2),),
    (FEED_FORWARD, 0): ((F1, 2),),
    (FEED_FORWARD, 2): ((F2, 3),),
    (FEED_FORWARD, 4): ((F3, 3),),
    (FEED_GRAD, 2): ((SUM + F0, 0),),
    (FEED_BACK, 3): ((SUM + F1, 0),),
    (CROSS_BACK, 0): ((SUM + F3, 0), (SUM + F2, 0),),
    (CROSS_BACK, 2): ((ROWS + 0, 0),),
    (GRAD, SELF + 3): ((ROWS + 1, 0), (ROWS + 2, 0), (SUM + F0, 1), (SUM + F3, 1), (SUM + F2, 1), (SUM + F1, 1),),
    (SELF_BACK, 0): ((ROWS + 3, 0),),
    (SELF_BACK, 3): ((SUM + O, 0), (SUM + F3, 2),),
    (GRAD, CROSS + 1): ((SUM + V, 0),),
    (GRAD, CROSS + 2): ((SUM + K, 0), (SUM + Q, 0),),
    (TAIL, 0): ((SUM + C0, 0), (SUM + C1, 0), (SUM + O, 1), (SUM + K, 1), (SUM + V, 1), (SUM + F0, 2), (SUM + F1, 2), (SUM + Q, 1), (SUM + C1, 1), (SUM + F2, 2),),
    (TAIL, 1): ((SUM + C0, 1), (SUM + F3, 3), (SUM + Q, 2), (SUM + F1, 3), (SUM + K, 2), (SUM + F2, 3), (SUM + C0, 2), (SUM + O, 2), (SUM + Q, 3), (SUM + C1, 2),),
}


class ScatterNorms(Stages):
    def __init__(self, link, place):
        super().__init__(link, (1, 1, 1, NZ - 1))
        self.p = place

    def copies(self, stage):
        p, r, send, keys = self.p, self.link.r, self.link.send, self.keys[stage]
        if stage == 0:
            return [send(keys[0], r.g_norm, r.n_box0, p.peer("core"))]
        if stage == 1:
            return [send(keys[0], r.n_box0, r.n_box1, p.peer("y"))]
        if stage == 2:
            return [send(keys[0], r.n_box1.at[:, 1 - p.b], r.n_box2, p.peer("x"))]
        return [
            send(keys[k - 1], r.n_box2.at[p.up(k)], r.n_box3.at[k - 1], p.peer("z", k))
            for k in range(1, NZ)
        ]

    def step(self, stage):
        p, r = self.p, self.link.r
        self.wait(stage)
        if stage == 0:
            r.n_box0[...] = r.g_norm[...] + r.n_box0[...]
        elif stage == 1:
            r.n_box1[...] = r.n_box0[...] + r.n_box1[...]
        else:
            r.n_box2[...] = r.n_box1[:, p.b] + r.n_box2[...]
        self.start(stage + 1)

    def total(self):
        r = self.link.r
        return r.n_box2[self.p.a] + ((r.n_box3[0] + r.n_box3[1]) + r.n_box3[2])


class ScatterEncoder(Stages):
    def __init__(self, link, place, share, micro):
        super().__init__(link, (NY * micro, micro))
        self.p, self.share, self.micro = place, share, micro
        self.boxes = (link.r.d_third, link.r.second_low)

    def rows(self, m, y, c):
        at = pl.multiple_of((y * NC + c) * self.share, self.share)
        return self.link.r.big1.at[m, pl.ds(at, self.share), :]

    def one(self, stage, m):
        p, r, send = self.p, self.link.r, self.link.send
        key = self.keys[stage][0]
        if stage == 0:
            return [
                send(
                    key + NY * m + y,
                    self.rows(m, y, 1 - p.c),
                    self.boxes[y].at[m],
                    p.peer("core"),
                )
                for y in range(NY)
            ]
        return [send(key + m, self.rows(m, 1 - p.y, p.c), r.e_box1.at[m], p.peer("y"))]

    def copies(self, stage):
        return [copy for m in range(self.micro) for copy in self.one(stage, m)]

    def begin(self, m):
        for copy in self.one(0, m):
            copy.start()

    def step(self, m):
        for copy in self.one(0, m):
            copy.wait_recv()
        for y in range(NY):
            ref = self.rows(m, y, self.p.c)
            ref[...] = ref[...] + self.boxes[y][m]
        for copy in self.one(1, m):
            copy.start()

    def finish(self):
        self.wait(1)
        for m in range(self.micro):
            ref = self.rows(m, self.p.y, self.p.c)
            ref[...] = ref[...] + self.link.r.e_box1[m]


class EncoderPart:
    def __init__(self, rows, m):
        self.rows, self.m = rows, m

    def turn(self, stage):
        self.rows.step(self.m)


class ShareFfn(Stages):
    def __init__(self, link, place, box, first, item):
        super().__init__(link, (3,))
        self.p, self.box, self.first, self.item = place, box, first, item

    def copies(self, stage):
        p, send, keys = self.p, self.link.send, self.keys[0]
        ref = self.box.at[p.t, pl.ds(self.first, self.item.count)]
        axes = ("core", "y", "both")
        return [send(keys[i], ref, ref, p.peer(axes[i])) for i in range(3)]

    def go(self):
        self.item.last()
        for k in range(self.item.count):
            self.box[self.p.t, self.first + k] = self.item.total(k).astype(BF16)
        self.start(0)


def each(count, body, ticks=None):
    def step(i, carry):
        for k, tick in (ticks or {}).items():
            pl.when(i == k)(tick)
        body(i)
        return carry

    lax.fori_loop(0, count, step, 0)


SEMS = 180


def layer_kernel(names, groups, scale, *refs):
    r = Refs()
    for name, ref in zip(names, refs):
        setattr(r, name, ref)
    micro, r.share = r.stream.shape[0], r.stream.shape[1]
    r.slots = r.share // SLOT
    r.quads = r.stream.shape[2] // QUAD
    r.enc_len = r.encoder.shape[1]
    r.frame = frame_rows(r.share)
    r.halves = micro // PIECE
    p = Place(groups)
    link = Link(r)

    mine = pl.ds(pl.multiple_of(p.t * r.share, r.share), r.share)
    half = pl.ds(pl.multiple_of(p.t * (r.share // 2), r.share // 2), r.share // 2)
    pairs = [
        (r.self_query, r.w.at[SELF, p.y, p.c, p.a1, p.a0, p.b]),
        (r.self_key_value, r.w.at[pl.ds(SELF + 1, 2), p.y, p.c, p.a1, p.a0, p.b]),
        (r.cross_query, r.w.at[CROSS, p.y, p.c, p.a1, p.a0, p.b]),
        (r.cross_key_value, r.w.at[pl.ds(CROSS + 1, 2), p.y, p.c, p.a1, p.a0, p.b]),
        (r.self_output, r.w.at[SELF + 3, p.y, p.c, p.a1, p.a0, p.b]),
        (r.cross_output, r.w.at[CROSS + 3, p.y, p.c, p.a1, p.a0, p.b]),
    ]
    down = pl.ds(pl.multiple_of(p.t * 128, 128), 128)
    for j in range(4):
        pairs.append(
            (
                r.ffn_out.at[pl.ds(j * 64, 64), down],
                r.w.at[FEED + 2 * j + 1, p.y, p.c, p.a1, p.a0, p.b],
            )
        )
    up = pl.ds(pl.multiple_of(p.t * 512, 512), 512)
    pairs.append((r.ffn_in.at[:, up], r.own_up))
    weights = len(pairs)
    pairs += [
        (r.stream_hbm.at[:, mine, :], r.stream),
        (r.context_hbm.at[:, mine, :], r.context),
        (r.masks_hbm.at[:, half, :], r.masks),
        (r.encoder, r.big1),
        (r.out_grad, r.cotangent),
    ]
    copies = [
        pltpu.make_async_copy(source, target, r.sems.at[i])
        for i, (source, target) in enumerate(pairs)
    ]
    for copy in copies:
        copy.start()
    partners = [p.peer("z", k) for k in range(1, NZ)]
    partners += [p.peer(axis) for axis in ("x", "y", "core", "both")]
    partners.append(p.device(b=1 - p.b, y=1 - p.y))
    barrier = pltpu.get_barrier_semaphore()
    for device in partners:
        pl.semaphore_signal(barrier, inc=1, device_id=device, device_id_type=MESH)
    r.pack[p.a, p.b, 0:3, :64] = r.norm_gain[...].astype(F32)
    r.pack[p.a, p.b, 3:6, :64] = r.norm_bias[...].astype(F32)
    for copy in copies[:weights]:
        copy.wait()
    for j in range(4):
        at = j * 64
        r.w[FEED + 2 * j, p.y, p.c, p.a1, p.a0, p.b] = jnp.concatenate(
            [r.own_up[:, at : at + 64], r.own_up[:, 256 + at : 320 + at]], axis=1
        )
    pl.semaphore_wait(barrier, len(partners))

    chains = {name: Gather(link, p, *spec) for name, spec in GATHERS.items()}
    norms = GatherNorms(link, p)

    def run(phase, step):
        for name, stage in PLAN.get((phase, step), ()):
            if stage < 0:
                chains[name].start(0)
            else:
                chains[name].turn(stage)

    def loop(phase, count, body, needs=None):
        ticks = {}
        for i in range(count):
            names = (needs or {}).get(i, ())
            if PLAN.get((phase, i)) or names:

                def tick(i=i, names=names):
                    run(phase, i)
                    for name in names:
                        chains[name].last()

                ticks[i] = tick
        each(count, functools.partial(body, r), ticks)

    r.sums[...] = jnp.zeros(r.sums.shape, F32)
    run(START, 0)
    norms.start(0)
    run(START, 1)
    for copy in copies[weights:]:
        copy.wait()
    run(START, 2)
    norms.wait(0)
    norms.start(1)
    for name in (Q, K, V):
        chains[name].last()
    loop(SELF_FORWARD, micro, forward_self)
    norms.wait(1)
    r.norms[...] = jnp.concatenate(
        [r.pack[d // NX, d % NX, :, :64] for d in range(NZ * NX)], axis=1
    )
    loop(NORM_FORWARD, micro, first_norm, {0: (O,)})
    loop(CROSS_FORWARD, micro, forward_cross, {0: (C0, C1)})
    loop(FEED_FORWARD, 4 * r.halves, feed, {j * r.halves: (F0 + j,) for j in range(4)})
    for item in link.all:
        item.drain()
    link.all = []
    each(micro, functools.partial(third_norm, r))
    out = [pltpu.make_async_copy(r.d_first, r.block_out, r.sems.at[0])]
    out[0].start()

    sums = {}
    for name, spec in SCATTERS.items():
        boxes = [getattr(r, box_name(name, i)) for i in range(1 + len(spec[2]))]
        sums[name] = Scatter(link, p, *spec, boxes)
        if name >= F0:
            sums[name].share = ShareFfn(link, p, r.all_ffn, 2 * (name - F0), sums[name])
    norm_sums = ScatterNorms(link, p)
    rows = ScatterEncoder(link, p, r.share, micro)
    chains = {SUM + name: item for name, item in sums.items()}
    for m in range(micro):
        chains[ROWS + m] = EncoderPart(rows, m)

    def feed_both(j):
        for i in range(4):
            pl.when(j == i)(functools.partial(run, FEED_BACK, i))
        feed_back(r, j)
        for i in range(4):
            pl.when(j == i)(functools.partial(run, FEED_GRAD, i))
        feed_grad(r, j)
        for i in range(4):
            pl.when(j == i)(functools.partial(sums[F0 + i].start, 0))

    each(4, feed_both)
    run(NORM_BACK, 0)
    each(micro, functools.partial(second_back, r))
    clear_pads(r)
    out[0].wait()

    def cross_back(r, m):
        backward_cross(r, m)
        rows.begin(m)

    loop(CROSS_BACK, micro, cross_back)
    for d in range(NZ * NX):
        r.g_norm[d // NX, d % NX] = jnp.zeros(r.g_norm.shape[2:], F32)
        r.g_norm[d // NX, d % NX, :, :64] = r.sums[:, d * 64 : (d + 1) * 64]
    norm_sums.start(0)

    def grad(kind):
        run(GRAD, kind)
        weight_grad(r, kind)

    def cross_grads(pair):
        for k in (2 * pair, 2 * pair + 1):
            grad(CROSS + k)
        sums[C0 + pair].start(0)

    for pair in range(2 - LATE):
        cross_grads(pair)
    grad(SELF + 3)
    sums[O].start(0)
    norm_sums.step(0)
    loop(SELF_BACK, micro, backward_self)
    out = [
        pltpu.make_async_copy(r.cotangent, r.stream_grad, r.sems.at[0]),
        pltpu.make_async_copy(r.second_low, r.context_grad, r.sems.at[1]),
    ]
    for copy in out:
        copy.start()
    for name, kind in ((V, SELF + 2), (Q, SELF), (K, SELF + 1)):
        grad(kind)
        sums[name].start(0)
    for pair in range(2 - LATE, 2):
        cross_grads(pair)
    norm_sums.step(1)
    run(TAIL, 0)
    norm_sums.step(2)
    rows.finish()
    mine = pl.ds(pl.multiple_of(p.t * r.share, r.share), r.share)
    out.append(pltpu.make_async_copy(r.big1.at[:, mine, :], r.encoder_grad, r.sems.at[2]))
    out[2].start()
    run(TAIL, 1)
    for j in range(4):
        sums[F0 + j].share.wait(0)
    for t in range(NY * NC):
        halves = [
            r.all_ffn[t, 2 * j, :, h * 64 : (h + 1) * 64] for h in range(2) for j in range(4)
        ]
        r.grad_ffn_in[:, t * 512 : (t + 1) * 512] = (
            jnp.concatenate(halves, axis=1).astype(F32) * scale
        )
        for j in range(4):
            r.grad_ffn_out[j * 64 : (j + 1) * 64, t * 128 : (t + 1) * 128] = (
                r.all_ffn[t, 2 * j + 1].astype(F32) * scale
            )
    norm_sums.wait(3)
    total = norm_sums.total() * scale
    r.grad_norm_gain[...] = total[0:3, :64]
    r.grad_norm_bias[...] = total[3:6, :64]
    for name in (C0, C1, O, Q, K, V):
        sums[name].last()
    r.grad_cross_query[...] = sums[C0].total(0) * scale
    r.grad_cross_key_value[0] = sums[C0].total(1) * scale
    r.grad_cross_key_value[1] = sums[C1].total(0) * scale
    r.grad_cross_output[...] = sums[C1].total(1) * scale
    r.grad_self_output[...] = sums[O].total(0) * scale
    r.grad_self_query[...] = sums[Q].total(0) * scale
    r.grad_self_key_value[0] = sums[K].total(0) * scale
    r.grad_self_key_value[1] = sums[V].total(0) * scale
    for item in link.all:
        item.drain()
    for copy in out:
        copy.wait()


def vmem():
    return pl.BlockSpec(memory_space=pltpu.VMEM)


def hbm():
    return pl.BlockSpec(memory_space=pl.ANY)


WEIGHTS = (
    "self_query", "self_key_value", "self_output",
    "cross_query", "cross_key_value", "cross_output",
    "ffn_in", "ffn_out", "norm_gain", "norm_bias",
)


def layer(groups, scale, stream, context, encoder, masks, table, out_grad, weights):
    micro, row, width = stream.shape
    share = out_grad.shape[1]
    enc_len = encoder.shape[1]
    frame, wide = frame_rows(share), window_rows()
    slots, quads = share // SLOT, width // QUAD
    small = ("norm_gain", "norm_bias")
    ins = [
        ("stream_hbm", stream, hbm()),
        ("context_hbm", context, hbm()),
        ("encoder", encoder, hbm()),
        ("masks_hbm", masks, hbm()),
        ("table", table, pl.BlockSpec(memory_space=pltpu.SMEM)),
        ("out_grad", out_grad, hbm()),
    ]
    for name, value in zip(WEIGHTS, weights):
        ins.append((name, value, vmem() if name in small else hbm()))
    part = jax.ShapeDtypeStruct((micro, share, width), BF16)
    outs = [
        ("block_out", part, hbm()),
        ("stream_grad", part, hbm()),
        ("context_grad", part, hbm()),
        ("encoder_grad", part, hbm()),
    ]
    for name, value in zip(WEIGHTS, weights):
        outs.append(("grad_" + name, jax.ShapeDtypeStruct(value.shape, F32), vmem()))
    low = pltpu.VMEM((micro, share, width), BF16)
    high = pltpu.VMEM((micro, share, width), F32)
    window = pltpu.VMEM((micro, frame, width), BF16)
    big = pltpu.VMEM((micro, enc_len, width), BF16)
    norm = pltpu.VMEM((NZ, NX, 8, 128), F32)
    scratch = [
        ("w", pltpu.VMEM((KINDS, NY, NC, NZ // 2, 2, NX, 64, 128), BF16)),
        ("g_ffn", pltpu.VMEM((8, NY, NC, NZ // 2, 2, NX, 64, 128), BF16)),
        ("stream", low),
        ("context", low),
        ("cotangent", low),
        ("masks", pltpu.VMEM((micro, share // 2, 128), jnp.int32)),
        ("q_self", low),
        ("k_self", low),
        ("v_self", low),
        ("mixed_self", low),
        ("first_low", low),
        ("q_cross", low),
        ("k_cross", window),
        ("v_cross", window),
        ("source", window),
        ("mixed_cross", low),
        ("second_low", low),
        ("d_third", low),
        ("d_second", low),
        ("d_first", low),
        ("p_self", pltpu.VMEM((micro, slots, quads, SLOT, QUAD), BF16)),
        ("p_cross", pltpu.VMEM((micro, slots, quads, wide, QUAD), BF16)),
        ("residual", high),
        ("normed1", low),
        ("normed2", low),
        ("factor", pltpu.VMEM((micro, share, 2), F32)),
        ("big1", big),
        ("big2", big),
        ("own_up", pltpu.VMEM((64, 512), BF16)),
        ("norms", pltpu.VMEM((8, width), F32)),
        ("sums", pltpu.VMEM((8, width), F32)),
        ("pack", norm),
        ("g_norm", norm),
        ("n_box0", norm),
        ("n_box1", norm),
        ("n_box2", pltpu.VMEM((NZ, 8, 128), F32)),
        ("n_box3", pltpu.VMEM((NZ - 1, 8, 128), F32)),
        ("e_box1", low),
        ("all_ffn", pltpu.VMEM((NY * NC, 8, 64, 128), BF16)),
        ("sems", pltpu.SemaphoreType.DMA((19,))),
        ("send_sems", pltpu.SemaphoreType.DMA((SEMS,))),
        ("recv_sems", pltpu.SemaphoreType.DMA((SEMS,))),
    ]
    for name, (_, count, order) in SCATTERS.items():
        scratch += scatter_boxes(name, count, order)
    names = [item[0] for item in ins + outs + scratch]
    return pl.pallas_call(
        functools.partial(layer_kernel, names, groups, scale),
        out_shape=[item[1] for item in outs],
        in_specs=[item[2] for item in ins],
        out_specs=[item[2] for item in outs],
        scratch_shapes=[item[1] for item in scratch],
        compiler_params=pltpu.CompilerParams(
            vmem_limit_bytes=VMEM_LIMIT, collective_id=0, has_side_effects=True
        ),
        cost_estimate=pl.CostEstimate(
            flops=30_000_000_000, bytes_accessed=30_000_000, transcendentals=4_000_000
        ),
    )(*[item[1] for item in ins])


def copy_kernel(count, *refs):
    given, results, held = (refs[i * count : (i + 1) * count] for i in range(3))
    sems = refs[3 * count]
    loads = [pltpu.make_async_copy(a, b, sems.at[0, i]) for i, (a, b) in enumerate(zip(given, held))]
    stores = [
        pltpu.make_async_copy(a, b, sems.at[1, i]) for i, (a, b) in enumerate(zip(held, results))
    ]
    for load in loads:
        load.start()
    for load, store in zip(loads, stores):
        load.wait()
        store.start()
    for store in stores:
        store.wait()


def copy_all(values):
    count = len(values)
    return pl.pallas_call(
        functools.partial(copy_kernel, count),
        out_shape=[jax.ShapeDtypeStruct(v.shape, v.dtype) for v in values],
        in_specs=[hbm()] * count,
        out_specs=[hbm()] * count,
        scratch_shapes=[pltpu.VMEM(v.shape, v.dtype) for v in values]
        + [pltpu.SemaphoreType.DMA((2, count))],
        compiler_params=pltpu.CompilerParams(vmem_limit_bytes=VMEM_LIMIT),
    )(*values)


GATHER_DIM = (0, 1, 0, 0, 1, 0, 0, 0, 1, 1)


def per_device(
    query_stream,
    context_stream,
    encoder_out,
    query_masks,
    source_segments,
    out_grad,
    *weights,
):
    micro, row, width = query_stream.shape
    share = out_grad.shape[1]
    slots = share // SLOT
    t = lax.axis_index(TENSOR)
    replicas = lax.axis_size(DP)
    scale = float(micro * row * replicas) ** (-0.5)
    groups = replicas // (NZ * NX)
    weights = [item.T if i in (2, 5) else item for i, item in enumerate(weights)]
    near = [[i * groups + j for j in range(groups)] for i in range(NZ * NX)]
    if groups > 1:
        weights = [
            lax.all_gather(item, DP, axis=dim, tiled=True, axis_index_groups=near)
            for item, dim in zip(weights, GATHER_DIM)
        ]
    bounds = t * slots + jnp.arange(slots + 1, dtype=jnp.int32)
    starts = jnp.sum(
        (source_segments < bounds[None, :, None]).astype(jnp.int32), axis=-1
    )
    table = window_table(starts, share, encoder_out.shape[1])
    results = layer(
        groups, scale, query_stream, context_stream, encoder_out, query_masks, table,
        out_grad, weights,
    )
    results = copy_all(results)
    grads = results[4:]
    if groups > 1:
        grads = [
            lax.psum_scatter(
                item, DP, scatter_dimension=dim, tiled=True, axis_index_groups=near
            )
            for item, dim in zip(grads, GATHER_DIM)
        ]
    grads = [item.T if i in (2, 5) else item for i, item in enumerate(grads)]
    return (*results[:4], *grads)


def solution(mesh):
    in_specs = (
        P(None, DP, None),
        P(None, DP, None),
        P(None, DP, None),
        P(None, DP, None),
        P(None, DP, None),
        P(None, (DP, TENSOR), None),
        P(DP, TENSOR),
        P(None, DP, TENSOR),
        P(TENSOR, DP),
        P(DP, TENSOR),
        P(None, DP, TENSOR),
        P(TENSOR, DP),
        P(DP, None),
        P(DP, None),
        P(None, DP),
        P(None, DP),
    )
    out_specs = (
        P(None, (DP, TENSOR), None),
        P(None, (DP, TENSOR), None),
        P(None, (DP, TENSOR), None),
        P(None, (DP, TENSOR), None),
        P(DP, TENSOR),
        P(None, DP, TENSOR),
        P(TENSOR, DP),
        P(DP, TENSOR),
        P(None, DP, TENSOR),
        P(TENSOR, DP),
        P(DP, None),
        P(DP, None),
        P(None, DP),
        P(None, DP),
    )
    return jax.shard_map(
        per_device, mesh=mesh, in_specs=in_specs, out_specs=out_specs, check_vma=False
    )
```

```python
import functools

import jax
import jax.numpy as jnp
from jax import lax
from jax.experimental import pallas as pl
from jax.experimental.pallas import tpu as pltpu
from jax.sharding import PartitionSpec as P

HEAD_DIM = 64
SLOT = 64
SEG_MOST = 128
QUAD = 4 * HEAD_DIM
PAIR = 2 * HEAD_DIM
NZ, NX, NY, NC = 4, 2, 2, 2
PIECE = 2
SELF, CROSS, FEED, KINDS = 0, 4, 8, 16
BF16 = jnp.bfloat16
F32 = jnp.float32
MESH = pl.DeviceIdType.MESH
DP, TENSOR = "dp", "tensor"

epsilon = 1e-05
neg_fill = -1e30
gelu_coef = 0.7978845608028654
gelu_cube = 0.044715
VMEM_LIMIT = 65400 * 1024


def mm(left, right):
    return jnp.dot(left, right, preferred_element_type=F32)


def mm_nt(left, right):
    return lax.dot_general(left, right, (((1,), (1,)), ((), ())), preferred_element_type=F32)


def mm_tn(left, right):
    return lax.dot_general(left, right, (((0,), (0,)), ((), ())), preferred_element_type=F32)


def norm_forward(value, gain, bias):
    center = jnp.mean(value, axis=-1, keepdims=True)
    shifted = value - center
    factor = lax.rsqrt(jnp.mean(shifted * shifted, axis=-1, keepdims=True) + epsilon)
    normed = shifted * factor
    return normed * gain + bias, normed, factor


def norm_backward(incoming, normed, factor, gain):
    scaled = incoming * gain
    inside = (
        scaled
        - jnp.mean(scaled, axis=-1, keepdims=True)
        - normed * jnp.mean(scaled * normed, axis=-1, keepdims=True)
    )
    return (
        factor * inside,
        jnp.sum(incoming * normed, axis=0, keepdims=True),
        jnp.sum(incoming, axis=0, keepdims=True),
    )


def columns(r, kind):
    parts = [r.w[kind, t // NC, t % NC].reshape(-1, 128) for t in range(NY * NC)]
    return jnp.concatenate(parts, axis=1)


def grad_place(r, kind):
    if kind >= FEED:
        return r.g_ffn, kind - FEED
    return r.w, kind + FEED


def store_columns(ref, at, value):
    for t in range(NY * NC):
        ref[at, t // NC, t % NC] = value[:, t * 128 : (t + 1) * 128].reshape(NZ // 2, 2, NX, -1, 128)


def head_marks():
    lane = lax.broadcasted_iota(jnp.int32, (1, QUAD), 1) // HEAD_DIM
    return [jnp.where(lane == h, 1.0, 0.0).astype(BF16) for h in range(4)]


def spread_heads(rows, marks):
    return jnp.concatenate([rows * mark for mark in marks], axis=0)


def fold_pairs(weights, rows):
    first = lax.broadcasted_iota(jnp.int32, (SLOT, PAIR), 1) < HEAD_DIM
    parts = []
    for p in range(2):
        cut = slice(p * PAIR, (p + 1) * PAIR)
        full = mm_tn(weights[:, cut], rows[:, cut])
        parts.append(jnp.where(first, full[:SLOT], full[SLOT:]))
    return jnp.concatenate(parts, axis=1)


def soft_keys(scores, allowed):
    scores = jnp.where(allowed, scores, neg_fill)
    top = jnp.max(scores, axis=0, keepdims=True)
    raised = jnp.exp(scores - top)
    return (raised * (1.0 / jnp.sum(raised, axis=0, keepdims=True))).astype(BF16)


def attend_back(items, marks):
    d_spread = [spread_heads(item[4], marks) for item in items]
    d_probs = [mm_nt(item[2], spread) for item, spread in zip(items, d_spread)]
    d_values = [mm(item[0], spread).astype(BF16) for item, spread in zip(items, d_spread)]
    d_scores = []
    for item, d_prob in zip(items, d_probs):
        wide = item[0].astype(F32)
        inner = jnp.sum(wide * d_prob, axis=0, keepdims=True)
        d_scores.append((wide * (d_prob - inner)).astype(BF16))
    d_keys = [
        mm(d_score, spread_heads(item[3], marks)).astype(BF16)
        for item, d_score in zip(items, d_scores)
    ]
    d_queries = [
        (fold_pairs(d_score, item[1]) * HEAD_DIM ** (-0.5)).astype(BF16)
        for item, d_score in zip(items, d_scores)
    ]
    return d_queries, d_keys, d_values


def cut(value, s, g):
    return value[s * SLOT : (s + 1) * SLOT, g * QUAD : (g + 1) * QUAD]


class Refs:
    pass


def frame_rows(share):
    return (share // SLOT) * SEG_MOST + 16


def window_rows():
    return SEG_MOST + 16


def window_table(starts, share, enc_len):
    frame, wide = frame_rows(share), window_rows()
    base = jnp.minimum(starts[:, :1] // 16 * 16, enc_len - frame)
    begin = starts[:, :-1] - base
    at = jnp.minimum(begin // 16 * 16, frame - wide)
    low = begin - at
    high = low + starts[:, 1:] - starts[:, :-1]
    return jnp.concatenate(
        [base // 16, (enc_len - frame - base) // 16, at // 16, low, high, (frame - wide - at) // 16],
        axis=1,
    )


def frame_start(r, m):
    return r.table[m, 0] * 16


def slot_window(r, m, s):
    at = r.table[m, 2 + s] * 16
    return at, r.table[m, 2 + r.slots + s], r.table[m, 2 + 2 * r.slots + s]


def slot_shift(r, m, s):
    return r.table[m, 2 + 3 * r.slots + s] * 16


def forward_self(r, m):
    marks = head_marks()
    stream, context = r.stream[m], r.context[m]
    queries = (mm(stream, columns(r, SELF + 0)) * HEAD_DIM ** (-0.5)).astype(BF16)
    keys = mm(context, columns(r, SELF + 1)).astype(BF16)
    values = mm(context, columns(r, SELF + 2)).astype(BF16)
    r.q_self[m], r.k_self[m], r.v_self[m] = queries, keys, values
    row = lax.broadcasted_iota(jnp.int32, (SLOT, QUAD), 0)
    lane = lax.broadcasted_iota(jnp.int32, (SLOT, QUAD), 1) % SLOT
    place = jnp.where(lane == 2 * (row % 32) + row // 32, 1.0, 0.0).astype(BF16)
    units = [(s, g) for s in range(r.slots) for g in range(r.quads)]
    allowed = []
    for s in range(r.slots):
        bits = r.masks[m, s * 32 : (s + 1) * 32].astype(F32)
        bits = jnp.concatenate([bits[:, :SLOT], bits[:, SLOT:]], axis=0).astype(BF16)
        allowed.append(mm_tn(bits, place) > 0.5)
    scores = [mm_nt(cut(keys, s, g), spread_heads(cut(queries, s, g), marks)) for s, g in units]
    probs = [soft_keys(score, allowed[s]) for score, (s, g) in zip(scores, units)]
    mixed = [fold_pairs(prob, cut(values, s, g)).astype(BF16) for prob, (s, g) in zip(probs, units)]
    for prob, one, (s, g) in zip(probs, mixed, units):
        r.p_self[m, s, g] = prob
        r.mixed_self[m, s * SLOT : (s + 1) * SLOT, g * QUAD : (g + 1) * QUAD] = one


def first_norm(r, m):
    attn = mm_nt(r.mixed_self[m], columns(r, SELF + 3))
    first, normed, factor = norm_forward(
        r.stream[m].astype(F32) + attn, r.norms[0:1, :], r.norms[3:4, :]
    )
    r.residual[m], r.factor[m, :, 0:1] = first, factor
    r.normed1[m] = normed.astype(BF16)
    r.first_low[m] = first.astype(BF16)


def forward_cross(r, m):
    marks = head_marks()
    base = frame_start(r, m)
    source = r.big1[m, pl.ds(base, r.frame), :]
    r.source[m] = source
    r.k_cross[m] = mm(source, columns(r, CROSS + 1)).astype(BF16)
    r.v_cross[m] = mm(source, columns(r, CROSS + 2)).astype(BF16)
    queries = (mm(r.first_low[m], columns(r, CROSS + 0)) * HEAD_DIM ** (-0.5)).astype(BF16)
    r.q_cross[m] = queries
    wide = window_rows()
    row = lax.broadcasted_iota(jnp.int32, (wide, QUAD), 0)
    units = [(s, g) for s in range(r.slots) for g in range(r.quads)]
    windows = [slot_window(r, m, s) for s in range(r.slots)]
    allowed = [(row >= low) & (row < high) for _, low, high in windows]

    def view(ref, s, g):
        return ref[m, pl.ds(windows[s][0], wide), g * QUAD : (g + 1) * QUAD]

    scores = [
        mm_nt(view(r.k_cross, s, g), spread_heads(cut(queries, s, g), marks)) for s, g in units
    ]
    probs = [soft_keys(score, allowed[s]) for score, (s, g) in zip(scores, units)]
    mixed = [
        fold_pairs(prob, view(r.v_cross, s, g)).astype(BF16) for prob, (s, g) in zip(probs, units)
    ]
    for prob, (s, g) in zip(probs, units):
        r.p_cross[m, s, g] = prob
    mixed = jnp.concatenate(
        [
            jnp.concatenate(mixed[s * r.quads : (s + 1) * r.quads], axis=1)
            for s in range(r.slots)
        ],
        axis=0,
    )
    r.mixed_cross[m] = mixed
    attn = mm_nt(mixed, columns(r, CROSS + 3))
    second, normed, factor = norm_forward(
        r.residual[m] + attn, r.norms[1:2, :], r.norms[4:5, :]
    )
    r.residual[m], r.factor[m, :, 1:2] = second, factor
    r.normed2[m] = normed.astype(BF16)
    r.second_low[m] = second.astype(BF16)


def tokens(ref):
    value = ref[...]
    return value.reshape(-1, value.shape[-1])


def pieces(r, i):
    return pl.ds(i * PIECE, PIECE), pl.ds(pl.multiple_of(i * PIECE * r.share, 512), PIECE * r.share)


def feed(r, i):
    j = lax.div(i, r.halves)
    some, rows = pieces(r, lax.rem(i, r.halves))
    low = tokens(r.second_low.at[some])
    up, down = columns(r, FEED + 2 * j), columns(r, FEED + 2 * j + 1)
    for at in range(0, 512, 256):
        inner = mm(low, up[:, at : at + 256])
        square = inner * inner
        half = 0.5 + 0.5 * jnp.tanh(inner * (gelu_coef + gelu_coef * gelu_cube * square))
        hidden = inner * half
        r.big1[j, rows, at : at + 256] = hidden.astype(BF16)
        slope = half + hidden * (1.0 - half) * (
            2.0 * gelu_coef + 6.0 * gelu_coef * gelu_cube * square
        )
        r.big2[j, rows, at : at + 256] = slope.astype(BF16)
    r.residual[some] += mm(r.big1[j, rows, :], down).reshape(PIECE, r.share, -1)


def third_norm(r, m):
    result, normed, factor = norm_forward(r.residual[m], r.norms[2:3, :], r.norms[5:6, :])
    r.d_first[m] = result.astype(BF16)
    d_third, gain, bias = norm_backward(
        r.cotangent[m].astype(F32), normed, factor, r.norms[2:3, :]
    )
    r.sums[2:3, :] += gain
    r.sums[5:6, :] += bias
    r.d_third[m] = d_third.astype(BF16)
    r.residual[m] = d_third


def feed_back(r, j):
    up, down = columns(r, FEED + 2 * j), columns(r, FEED + 2 * j + 1)
    for i in range(r.halves):
        some, rows = pieces(r, i)
        slope = r.big2[j, rows, :].astype(F32)
        d_inner = (mm_nt(tokens(r.d_third.at[some]), down) * slope).astype(BF16)
        r.big2[j, rows, :] = d_inner
        r.residual[some] += mm_nt(d_inner, up).reshape(PIECE, r.share, -1)


def feed_grad(r, j):
    store_columns(r.g_ffn, 2 * j, mm_tn(tokens(r.second_low), r.big2[j]).astype(BF16))
    store_columns(r.g_ffn, 2 * j + 1, mm_tn(r.big1[j], tokens(r.d_third)).astype(BF16))


def second_back(r, m):
    d_cross, gain, bias = norm_backward(
        r.residual[m], r.normed2[m].astype(F32), r.factor[m, :, 1:2], r.norms[1:2, :]
    )
    r.sums[1:2, :] += gain
    r.sums[4:5, :] += bias
    r.residual[m] = d_cross
    r.d_second[m] = d_cross.astype(BF16)


def clear_pads(r):
    for s in range(r.slots):
        r.big2[s] = jnp.zeros(r.big2.shape[1:], BF16)


def backward_cross(r, m):
    marks = head_marks()
    wide = window_rows()
    reach = r.frame - wide
    d_mixed = mm(r.d_second[m], columns(r, CROSS + 3)).astype(BF16)
    queries = r.q_cross[m]
    windows = [slot_window(r, m, s) for s in range(r.slots)]

    def view(ref, s, g):
        return ref[m, pl.ds(windows[s][0], wide), g * QUAD : (g + 1) * QUAD]

    d_queries = []
    for g in range(r.quads):
        d_q, d_k, d_v = attend_back(
            [
                (
                    r.p_cross[m, s, g],
                    view(r.k_cross, s, g),
                    view(r.v_cross, s, g),
                    cut(queries, s, g),
                    cut(d_mixed, s, g),
                )
                for s in range(r.slots)
            ],
            marks,
        )
        for s in range(r.slots):
            r.big2[s, reach : reach + wide, :QUAD] = d_k[s]
            r.big2[s, reach : reach + wide, QUAD:] = d_v[s]
        total = None
        for s in range(r.slots):
            piece = r.big2[s, pl.ds(slot_shift(r, m, s), r.frame), :]
            total = piece if total is None else total + piece
        r.k_cross[m, :, g * QUAD : (g + 1) * QUAD] = total[:, :QUAD]
        r.v_cross[m, :, g * QUAD : (g + 1) * QUAD] = total[:, QUAD:]
        d_queries.append(jnp.concatenate(d_q, axis=0))
    d_queries = jnp.concatenate(d_queries, axis=1)
    r.q_cross[m] = d_queries
    d_first = r.residual[m] + mm_nt(d_queries, columns(r, CROSS + 0))
    d_attn, gain, bias = norm_backward(d_first, r.normed1[m].astype(F32), r.factor[m, :, 0:1], r.norms[0:1, :])
    r.sums[0:1, :] += gain
    r.sums[3:4, :] += bias
    r.residual[m] = d_attn
    r.d_first[m] = d_attn.astype(BF16)
    source_term = mm_nt(r.k_cross[m], columns(r, CROSS + 1)) + mm_nt(
        r.v_cross[m], columns(r, CROSS + 2)
    )
    low, edge, half = source_term.astype(BF16), r.enc_len - r.frame, r.enc_len // 2
    shift = r.table[m, 1] * 16
    r.big2[0, reach:edge, :] = jnp.zeros((edge - reach, low.shape[1]), BF16)
    r.big2[0, edge:, :] = low
    r.big2[1, : r.frame, :] = low
    r.big1[m, :half, :] = r.big2[0, pl.ds(shift, half), :]
    r.big1[m, half:, :] = r.big2[1, pl.ds(shift + (half - edge), half), :]
    r.big2[0, edge:, :] = jnp.zeros_like(low)
    r.big2[1, : r.frame, :] = jnp.zeros_like(low)


def backward_self(r, m):
    marks = head_marks()
    d_mixed = mm(r.d_first[m], columns(r, SELF + 3)).astype(BF16)
    queries, keys, values = r.q_self[m], r.k_self[m], r.v_self[m]
    units = [(s, g) for s in range(r.slots) for g in range(r.quads)]
    parts = attend_back(
        [
            (
                r.p_self[m, s, g],
                cut(keys, s, g),
                cut(values, s, g),
                cut(queries, s, g),
                cut(d_mixed, s, g),
            )
            for s, g in units
        ],
        marks,
    )
    d_q, d_k, d_v = [
        jnp.concatenate([jnp.concatenate(part[g :: r.quads], axis=0) for g in range(r.quads)], axis=1)
        for part in parts
    ]
    r.q_self[m], r.k_self[m], r.v_self[m] = d_q, d_k, d_v
    r.cotangent[m] = (r.residual[m] + mm_nt(d_q, columns(r, SELF + 0))).astype(BF16)
    r.second_low[m] = (
        mm_nt(d_k, columns(r, SELF + 1)) + mm_nt(d_v, columns(r, SELF + 2))
    ).astype(BF16)


def weight_grad(r, kind):
    left, right = {
        SELF: (r.stream, r.q_self),
        SELF + 1: (r.context, r.k_self),
        SELF + 2: (r.context, r.v_self),
        SELF + 3: (r.d_first, r.mixed_self),
        CROSS: (r.first_low, r.q_cross),
        CROSS + 1: (r.source, r.k_cross),
        CROSS + 2: (r.source, r.v_cross),
        CROSS + 3: (r.d_second, r.mixed_cross),
    }[kind]
    store_columns(*grad_place(r, kind), mm_tn(tokens(left), tokens(right)).astype(BF16))


AXES = ("y", "core", "p", "n", "x")
SIZES = {"y": NY, "core": NC, "z": NZ, "p": NZ // 2, "n": 2, "x": NX, "w": NX * NY}
JOINED = {"w": ("x", "y"), "z": ("p", "n")}


def plain(axes):
    return [part for axis in axes for part in JOINED.get(axis, (axis,))]


class Place:
    def __init__(self, groups):
        d, t = lax.axis_index(DP), lax.axis_index(TENSOR)
        high, self.low = lax.div(d, groups), lax.rem(d, groups)
        self.groups = groups
        self.a, self.b = lax.div(high, NX), lax.rem(high, NX)
        self.a1, self.a0 = lax.div(self.a, 2), lax.rem(self.a, 2)
        self.y, self.c = lax.div(t, NC), lax.rem(t, NC)
        self.t = t

    def device(self, a=None, b=None, y=None, c=None):
        a, b = self.a if a is None else a, self.b if b is None else b
        y, c = self.y if y is None else y, self.c if c is None else c
        return ((a * NX + b) * self.groups + self.low, y * NC + c)

    def up(self, k):
        return lax.rem(self.a + k, NZ)

    def peer(self, axis, k=0):
        if axis == "z":
            return self.device(a=self.up(k))
        if axis == "x":
            return self.device(b=1 - self.b)
        if axis == "y":
            return self.device(y=1 - self.y)
        if axis == "core":
            return self.device(c=1 - self.c)
        return self.device(y=1 - self.y, c=1 - self.c)

    def region(self, fixed):
        return tuple(fixed[a] if a in fixed else slice(None) for a in AXES)

    def own(self, axes):
        place = {"y": self.y, "core": self.c, "p": self.a1, "n": self.a0, "x": self.b}
        return {a: place[a] for a in plain(axes)}

    def others(self, axis):
        if axis == "z":
            ups = [self.up(k) for k in range(1, NZ)]
            return [{"p": lax.div(up, 2), "n": lax.rem(up, 2)} for up in ups]
        far = {axis: 1 - place for axis, place in self.own(AXES).items()}
        if axis == "w":
            x, y = far["x"], far["y"]
            return [{"x": x, "y": self.y}, {"x": self.b, "y": y}, {"x": x, "y": y}]
        return [{axis: far[axis]}]

    def peers(self, axis):
        if axis == "z":
            return [self.peer("z", k) for k in range(1, NZ)]
        if axis == "w":
            return [self.peer("x"), self.peer("y"), self.device(b=1 - self.b, y=1 - self.y)]
        if axis == "p":
            return [self.device(a=(1 - self.a1) * 2 + self.a0)]
        if axis == "n":
            return [self.device(a=self.a1 * 2 + 1 - self.a0)]
        return [self.peer(axis)]


class Link:
    def __init__(self, r):
        self.r = r
        self.used = 0
        self.all = []

    def slot(self):
        self.used += 1
        return self.used - 1

    def send(self, key, source, target, device):
        return pltpu.make_async_remote_copy(
            src_ref=source,
            dst_ref=target,
            send_sem=self.r.send_sems.at[key],
            recv_sem=self.r.recv_sems.at[key],
            device_id=device,
            device_id_type=MESH,
        )


class Stages:
    def __init__(self, link, counts):
        self.link = link
        self.keys = [[link.slot() for _ in range(n)] for n in counts]
        link.all.append(self)

    def start(self, stage):
        for copy in self.copies(stage):
            copy.start()

    def wait(self, stage):
        for copy in self.copies(stage):
            copy.wait_recv()

    def last(self):
        self.wait(len(self.keys) - 1)

    def turn(self, stage):
        self.wait(stage)
        self.start(stage + 1)

    def drain(self):
        for stage in range(len(self.keys)):
            for copy in self.copies(stage):
                copy.wait_send()


class Gather(Stages):
    def __init__(self, link, place, first, count, order):
        self.axes = (*order, "core")
        super().__init__(link, [SIZES[a] - 1 for a in self.axes])
        self.p, self.kinds = place, pl.ds(first, count)

    def copies(self, stage):
        p, link = self.p, self.link
        region = p.region(p.own(self.axes[stage:]))
        ref = link.r.w.at[(self.kinds, *region)]
        peers = p.peers(self.axes[stage])
        return [link.send(key, ref, ref, peer) for key, peer in zip(self.keys[stage], peers)]


class GatherNorms(Stages):
    def __init__(self, link, place):
        super().__init__(link, (NZ - 1, 1))
        self.p = place

    def copies(self, stage):
        p, pack, send = self.p, self.link.r.pack, self.link.send
        keys = self.keys[stage]
        if stage == 0:
            ref = pack.at[p.a, p.b]
            return [send(keys[k - 1], ref, ref, p.peer("z", k)) for k in range(1, NZ)]
        ref = pack.at[:, p.b]
        return [send(keys[0], ref, ref, p.peer("x"))]


class Scatter(Stages):
    def __init__(self, link, place, first, count, order, boxes):
        self.axes = ("core", *order)
        super().__init__(link, [SIZES[a] - 1 for a in self.axes])
        self.p, self.count, self.boxes = place, count, boxes
        self.ref, self.first = grad_place(link.r, first)

    def copies(self, stage):
        p, link = self.p, self.link
        axis, kept = self.axes[stage], p.own(self.axes[:stage])
        peers, others = p.peers(axis), p.others(axis)
        out = []
        for i, key in enumerate(self.keys[stage]):
            region = p.region({**kept, **others[i]})
            source = self.ref.at[(pl.ds(self.first, self.count), *region)]
            out.append(link.send(key, source, self.boxes[stage].at[i], peers[i]))
        return out

    def summed(self, stage, k):
        at = (self.first + k, *self.p.region(self.p.own(self.axes[: stage + 1])))
        box = self.boxes[stage]
        if box.shape[0] == 1:
            return at, self.ref[at].astype(F32) + box[0, k].astype(F32)
        total = self.ref[at].astype(F32)
        for i in range(box.shape[0]):
            total = total + box[i, k].astype(F32)
        return at, total

    def turn(self, stage):
        if stage == len(self.keys) - 1:
            self.share.go()
            return
        self.wait(stage)
        for k in range(self.count):
            at, total = self.summed(stage, k)
            self.ref[at] = total.astype(BF16)
        self.start(stage + 1)

    def total(self, k):
        return self.summed(len(self.keys) - 1, k)[1]


def box_name(name, stage):
    return "box_%d_%d" % (name, stage)


def scatter_boxes(name, count, order):
    out, axes = [], ("core", *order)
    for i, axis in enumerate(axes):
        free = [SIZES[a] for a in AXES if a not in plain(axes[: i + 1])]
        shape = (SIZES[axis] - 1, count, *free, 64, 128)
        out.append((box_name(name, i), pltpu.VMEM(shape, BF16)))
    return out


Q, K, V, O, C0, C1, F0, F1, F2, F3 = range(10)
SUM, ROWS = 10, 20
(
    START, SELF_FORWARD, NORM_FORWARD, CROSS_FORWARD, FEED_FORWARD, FEED_BACK,
    FEED_GRAD, NORM_BACK, CROSS_BACK, GRAD, SELF_BACK, TAIL,
) = range(12)
GATHERS = {
    Q: (SELF, 1, "pnw"),
    K: (SELF + 1, 1, "pxny"),
    V: (SELF + 2, 1, "yzx"),
    O: (SELF + 3, 1, "pxny"),
    C0: (CROSS, 2, "pnyx"),
    C1: (CROSS + 2, 2, "yxz"),
    F0: (FEED, 2, "zw"),
    F1: (FEED + 2, 2, "pnw"),
    F2: (FEED + 4, 2, "xypn"),
    F3: (FEED + 6, 2, "pynx"),
}
SCATTERS = {
    F0: (FEED, 2, "wz"),
    F1: (FEED + 2, 2, "zxy"),
    F2: (FEED + 4, 2, "xzy"),
    F3: (FEED + 6, 2, "yxz"),
    C0: (CROSS, 2, "yxz"),
    C1: (CROSS + 2, 2, "xzy"),
    O: (SELF + 3, 1, "xzy"),
    Q: (SELF, 1, "xnyp"),
    K: (SELF + 1, 1, "npw"),
    V: (SELF + 2, 1, "zw"),
}
LATE = 2
PLAN = {
    (START, 0): ((C0, -1), (F2, -1), (C1, -1), (Q, -1), (K, -1), (V, -1), (V, 0), (O, -1), (C1, 0), (F3, -1),),
    (START, 1): ((K, 0), (Q, 0), (F2, 0), (C0, 0), (K, 1), (O, 0), (F1, -1), (Q, 1), (F0, -1), (O, 1),),
    (START, 2): ((C0, 1), (C1, 1), (Q, 2), (V, 1), (K, 2), (C0, 2), (O, 2), (K, 3), (F3, 0), (V, 2),),
    (SELF_FORWARD, 1): ((O, 3), (F1, 0), (F0, 0),),
    (SELF_FORWARD, 2): ((F2, 1),),
    (SELF_FORWARD, 3): ((F3, 1), (C0, 3),),
    (NORM_FORWARD, 0): ((C1, 2),),
    (CROSS_FORWARD, 0): ((F1, 1),),
    (CROSS_FORWARD, 2): ((F2, 2), (F0, 1),),
    (CROSS_FORWARD, 3): ((F3, 2),),
    (FEED_FORWARD, 0): ((F1, 2),),
    (FEED_FORWARD, 2): ((F2, 3),),
    (FEED_FORWARD, 4): ((F3, 3),),
    (FEED_GRAD, 2): ((SUM + F0, 0),),
    (FEED_BACK, 3): ((SUM + F1, 0),),
    (CROSS_BACK, 0): ((SUM + F3, 0), (SUM + F2, 0),),
    (CROSS_BACK, 2): ((ROWS + 0, 0),),
    (GRAD, SELF + 3): ((ROWS + 1, 0), (ROWS + 2, 0), (SUM + F0, 1), (SUM + F3, 1), (SUM + F2, 1), (SUM + F1, 1),),
    (SELF_BACK, 0): ((ROWS + 3, 0),),
    (SELF_BACK, 3): ((SUM + O, 0), (SUM + F3, 2),),
    (GRAD, CROSS + 1): ((SUM + V, 0),),
    (GRAD, CROSS + 2): ((SUM + K, 0), (SUM + Q, 0),),
    (TAIL, 0): ((SUM + C0, 0), (SUM + C1, 0), (SUM + O, 1), (SUM + K, 1), (SUM + V, 1), (SUM + F0, 2), (SUM + F1, 2), (SUM + Q, 1), (SUM + C1, 1), (SUM + F2, 2),),
    (TAIL, 1): ((SUM + C0, 1), (SUM + F3, 3), (SUM + Q, 2), (SUM + F1, 3), (SUM + K, 2), (SUM + F2, 3), (SUM + C0, 2), (SUM + O, 2), (SUM + Q, 3), (SUM + C1, 2),),
}


class ScatterNorms(Stages):
    def __init__(self, link, place):
        super().__init__(link, (1, 1, 1, NZ - 1))
        self.p = place

    def copies(self, stage):
        p, r, send, keys = self.p, self.link.r, self.link.send, self.keys[stage]
        if stage == 0:
            return [send(keys[0], r.g_norm, r.n_box0, p.peer("core"))]
        if stage == 1:
            return [send(keys[0], r.n_box0, r.n_box1, p.peer("y"))]
        if stage == 2:
            return [send(keys[0], r.n_box1.at[:, 1 - p.b], r.n_box2, p.peer("x"))]
        return [
            send(keys[k - 1], r.n_box2.at[p.up(k)], r.n_box3.at[k - 1], p.peer("z", k))
            for k in range(1, NZ)
        ]

    def step(self, stage):
        p, r = self.p, self.link.r
        self.wait(stage)
        if stage == 0:
            r.n_box0[...] = r.g_norm[...] + r.n_box0[...]
        elif stage == 1:
            r.n_box1[...] = r.n_box0[...] + r.n_box1[...]
        else:
            r.n_box2[...] = r.n_box1[:, p.b] + r.n_box2[...]
        self.start(stage + 1)

    def total(self):
        r = self.link.r
        return r.n_box2[self.p.a] + ((r.n_box3[0] + r.n_box3[1]) + r.n_box3[2])


class ScatterEncoder(Stages):
    def __init__(self, link, place, share, micro):
        super().__init__(link, (NY * micro, micro))
        self.p, self.share, self.micro = place, share, micro
        self.boxes = (link.r.d_third, link.r.second_low)

    def rows(self, m, y, c):
        at = pl.multiple_of((y * NC + c) * self.share, self.share)
        return self.link.r.big1.at[m, pl.ds(at, self.share), :]

    def one(self, stage, m):
        p, r, send = self.p, self.link.r, self.link.send
        key = self.keys[stage][0]
        if stage == 0:
            return [
                send(
                    key + NY * m + y,
                    self.rows(m, y, 1 - p.c),
                    self.boxes[y].at[m],
                    p.peer("core"),
                )
                for y in range(NY)
            ]
        return [send(key + m, self.rows(m, 1 - p.y, p.c), r.e_box1.at[m], p.peer("y"))]

    def copies(self, stage):
        return [copy for m in range(self.micro) for copy in self.one(stage, m)]

    def begin(self, m):
        for copy in self.one(0, m):
            copy.start()

    def step(self, m):
        for copy in self.one(0, m):
            copy.wait_recv()
        for y in range(NY):
            ref = self.rows(m, y, self.p.c)
            ref[...] = ref[...] + self.boxes[y][m]
        for copy in self.one(1, m):
            copy.start()

    def finish(self):
        self.wait(1)
        for m in range(self.micro):
            ref = self.rows(m, self.p.y, self.p.c)
            ref[...] = ref[...] + self.link.r.e_box1[m]


class EncoderPart:
    def __init__(self, rows, m):
        self.rows, self.m = rows, m

    def turn(self, stage):
        self.rows.step(self.m)


class ShareFfn(Stages):
    def __init__(self, link, place, box, first, item):
        super().__init__(link, (3,))
        self.p, self.box, self.first, self.item = place, box, first, item

    def copies(self, stage):
        p, send, keys = self.p, self.link.send, self.keys[0]
        ref = self.box.at[p.t, pl.ds(self.first, self.item.count)]
        axes = ("core", "y", "both")
        return [send(keys[i], ref, ref, p.peer(axes[i])) for i in range(3)]

    def go(self):
        self.item.last()
        for k in range(self.item.count):
            self.box[self.p.t, self.first + k] = self.item.total(k).astype(BF16)
        self.start(0)


def each(count, body, ticks=None):
    def step(i, carry):
        for k, tick in (ticks or {}).items():
            pl.when(i == k)(tick)
        body(i)
        return carry

    lax.fori_loop(0, count, step, 0)


SEMS = 180


def layer_kernel(names, groups, scale, *refs):
    r = Refs()
    for name, ref in zip(names, refs):
        setattr(r, name, ref)
    micro, r.share = r.stream.shape[0], r.stream.shape[1]
    r.slots = r.share // SLOT
    r.quads = r.stream.shape[2] // QUAD
    r.enc_len = r.encoder.shape[1]
    r.frame = frame_rows(r.share)
    r.halves = micro // PIECE
    p = Place(groups)
    link = Link(r)

    mine = pl.ds(pl.multiple_of(p.t * r.share, r.share), r.share)
    half = pl.ds(pl.multiple_of(p.t * (r.share // 2), r.share // 2), r.share // 2)
    pairs = [
        (r.self_query, r.w.at[SELF, p.y, p.c, p.a1, p.a0, p.b]),
        (r.self_key_value, r.w.at[pl.ds(SELF + 1, 2), p.y, p.c, p.a1, p.a0, p.b]),
        (r.cross_query, r.w.at[CROSS, p.y, p.c, p.a1, p.a0, p.b]),
        (r.cross_key_value, r.w.at[pl.ds(CROSS + 1, 2), p.y, p.c, p.a1, p.a0, p.b]),
        (r.self_output, r.w.at[SELF + 3, p.y, p.c, p.a1, p.a0, p.b]),
        (r.cross_output, r.w.at[CROSS + 3, p.y, p.c, p.a1, p.a0, p.b]),
    ]
    down = pl.ds(pl.multiple_of(p.t * 128, 128), 128)
    for j in range(4):
        pairs.append(
            (
                r.ffn_out.at[pl.ds(j * 64, 64), down],
                r.w.at[FEED + 2 * j + 1, p.y, p.c, p.a1, p.a0, p.b],
            )
        )
    up = pl.ds(pl.multiple_of(p.t * 512, 512), 512)
    pairs.append((r.ffn_in.at[:, up], r.own_up))
    weights = len(pairs)
    pairs += [
        (r.stream_hbm.at[:, mine, :], r.stream),
        (r.context_hbm.at[:, mine, :], r.context),
        (r.masks_hbm.at[:, half, :], r.masks),
        (r.encoder, r.big1),
        (r.out_grad, r.cotangent),
    ]
    copies = [
        pltpu.make_async_copy(source, target, r.sems.at[i])
        for i, (source, target) in enumerate(pairs)
    ]
    partners = [p.peer("z", k) for k in range(1, NZ)]
    partners += [p.peer(axis) for axis in ("x", "y", "core", "both")]
    partners.append(p.device(b=1 - p.b, y=1 - p.y))
    barrier = pltpu.get_barrier_semaphore()
    for device in partners:
        pl.semaphore_signal(barrier, inc=1, device_id=device, device_id_type=MESH)
    for copy in copies[:weights]:
        copy.start()
    r.pack[p.a, p.b, 0:3, :64] = r.norm_gain[...].astype(F32)
    r.pack[p.a, p.b, 3:6, :64] = r.norm_bias[...].astype(F32)
    for copy in copies[:weights]:
        copy.wait()
    for j in range(4):
        at = j * 64
        r.w[FEED + 2 * j, p.y, p.c, p.a1, p.a0, p.b] = jnp.concatenate(
            [r.own_up[:, at : at + 64], r.own_up[:, 256 + at : 320 + at]], axis=1
        )
    pl.semaphore_wait(barrier, len(partners))
    for copy in copies[weights:]:
        copy.start()

    chains = {name: Gather(link, p, *spec) for name, spec in GATHERS.items()}
    norms = GatherNorms(link, p)

    def run(phase, step):
        for name, stage in PLAN.get((phase, step), ()):
            if stage < 0:
                chains[name].start(0)
            else:
                chains[name].turn(stage)

    def loop(phase, count, body, needs=None):
        ticks = {}
        for i in range(count):
            names = (needs or {}).get(i, ())
            if PLAN.get((phase, i)) or names:

                def tick(i=i, names=names):
                    run(phase, i)
                    for name in names:
                        chains[name].last()

                ticks[i] = tick
        each(count, functools.partial(body, r), ticks)

    r.sums[...] = jnp.zeros(r.sums.shape, F32)
    run(START, 0)
    norms.start(0)
    run(START, 1)
    for copy in copies[weights:]:
        copy.wait()
    run(START, 2)
    norms.wait(0)
    norms.start(1)
    for name in (Q, K, V):
        chains[name].last()
    loop(SELF_FORWARD, micro, forward_self)
    norms.wait(1)
    r.norms[...] = jnp.concatenate(
        [r.pack[d // NX, d % NX, :, :64] for d in range(NZ * NX)], axis=1
    )
    loop(NORM_FORWARD, micro, first_norm, {0: (O,)})
    loop(CROSS_FORWARD, micro, forward_cross, {0: (C0, C1)})
    loop(FEED_FORWARD, 4 * r.halves, feed, {j * r.halves: (F0 + j,) for j in range(4)})
    for item in link.all:
        item.drain()
    link.all = []
    each(micro, functools.partial(third_norm, r))
    out = [pltpu.make_async_copy(r.d_first, r.block_out, r.sems.at[0])]
    out[0].start()

    sums = {}
    for name, spec in SCATTERS.items():
        boxes = [getattr(r, box_name(name, i)) for i in range(1 + len(spec[2]))]
        sums[name] = Scatter(link, p, *spec, boxes)
        if name >= F0:
            sums[name].share = ShareFfn(link, p, r.all_ffn, 2 * (name - F0), sums[name])
    norm_sums = ScatterNorms(link, p)
    rows = ScatterEncoder(link, p, r.share, micro)
    chains = {SUM + name: item for name, item in sums.items()}
    for m in range(micro):
        chains[ROWS + m] = EncoderPart(rows, m)

    def feed_both(j):
        for i in range(4):
            pl.when(j == i)(functools.partial(run, FEED_BACK, i))
        feed_back(r, j)
        for i in range(4):
            pl.when(j == i)(functools.partial(run, FEED_GRAD, i))
        feed_grad(r, j)
        for i in range(4):
            pl.when(j == i)(functools.partial(sums[F0 + i].start, 0))

    each(4, feed_both)
    run(NORM_BACK, 0)
    each(micro, functools.partial(second_back, r))
    clear_pads(r)
    out[0].wait()

    def cross_back(r, m):
        backward_cross(r, m)
        rows.begin(m)

    loop(CROSS_BACK, micro, cross_back)
    for d in range(NZ * NX):
        r.g_norm[d // NX, d % NX] = jnp.zeros(r.g_norm.shape[2:], F32)
        r.g_norm[d // NX, d % NX, :, :64] = r.sums[:, d * 64 : (d + 1) * 64]
    norm_sums.start(0)

    def grad(kind):
        run(GRAD, kind)
        weight_grad(r, kind)

    def cross_grads(pair):
        for k in (2 * pair, 2 * pair + 1):
            grad(CROSS + k)
        sums[C0 + pair].start(0)

    for pair in range(2 - LATE):
        cross_grads(pair)
    grad(SELF + 3)
    sums[O].start(0)
    norm_sums.step(0)
    loop(SELF_BACK, micro, backward_self)
    out = [
        pltpu.make_async_copy(r.cotangent, r.stream_grad, r.sems.at[0]),
        pltpu.make_async_copy(r.second_low, r.context_grad, r.sems.at[1]),
    ]
    for copy in out:
        copy.start()
    for name, kind in ((V, SELF + 2), (Q, SELF), (K, SELF + 1)):
        grad(kind)
        sums[name].start(0)
    for pair in range(2 - LATE, 2):
        cross_grads(pair)
    run(TAIL, 0)
    norm_sums.step(1)
    run(TAIL, 1)
    norm_sums.step(2)
    rows.finish()
    mine = pl.ds(pl.multiple_of(p.t * r.share, r.share), r.share)
    out.append(pltpu.make_async_copy(r.big1.at[:, mine, :], r.encoder_grad, r.sems.at[2]))
    out[2].start()
    for j in range(4):
        sums[F0 + j].share.wait(0)
    for t in range(NY * NC):
        halves = [
            r.all_ffn[t, 2 * j, :, h * 64 : (h + 1) * 64] for h in range(2) for j in range(4)
        ]
        r.grad_ffn_in[:, t * 512 : (t + 1) * 512] = (
            jnp.concatenate(halves, axis=1).astype(F32) * scale
        )
        for j in range(4):
            r.grad_ffn_out[j * 64 : (j + 1) * 64, t * 128 : (t + 1) * 128] = (
                r.all_ffn[t, 2 * j + 1].astype(F32) * scale
            )
    norm_sums.wait(3)
    total = norm_sums.total() * scale
    r.grad_norm_gain[...] = total[0:3, :64]
    r.grad_norm_bias[...] = total[3:6, :64]
    for name in (C0, C1, O, Q, K, V):
        sums[name].last()
    r.grad_cross_query[...] = sums[C0].total(0) * scale
    r.grad_cross_key_value[0] = sums[C0].total(1) * scale
    r.grad_cross_key_value[1] = sums[C1].total(0) * scale
    r.grad_cross_output[...] = sums[C1].total(1) * scale
    r.grad_self_output[...] = sums[O].total(0) * scale
    r.grad_self_query[...] = sums[Q].total(0) * scale
    r.grad_self_key_value[0] = sums[K].total(0) * scale
    r.grad_self_key_value[1] = sums[V].total(0) * scale
    for item in link.all:
        item.drain()
    for copy in out:
        copy.wait()


def vmem():
    return pl.BlockSpec(memory_space=pltpu.VMEM)


def hbm():
    return pl.BlockSpec(memory_space=pl.ANY)


WEIGHTS = (
    "self_query", "self_key_value", "self_output",
    "cross_query", "cross_key_value", "cross_output",
    "ffn_in", "ffn_out", "norm_gain", "norm_bias",
)


def layer(groups, scale, stream, context, encoder, masks, table, out_grad, weights):
    micro, row, width = stream.shape
    share = out_grad.shape[1]
    enc_len = encoder.shape[1]
    frame, wide = frame_rows(share), window_rows()
    slots, quads = share // SLOT, width // QUAD
    small = ("norm_gain", "norm_bias")
    ins = [
        ("stream_hbm", stream, hbm()),
        ("context_hbm", context, hbm()),
        ("encoder", encoder, hbm()),
        ("masks_hbm", masks, hbm()),
        ("table", table, pl.BlockSpec(memory_space=pltpu.SMEM)),
        ("out_grad", out_grad, hbm()),
    ]
    for name, value in zip(WEIGHTS, weights):
        ins.append((name, value, vmem() if name in small else hbm()))
    part = jax.ShapeDtypeStruct((micro, share, width), BF16)
    outs = [
        ("block_out", part, hbm()),
        ("stream_grad", part, hbm()),
        ("context_grad", part, hbm()),
        ("encoder_grad", part, hbm()),
    ]
    for name, value in zip(WEIGHTS, weights):
        outs.append(("grad_" + name, jax.ShapeDtypeStruct(value.shape, F32), vmem()))
    low = pltpu.VMEM((micro, share, width), BF16)
    high = pltpu.VMEM((micro, share, width), F32)
    window = pltpu.VMEM((micro, frame, width), BF16)
    big = pltpu.VMEM((micro, enc_len, width), BF16)
    norm = pltpu.VMEM((NZ, NX, 8, 128), F32)
    scratch = [
        ("w", pltpu.VMEM((KINDS, NY, NC, NZ // 2, 2, NX, 64, 128), BF16)),
        ("g_ffn", pltpu.VMEM((8, NY, NC, NZ // 2, 2, NX, 64, 128), BF16)),
        ("stream", low),
        ("context", low),
        ("cotangent", low),
        ("masks", pltpu.VMEM((micro, share // 2, 128), jnp.int32)),
        ("q_self", low),
        ("k_self", low),
        ("v_self", low),
        ("mixed_self", low),
        ("first_low", low),
        ("q_cross", low),
        ("k_cross", window),
        ("v_cross", window),
        ("source", window),
        ("mixed_cross", low),
        ("second_low", low),
        ("d_third", low),
        ("d_second", low),
        ("d_first", low),
        ("p_self", pltpu.VMEM((micro, slots, quads, SLOT, QUAD), BF16)),
        ("p_cross", pltpu.VMEM((micro, slots, quads, wide, QUAD), BF16)),
        ("residual", high),
        ("normed1", low),
        ("normed2", low),
        ("factor", pltpu.VMEM((micro, share, 2), F32)),
        ("big1", big),
        ("big2", big),
        ("own_up", pltpu.VMEM((64, 512), BF16)),
        ("norms", pltpu.VMEM((8, width), F32)),
        ("sums", pltpu.VMEM((8, width), F32)),
        ("pack", norm),
        ("g_norm", norm),
        ("n_box0", norm),
        ("n_box1", norm),
        ("n_box2", pltpu.VMEM((NZ, 8, 128), F32)),
        ("n_box3", pltpu.VMEM((NZ - 1, 8, 128), F32)),
        ("e_box1", low),
        ("all_ffn", pltpu.VMEM((NY * NC, 8, 64, 128), BF16)),
        ("sems", pltpu.SemaphoreType.DMA((19,))),
        ("send_sems", pltpu.SemaphoreType.DMA((SEMS,))),
        ("recv_sems", pltpu.SemaphoreType.DMA((SEMS,))),
    ]
    for name, (_, count, order) in SCATTERS.items():
        scratch += scatter_boxes(name, count, order)
    names = [item[0] for item in ins + outs + scratch]
    return pl.pallas_call(
        functools.partial(layer_kernel, names, groups, scale),
        out_shape=[item[1] for item in outs],
        in_specs=[item[2] for item in ins],
        out_specs=[item[2] for item in outs],
        scratch_shapes=[item[1] for item in scratch],
        compiler_params=pltpu.CompilerParams(
            vmem_limit_bytes=VMEM_LIMIT, collective_id=0, has_side_effects=True
        ),
        cost_estimate=pl.CostEstimate(
            flops=30_000_000_000, bytes_accessed=30_000_000, transcendentals=4_000_000
        ),
    )(*[item[1] for item in ins])


def copy_kernel(count, *refs):
    given, results, held = (refs[i * count : (i + 1) * count] for i in range(3))
    sems = refs[3 * count]
    loads = [pltpu.make_async_copy(a, b, sems.at[0, i]) for i, (a, b) in enumerate(zip(given, held))]
    stores = [
        pltpu.make_async_copy(a, b, sems.at[1, i]) for i, (a, b) in enumerate(zip(held, results))
    ]
    for load in loads:
        load.start()
    for load, store in zip(loads, stores):
        load.wait()
        store.start()
    for store in stores:
        store.wait()


def copy_all(values):
    count = len(values)
    return pl.pallas_call(
        functools.partial(copy_kernel, count),
        out_shape=[jax.ShapeDtypeStruct(v.shape, v.dtype) for v in values],
        in_specs=[hbm()] * count,
        out_specs=[hbm()] * count,
        scratch_shapes=[pltpu.VMEM(v.shape, v.dtype) for v in values]
        + [pltpu.SemaphoreType.DMA((2, count))],
        compiler_params=pltpu.CompilerParams(vmem_limit_bytes=VMEM_LIMIT),
    )(*values)


GATHER_DIM = (0, 1, 0, 0, 1, 0, 0, 0, 1, 1)


def per_device(
    query_stream,
    context_stream,
    encoder_out,
    query_masks,
    source_segments,
    out_grad,
    *weights,
):
    micro, row, width = query_stream.shape
    share = out_grad.shape[1]
    slots = share // SLOT
    t = lax.axis_index(TENSOR)
    replicas = lax.axis_size(DP)
    scale = float(micro * row * replicas) ** (-0.5)
    groups = replicas // (NZ * NX)
    weights = [item.T if i in (2, 5) else item for i, item in enumerate(weights)]
    near = [[i * groups + j for j in range(groups)] for i in range(NZ * NX)]
    if groups > 1:
        weights = [
            lax.all_gather(item, DP, axis=dim, tiled=True, axis_index_groups=near)
            for item, dim in zip(weights, GATHER_DIM)
        ]
    bounds = t * slots + jnp.arange(slots + 1, dtype=jnp.int32)
    starts = jnp.sum(
        (source_segments < bounds[None, :, None]).astype(jnp.int32), axis=-1
    )
    table = window_table(starts, share, encoder_out.shape[1])
    results = layer(
        groups, scale, query_stream, context_stream, encoder_out, query_masks, table,
        out_grad, weights,
    )
    results = copy_all(results)
    grads = results[4:]
    if groups > 1:
        grads = [
            lax.psum_scatter(
                item, DP, scatter_dimension=dim, tiled=True, axis_index_groups=near
            )
            for item, dim in zip(grads, GATHER_DIM)
        ]
    grads = [item.T if i in (2, 5) else item for i, item in enumerate(grads)]
    return (*results[:4], *grads)


def solution(mesh):
    in_specs = (
        P(None, DP, None),
        P(None, DP, None),
        P(None, DP, None),
        P(None, DP, None),
        P(None, DP, None),
        P(None, (DP, TENSOR), None),
        P(DP, TENSOR),
        P(None, DP, TENSOR),
        P(TENSOR, DP),
        P(DP, TENSOR),
        P(None, DP, TENSOR),
        P(TENSOR, DP),
        P(DP, None),
        P(DP, None),
        P(None, DP),
        P(None, DP),
    )
    out_specs = (
        P(None, (DP, TENSOR), None),
        P(None, (DP, TENSOR), None),
        P(None, (DP, TENSOR), None),
        P(None, (DP, TENSOR), None),
        P(DP, TENSOR),
        P(None, DP, TENSOR),
        P(TENSOR, DP),
        P(DP, TENSOR),
        P(None, DP, TENSOR),
        P(TENSOR, DP),
        P(DP, None),
        P(DP, None),
        P(None, DP),
        P(None, DP),
    )
    return jax.shard_map(
        per_device, mesh=mesh, in_specs=in_specs, out_specs=out_specs, check_vma=False
    )
```

```python
import functools

import jax
import jax.numpy as jnp
from jax import lax
from jax.experimental import pallas as pl
from jax.experimental.pallas import tpu as pltpu
from jax.sharding import PartitionSpec as P

HEAD_DIM = 64
SLOT = 64
SEG_MOST = 128
QUAD = 4 * HEAD_DIM
PAIR = 2 * HEAD_DIM
NZ, NX, NY, NC = 4, 2, 2, 2
PIECE = 2
SELF, CROSS, FEED, KINDS = 0, 4, 8, 16
BF16 = jnp.bfloat16
F32 = jnp.float32
MESH = pl.DeviceIdType.MESH
DP, TENSOR = "dp", "tensor"

epsilon = 1e-05
neg_fill = -1e30
gelu_coef = 0.7978845608028654
gelu_cube = 0.044715
VMEM_LIMIT = 65400 * 1024


def mm(left, right):
    return jnp.dot(left, right, preferred_element_type=F32)


def mm_nt(left, right):
    return lax.dot_general(left, right, (((1,), (1,)), ((), ())), preferred_element_type=F32)


def mm_tn(left, right):
    return lax.dot_general(left, right, (((0,), (0,)), ((), ())), preferred_element_type=F32)


def norm_forward(value, gain, bias):
    center = jnp.mean(value, axis=-1, keepdims=True)
    shifted = value - center
    factor = lax.rsqrt(jnp.mean(shifted * shifted, axis=-1, keepdims=True) + epsilon)
    normed = shifted * factor
    return normed * gain + bias, normed, factor


def norm_backward(incoming, normed, factor, gain):
    scaled = incoming * gain
    inside = (
        scaled
        - jnp.mean(scaled, axis=-1, keepdims=True)
        - normed * jnp.mean(scaled * normed, axis=-1, keepdims=True)
    )
    return (
        factor * inside,
        jnp.sum(incoming * normed, axis=0, keepdims=True),
        jnp.sum(incoming, axis=0, keepdims=True),
    )


def columns(r, kind):
    parts = [r.w[kind, t // NC, t % NC].reshape(-1, 128) for t in range(NY * NC)]
    return jnp.concatenate(parts, axis=1)


def grad_place(r, kind):
    if kind >= FEED:
        return r.g_ffn, kind - FEED
    return r.w, kind + FEED


def store_columns(ref, at, value):
    for t in range(NY * NC):
        ref[at, t // NC, t % NC] = value[:, t * 128 : (t + 1) * 128].reshape(NZ // 2, 2, NX, -1, 128)


def head_marks():
    lane = lax.broadcasted_iota(jnp.int32, (1, QUAD), 1) // HEAD_DIM
    return [jnp.where(lane == h, 1.0, 0.0).astype(BF16) for h in range(4)]


def spread_heads(rows, marks):
    return jnp.concatenate([rows * mark for mark in marks], axis=0)


def fold_pairs(weights, rows):
    first = lax.broadcasted_iota(jnp.int32, (SLOT, PAIR), 1) < HEAD_DIM
    parts = []
    for p in range(2):
        cut = slice(p * PAIR, (p + 1) * PAIR)
        full = mm_tn(weights[:, cut], rows[:, cut])
        parts.append(jnp.where(first, full[:SLOT], full[SLOT:]))
    return jnp.concatenate(parts, axis=1)


def soft_keys(scores, allowed):
    scores = jnp.where(allowed, scores, neg_fill)
    top = jnp.max(scores, axis=0, keepdims=True)
    raised = jnp.exp(scores - top)
    return (raised * (1.0 / jnp.sum(raised, axis=0, keepdims=True))).astype(BF16)


def attend_back(items, marks):
    d_spread = [spread_heads(item[4], marks) for item in items]
    d_probs = [mm_nt(item[2], spread) for item, spread in zip(items, d_spread)]
    d_values = [mm(item[0], spread).astype(BF16) for item, spread in zip(items, d_spread)]
    d_scores = []
    for item, d_prob in zip(items, d_probs):
        wide = item[0].astype(F32)
        inner = jnp.sum(wide * d_prob, axis=0, keepdims=True)
        d_scores.append((wide * (d_prob - inner)).astype(BF16))
    d_keys = [
        mm(d_score, spread_heads(item[3], marks)).astype(BF16)
        for item, d_score in zip(items, d_scores)
    ]
    d_queries = [
        (fold_pairs(d_score, item[1]) * HEAD_DIM ** (-0.5)).astype(BF16)
        for item, d_score in zip(items, d_scores)
    ]
    return d_queries, d_keys, d_values


def cut(value, s, g):
    return value[s * SLOT : (s + 1) * SLOT, g * QUAD : (g + 1) * QUAD]


class Refs:
    pass


def frame_rows(share):
    return (share // SLOT) * SEG_MOST + 16


def window_rows():
    return SEG_MOST + 16


def window_table(starts, share, enc_len):
    frame, wide = frame_rows(share), window_rows()
    base = jnp.minimum(starts[:, :1] // 16 * 16, enc_len - frame)
    begin = starts[:, :-1] - base
    at = jnp.minimum(begin // 16 * 16, frame - wide)
    low = begin - at
    high = low + starts[:, 1:] - starts[:, :-1]
    return jnp.concatenate(
        [base // 16, (enc_len - frame - base) // 16, at // 16, low, high, (frame - wide - at) // 16],
        axis=1,
    )


def frame_start(r, m):
    return r.table[m, 0] * 16


def slot_window(r, m, s):
    at = r.table[m, 2 + s] * 16
    return at, r.table[m, 2 + r.slots + s], r.table[m, 2 + 2 * r.slots + s]


def slot_shift(r, m, s):
    return r.table[m, 2 + 3 * r.slots + s] * 16


def forward_self(r, m):
    marks = head_marks()
    stream, context = r.stream[m], r.context[m]
    queries = (mm(stream, columns(r, SELF + 0)) * HEAD_DIM ** (-0.5)).astype(BF16)
    keys = mm(context, columns(r, SELF + 1)).astype(BF16)
    values = mm(context, columns(r, SELF + 2)).astype(BF16)
    r.q_self[m], r.k_self[m], r.v_self[m] = queries, keys, values
    row = lax.broadcasted_iota(jnp.int32, (SLOT, QUAD), 0)
    lane = lax.broadcasted_iota(jnp.int32, (SLOT, QUAD), 1) % SLOT
    place = jnp.where(lane == 2 * (row % 32) + row // 32, 1.0, 0.0).astype(BF16)
    units = [(s, g) for s in range(r.slots) for g in range(r.quads)]
    allowed = []
    for s in range(r.slots):
        bits = r.masks[m, s * 32 : (s + 1) * 32].astype(F32)
        bits = jnp.concatenate([bits[:, :SLOT], bits[:, SLOT:]], axis=0).astype(BF16)
        allowed.append(mm_tn(bits, place) > 0.5)
    scores = [mm_nt(cut(keys, s, g), spread_heads(cut(queries, s, g), marks)) for s, g in units]
    probs = [soft_keys(score, allowed[s]) for score, (s, g) in zip(scores, units)]
    mixed = [fold_pairs(prob, cut(values, s, g)).astype(BF16) for prob, (s, g) in zip(probs, units)]
    for prob, one, (s, g) in zip(probs, mixed, units):
        r.p_self[m, s, g] = prob
        r.mixed_self[m, s * SLOT : (s + 1) * SLOT, g * QUAD : (g + 1) * QUAD] = one


def first_norm(r, m):
    attn = mm_nt(r.mixed_self[m], columns(r, SELF + 3))
    first, normed, factor = norm_forward(
        r.stream[m].astype(F32) + attn, r.norms[0:1, :], r.norms[3:4, :]
    )
    r.residual[m], r.factor[m, :, 0:1] = first, factor
    r.normed1[m] = normed.astype(BF16)
    r.first_low[m] = first.astype(BF16)


def forward_cross(r, m):
    marks = head_marks()
    base = frame_start(r, m)
    source = r.big1[m, pl.ds(base, r.frame), :]
    r.source[m] = source
    r.k_cross[m] = mm(source, columns(r, CROSS + 1)).astype(BF16)
    r.v_cross[m] = mm(source, columns(r, CROSS + 2)).astype(BF16)
    queries = (mm(r.first_low[m], columns(r, CROSS + 0)) * HEAD_DIM ** (-0.5)).astype(BF16)
    r.q_cross[m] = queries
    wide = window_rows()
    row = lax.broadcasted_iota(jnp.int32, (wide, QUAD), 0)
    units = [(s, g) for s in range(r.slots) for g in range(r.quads)]
    windows = [slot_window(r, m, s) for s in range(r.slots)]
    allowed = [(row >= low) & (row < high) for _, low, high in windows]

    def view(ref, s, g):
        return ref[m, pl.ds(windows[s][0], wide), g * QUAD : (g + 1) * QUAD]

    scores = [
        mm_nt(view(r.k_cross, s, g), spread_heads(cut(queries, s, g), marks)) for s, g in units
    ]
    probs = [soft_keys(score, allowed[s]) for score, (s, g) in zip(scores, units)]
    mixed = [
        fold_pairs(prob, view(r.v_cross, s, g)).astype(BF16) for prob, (s, g) in zip(probs, units)
    ]
    for prob, (s, g) in zip(probs, units):
        r.p_cross[m, s, g] = prob
    mixed = jnp.concatenate(
        [
            jnp.concatenate(mixed[s * r.quads : (s + 1) * r.quads], axis=1)
            for s in range(r.slots)
        ],
        axis=0,
    )
    r.mixed_cross[m] = mixed
    attn = mm_nt(mixed, columns(r, CROSS + 3))
    second, normed, factor = norm_forward(
        r.residual[m] + attn, r.norms[1:2, :], r.norms[4:5, :]
    )
    r.residual[m], r.factor[m, :, 1:2] = second, factor
    r.normed2[m] = normed.astype(BF16)
    r.second_low[m] = second.astype(BF16)


def tokens(ref):
    value = ref[...]
    return value.reshape(-1, value.shape[-1])


def pieces(r, i):
    return pl.ds(i * PIECE, PIECE), pl.ds(pl.multiple_of(i * PIECE * r.share, 512), PIECE * r.share)


def feed(r, i):
    j = lax.div(i, r.halves)
    some, rows = pieces(r, lax.rem(i, r.halves))
    low = tokens(r.second_low.at[some])
    up, down = columns(r, FEED + 2 * j), columns(r, FEED + 2 * j + 1)
    for at in range(0, 512, 256):
        inner = mm(low, up[:, at : at + 256])
        square = inner * inner
        half = 0.5 + 0.5 * jnp.tanh(inner * (gelu_coef + gelu_coef * gelu_cube * square))
        hidden = inner * half
        r.big1[j, rows, at : at + 256] = hidden.astype(BF16)
        slope = half + hidden * (1.0 - half) * (
            2.0 * gelu_coef + 6.0 * gelu_coef * gelu_cube * square
        )
        r.big2[j, rows, at : at + 256] = slope.astype(BF16)
    r.residual[some] += mm(r.big1[j, rows, :], down).reshape(PIECE, r.share, -1)


def third_norm(r, m):
    result, normed, factor = norm_forward(r.residual[m], r.norms[2:3, :], r.norms[5:6, :])
    r.d_first[m] = result.astype(BF16)
    d_third, gain, bias = norm_backward(
        r.cotangent[m].astype(F32), normed, factor, r.norms[2:3, :]
    )
    r.sums[2:3, :] += gain
    r.sums[5:6, :] += bias
    r.d_third[m] = d_third.astype(BF16)
    r.residual[m] = d_third


def feed_back(r, j):
    up, down = columns(r, FEED + 2 * j), columns(r, FEED + 2 * j + 1)
    for i in range(r.halves):
        some, rows = pieces(r, i)
        slope = r.big2[j, rows, :].astype(F32)
        d_inner = (mm_nt(tokens(r.d_third.at[some]), down) * slope).astype(BF16)
        r.big2[j, rows, :] = d_inner
        r.residual[some] += mm_nt(d_inner, up).reshape(PIECE, r.share, -1)


def feed_grad(r, j):
    store_columns(r.g_ffn, 2 * j, mm_tn(tokens(r.second_low), r.big2[j]).astype(BF16))
    store_columns(r.g_ffn, 2 * j + 1, mm_tn(r.big1[j], tokens(r.d_third)).astype(BF16))


def second_back(r, m):
    d_cross, gain, bias = norm_backward(
        r.residual[m], r.normed2[m].astype(F32), r.factor[m, :, 1:2], r.norms[1:2, :]
    )
    r.sums[1:2, :] += gain
    r.sums[4:5, :] += bias
    r.residual[m] = d_cross
    r.d_second[m] = d_cross.astype(BF16)


def clear_pads(r):
    for s in range(r.slots):
        r.big2[s] = jnp.zeros(r.big2.shape[1:], BF16)


def backward_cross(r, m):
    marks = head_marks()
    wide = window_rows()
    reach = r.frame - wide
    d_mixed = mm(r.d_second[m], columns(r, CROSS + 3)).astype(BF16)
    queries = r.q_cross[m]
    windows = [slot_window(r, m, s) for s in range(r.slots)]

    def view(ref, s, g):
        return ref[m, pl.ds(windows[s][0], wide), g * QUAD : (g + 1) * QUAD]

    d_queries = []
    for g in range(r.quads):
        d_q, d_k, d_v = attend_back(
            [
                (
                    r.p_cross[m, s, g],
                    view(r.k_cross, s, g),
                    view(r.v_cross, s, g),
                    cut(queries, s, g),
                    cut(d_mixed, s, g),
                )
                for s in range(r.slots)
            ],
            marks,
        )
        for s in range(r.slots):
            r.big2[s, reach : reach + wide, :QUAD] = d_k[s]
            r.big2[s, reach : reach + wide, QUAD:] = d_v[s]
        total = None
        for s in range(r.slots):
            piece = r.big2[s, pl.ds(slot_shift(r, m, s), r.frame), :]
            total = piece if total is None else total + piece
        r.k_cross[m, :, g * QUAD : (g + 1) * QUAD] = total[:, :QUAD]
        r.v_cross[m, :, g * QUAD : (g + 1) * QUAD] = total[:, QUAD:]
        d_queries.append(jnp.concatenate(d_q, axis=0))
    d_queries = jnp.concatenate(d_queries, axis=1)
    r.q_cross[m] = d_queries
    d_first = r.residual[m] + mm_nt(d_queries, columns(r, CROSS + 0))
    d_attn, gain, bias = norm_backward(d_first, r.normed1[m].astype(F32), r.factor[m, :, 0:1], r.norms[0:1, :])
    r.sums[0:1, :] += gain
    r.sums[3:4, :] += bias
    r.residual[m] = d_attn
    r.d_first[m] = d_attn.astype(BF16)
    source_term = mm_nt(r.k_cross[m], columns(r, CROSS + 1)) + mm_nt(
        r.v_cross[m], columns(r, CROSS + 2)
    )
    low, edge, half = source_term.astype(BF16), r.enc_len - r.frame, r.enc_len // 2
    shift = r.table[m, 1] * 16
    r.big2[0, reach:edge, :] = jnp.zeros((edge - reach, low.shape[1]), BF16)
    r.big2[0, edge:, :] = low
    r.big2[1, : r.frame, :] = low
    r.big1[m, :half, :] = r.big2[0, pl.ds(shift, half), :]
    r.big1[m, half:, :] = r.big2[1, pl.ds(shift + (half - edge), half), :]
    r.big2[0, edge:, :] = jnp.zeros_like(low)
    r.big2[1, : r.frame, :] = jnp.zeros_like(low)


def backward_self(r, m):
    marks = head_marks()
    d_mixed = mm(r.d_first[m], columns(r, SELF + 3)).astype(BF16)
    queries, keys, values = r.q_self[m], r.k_self[m], r.v_self[m]
    units = [(s, g) for s in range(r.slots) for g in range(r.quads)]
    parts = attend_back(
        [
            (
                r.p_self[m, s, g],
                cut(keys, s, g),
                cut(values, s, g),
                cut(queries, s, g),
                cut(d_mixed, s, g),
            )
            for s, g in units
        ],
        marks,
    )
    d_q, d_k, d_v = [
        jnp.concatenate([jnp.concatenate(part[g :: r.quads], axis=0) for g in range(r.quads)], axis=1)
        for part in parts
    ]
    r.q_self[m], r.k_self[m], r.v_self[m] = d_q, d_k, d_v
    r.cotangent[m] = (r.residual[m] + mm_nt(d_q, columns(r, SELF + 0))).astype(BF16)
    r.second_low[m] = (
        mm_nt(d_k, columns(r, SELF + 1)) + mm_nt(d_v, columns(r, SELF + 2))
    ).astype(BF16)


def weight_grad(r, kind):
    left, right = {
        SELF: (r.stream, r.q_self),
        SELF + 1: (r.context, r.k_self),
        SELF + 2: (r.context, r.v_self),
        SELF + 3: (r.d_first, r.mixed_self),
        CROSS: (r.first_low, r.q_cross),
        CROSS + 1: (r.source, r.k_cross),
        CROSS + 2: (r.source, r.v_cross),
        CROSS + 3: (r.d_second, r.mixed_cross),
    }[kind]
    store_columns(*grad_place(r, kind), mm_tn(tokens(left), tokens(right)).astype(BF16))


AXES = ("y", "core", "p", "n", "x")
SIZES = {"y": NY, "core": NC, "z": NZ, "p": NZ // 2, "n": 2, "x": NX, "w": NX * NY}
JOINED = {"w": ("x", "y"), "z": ("p", "n")}


def plain(axes):
    return [part for axis in axes for part in JOINED.get(axis, (axis,))]


class Place:
    def __init__(self, groups):
        d, t = lax.axis_index(DP), lax.axis_index(TENSOR)
        high, self.low = lax.div(d, groups), lax.rem(d, groups)
        self.groups = groups
        self.a, self.b = lax.div(high, NX), lax.rem(high, NX)
        self.a1, self.a0 = lax.div(self.a, 2), lax.rem(self.a, 2)
        self.y, self.c = lax.div(t, NC), lax.rem(t, NC)
        self.t = t

    def device(self, a=None, b=None, y=None, c=None):
        a, b = self.a if a is None else a, self.b if b is None else b
        y, c = self.y if y is None else y, self.c if c is None else c
        return ((a * NX + b) * self.groups + self.low, y * NC + c)

    def up(self, k):
        return lax.rem(self.a + k, NZ)

    def peer(self, axis, k=0):
        if axis == "z":
            return self.device(a=self.up(k))
        if axis == "x":
            return self.device(b=1 - self.b)
        if axis == "y":
            return self.device(y=1 - self.y)
        if axis == "core":
            return self.device(c=1 - self.c)
        return self.device(y=1 - self.y, c=1 - self.c)

    def region(self, fixed):
        return tuple(fixed[a] if a in fixed else slice(None) for a in AXES)

    def own(self, axes):
        place = {"y": self.y, "core": self.c, "p": self.a1, "n": self.a0, "x": self.b}
        return {a: place[a] for a in plain(axes)}

    def others(self, axis):
        if axis == "z":
            ups = [self.up(k) for k in range(1, NZ)]
            return [{"p": lax.div(up, 2), "n": lax.rem(up, 2)} for up in ups]
        far = {axis: 1 - place for axis, place in self.own(AXES).items()}
        if axis == "w":
            x, y = far["x"], far["y"]
            return [{"x": x, "y": self.y}, {"x": self.b, "y": y}, {"x": x, "y": y}]
        return [{axis: far[axis]}]

    def peers(self, axis):
        if axis == "z":
            return [self.peer("z", k) for k in range(1, NZ)]
        if axis == "w":
            return [self.peer("x"), self.peer("y"), self.device(b=1 - self.b, y=1 - self.y)]
        if axis == "p":
            return [self.device(a=(1 - self.a1) * 2 + self.a0)]
        if axis == "n":
            return [self.device(a=self.a1 * 2 + 1 - self.a0)]
        return [self.peer(axis)]


class Link:
    def __init__(self, r):
        self.r = r
        self.used = 0
        self.all = []

    def slot(self):
        self.used += 1
        return self.used - 1

    def send(self, key, source, target, device):
        return pltpu.make_async_remote_copy(
            src_ref=source,
            dst_ref=target,
            send_sem=self.r.send_sems.at[key],
            recv_sem=self.r.recv_sems.at[key],
            device_id=device,
            device_id_type=MESH,
        )


class Stages:
    def __init__(self, link, counts):
        self.link = link
        self.keys = [[link.slot() for _ in range(n)] for n in counts]
        link.all.append(self)

    def start(self, stage):
        for copy in self.copies(stage):
            copy.start()

    def wait(self, stage):
        for copy in self.copies(stage):
            copy.wait_recv()

    def last(self):
        self.wait(len(self.keys) - 1)

    def turn(self, stage):
        self.wait(stage)
        self.start(stage + 1)

    def drain(self):
        for stage in range(len(self.keys)):
            for copy in self.copies(stage):
                copy.wait_send()


class Gather(Stages):
    def __init__(self, link, place, first, count, order):
        self.axes = (*order, "core")
        super().__init__(link, [SIZES[a] - 1 for a in self.axes])
        self.p, self.kinds = place, pl.ds(first, count)

    def copies(self, stage):
        p, link = self.p, self.link
        region = p.region(p.own(self.axes[stage:]))
        ref = link.r.w.at[(self.kinds, *region)]
        peers = p.peers(self.axes[stage])
        return [link.send(key, ref, ref, peer) for key, peer in zip(self.keys[stage], peers)]


class GatherNorms(Stages):
    def __init__(self, link, place):
        super().__init__(link, (NZ - 1, 1))
        self.p = place

    def copies(self, stage):
        p, pack, send = self.p, self.link.r.pack, self.link.send
        keys = self.keys[stage]
        if stage == 0:
            ref = pack.at[p.a, p.b]
            return [send(keys[k - 1], ref, ref, p.peer("z", k)) for k in range(1, NZ)]
        ref = pack.at[:, p.b]
        return [send(keys[0], ref, ref, p.peer("x"))]


class Scatter(Stages):
    def __init__(self, link, place, first, count, order, boxes):
        self.axes = ("core", *order)
        super().__init__(link, [SIZES[a] - 1 for a in self.axes])
        self.p, self.count, self.boxes = place, count, boxes
        self.ref, self.first = grad_place(link.r, first)

    def copies(self, stage):
        p, link = self.p, self.link
        axis, kept = self.axes[stage], p.own(self.axes[:stage])
        peers, others = p.peers(axis), p.others(axis)
        out = []
        for i, key in enumerate(self.keys[stage]):
            region = p.region({**kept, **others[i]})
            source = self.ref.at[(pl.ds(self.first, self.count), *region)]
            out.append(link.send(key, source, self.boxes[stage].at[i], peers[i]))
        return out

    def summed(self, stage, k):
        at = (self.first + k, *self.p.region(self.p.own(self.axes[: stage + 1])))
        box = self.boxes[stage]
        if box.shape[0] == 1:
            return at, self.ref[at].astype(F32) + box[0, k].astype(F32)
        total = self.ref[at].astype(F32)
        for i in range(box.shape[0]):
            total = total + box[i, k].astype(F32)
        return at, total

    def turn(self, stage):
        if stage == len(self.keys) - 1:
            self.share.go()
            return
        self.wait(stage)
        for k in range(self.count):
            if self.boxes[stage].shape[0] == 1:
                at = (self.first + k, *self.p.region(self.p.own(self.axes[: stage + 1])))
                self.ref[at] = self.ref[at] + self.boxes[stage][0, k]
            else:
                at, total = self.summed(stage, k)
                self.ref[at] = total.astype(BF16)
        self.start(stage + 1)

    def total(self, k):
        return self.summed(len(self.keys) - 1, k)[1]


def box_name(name, stage):
    return "box_%d_%d" % (name, stage)


def scatter_boxes(name, count, order):
    out, axes = [], ("core", *order)
    for i, axis in enumerate(axes):
        free = [SIZES[a] for a in AXES if a not in plain(axes[: i + 1])]
        shape = (SIZES[axis] - 1, count, *free, 64, 128)
        out.append((box_name(name, i), pltpu.VMEM(shape, BF16)))
    return out


Q, K, V, O, C0, C1, F0, F1, F2, F3 = range(10)
SUM, ROWS = 10, 20
(
    START, SELF_FORWARD, NORM_FORWARD, CROSS_FORWARD, FEED_FORWARD, FEED_BACK,
    FEED_GRAD, NORM_BACK, CROSS_BACK, GRAD, SELF_BACK, TAIL,
) = range(12)
GATHERS = {
    Q: (SELF, 1, "pnw"),
    K: (SELF + 1, 1, "pxny"),
    V: (SELF + 2, 1, "yzx"),
    O: (SELF + 3, 1, "pxny"),
    C0: (CROSS, 2, "pnyx"),
    C1: (CROSS + 2, 2, "yxz"),
    F0: (FEED, 2, "zw"),
    F1: (FEED + 2, 2, "pnw"),
    F2: (FEED + 4, 2, "xypn"),
    F3: (FEED + 6, 2, "pynx"),
}
SCATTERS = {
    F0: (FEED, 2, "wz"),
    F1: (FEED + 2, 2, "zxy"),
    F2: (FEED + 4, 2, "xzy"),
    F3: (FEED + 6, 2, "yxz"),
    C0: (CROSS, 2, "yxz"),
    C1: (CROSS + 2, 2, "xzy"),
    O: (SELF + 3, 1, "xzy"),
    Q: (SELF, 1, "xnyp"),
    K: (SELF + 1, 1, "npw"),
    V: (SELF + 2, 1, "zw"),
}
LATE = 2
PLAN = {
    (START, 0): ((C0, -1), (F2, -1), (C1, -1), (Q, -1), (K, -1), (V, -1), (V, 0), (O, -1), (C1, 0), (F3, -1),),
    (START, 1): ((K, 0), (Q, 0), (F2, 0), (C0, 0), (K, 1), (O, 0), (F1, -1), (Q, 1), (F0, -1), (O, 1),),
    (START, 2): ((C0, 1), (C1, 1), (Q, 2), (V, 1), (K, 2), (C0, 2), (O, 2), (K, 3), (F3, 0), (V, 2),),
    (SELF_FORWARD, 1): ((O, 3), (F1, 0), (F0, 0),),
    (SELF_FORWARD, 2): ((F2, 1),),
    (SELF_FORWARD, 3): ((F3, 1), (C0, 3),),
    (NORM_FORWARD, 0): ((C1, 2),),
    (CROSS_FORWARD, 0): ((F1, 1),),
    (CROSS_FORWARD, 2): ((F2, 2), (F0, 1),),
    (CROSS_FORWARD, 3): ((F3, 2),),
    (FEED_FORWARD, 0): ((F1, 2),),
    (FEED_FORWARD, 2): ((F2, 3),),
    (FEED_FORWARD, 4): ((F3, 3),),
    (FEED_GRAD, 2): ((SUM + F0, 0),),
    (FEED_BACK, 3): ((SUM + F1, 0),),
    (CROSS_BACK, 0): ((SUM + F3, 0), (SUM + F2, 0),),
    (CROSS_BACK, 2): ((ROWS + 0, 0),),
    (GRAD, SELF + 3): ((ROWS + 1, 0), (ROWS + 2, 0), (SUM + F0, 1), (SUM + F3, 1), (SUM + F2, 1), (SUM + F1, 1),),
    (SELF_BACK, 0): ((ROWS + 3, 0),),
    (SELF_BACK, 3): ((SUM + O, 0), (SUM + F3, 2),),
    (GRAD, CROSS + 1): ((SUM + V, 0),),
    (GRAD, CROSS + 2): ((SUM + K, 0), (SUM + Q, 0),),
    (TAIL, 0): ((SUM + C0, 0), (SUM + C1, 0), (SUM + O, 1), (SUM + K, 1), (SUM + V, 1), (SUM + F0, 2), (SUM + F1, 2), (SUM + Q, 1), (SUM + C1, 1), (SUM + F2, 2),),
    (TAIL, 1): ((SUM + C0, 1), (SUM + F3, 3), (SUM + Q, 2), (SUM + F1, 3), (SUM + K, 2), (SUM + F2, 3), (SUM + C0, 2), (SUM + O, 2), (SUM + Q, 3), (SUM + C1, 2),),
}


class ScatterNorms(Stages):
    def __init__(self, link, place):
        super().__init__(link, (1, 1, 1, NZ - 1))
        self.p = place

    def copies(self, stage):
        p, r, send, keys = self.p, self.link.r, self.link.send, self.keys[stage]
        if stage == 0:
            return [send(keys[0], r.g_norm, r.n_box0, p.peer("core"))]
        if stage == 1:
            return [send(keys[0], r.n_box0, r.n_box1, p.peer("y"))]
        if stage == 2:
            return [send(keys[0], r.n_box1.at[:, 1 - p.b], r.n_box2, p.peer("x"))]
        return [
            send(keys[k - 1], r.n_box2.at[p.up(k)], r.n_box3.at[k - 1], p.peer("z", k))
            for k in range(1, NZ)
        ]

    def step(self, stage):
        p, r = self.p, self.link.r
        self.wait(stage)
        if stage == 0:
            r.n_box0[...] = r.g_norm[...] + r.n_box0[...]
        elif stage == 1:
            r.n_box1[...] = r.n_box0[...] + r.n_box1[...]
        else:
            r.n_box2[...] = r.n_box1[:, p.b] + r.n_box2[...]
        self.start(stage + 1)

    def total(self):
        r = self.link.r
        return r.n_box2[self.p.a] + ((r.n_box3[0] + r.n_box3[1]) + r.n_box3[2])


class ScatterEncoder(Stages):
    def __init__(self, link, place, share, micro):
        super().__init__(link, (NY * micro, micro))
        self.p, self.share, self.micro = place, share, micro
        self.boxes = (link.r.d_third, link.r.second_low)

    def rows(self, m, y, c):
        at = pl.multiple_of((y * NC + c) * self.share, self.share)
        return self.link.r.big1.at[m, pl.ds(at, self.share), :]

    def one(self, stage, m):
        p, r, send = self.p, self.link.r, self.link.send
        key = self.keys[stage][0]
        if stage == 0:
            return [
                send(
                    key + NY * m + y,
                    self.rows(m, y, 1 - p.c),
                    self.boxes[y].at[m],
                    p.peer("core"),
                )
                for y in range(NY)
            ]
        return [send(key + m, self.rows(m, 1 - p.y, p.c), r.e_box1.at[m], p.peer("y"))]

    def copies(self, stage):
        return [copy for m in range(self.micro) for copy in self.one(stage, m)]

    def begin(self, m):
        for copy in self.one(0, m):
            copy.start()

    def step(self, m):
        for copy in self.one(0, m):
            copy.wait_recv()
        for y in range(NY):
            ref = self.rows(m, y, self.p.c)
            ref[...] = ref[...] + self.boxes[y][m]
        for copy in self.one(1, m):
            copy.start()

    def finish(self):
        self.wait(1)
        for m in range(self.micro):
            ref = self.rows(m, self.p.y, self.p.c)
            ref[...] = ref[...] + self.link.r.e_box1[m]


class EncoderPart:
    def __init__(self, rows, m):
        self.rows, self.m = rows, m

    def turn(self, stage):
        self.rows.step(self.m)


class ShareFfn(Stages):
    def __init__(self, link, place, box, first, item):
        super().__init__(link, (3,))
        self.p, self.box, self.first, self.item = place, box, first, item

    def copies(self, stage):
        p, send, keys = self.p, self.link.send, self.keys[0]
        ref = self.box.at[p.t, pl.ds(self.first, self.item.count)]
        axes = ("core", "y", "both")
        return [send(keys[i], ref, ref, p.peer(axes[i])) for i in range(3)]

    def go(self):
        self.item.last()
        for k in range(self.item.count):
            self.box[self.p.t, self.first + k] = self.item.total(k).astype(BF16)
        self.start(0)


def each(count, body, ticks=None):
    def step(i, carry):
        for k, tick in (ticks or {}).items():
            pl.when(i == k)(tick)
        body(i)
        return carry

    lax.fori_loop(0, count, step, 0)


SEMS = 180


def layer_kernel(names, groups, scale, *refs):
    r = Refs()
    for name, ref in zip(names, refs):
        setattr(r, name, ref)
    micro, r.share = r.stream.shape[0], r.stream.shape[1]
    r.slots = r.share // SLOT
    r.quads = r.stream.shape[2] // QUAD
    r.enc_len = r.encoder.shape[1]
    r.frame = frame_rows(r.share)
    r.halves = micro // PIECE
    p = Place(groups)
    link = Link(r)

    mine = pl.ds(pl.multiple_of(p.t * r.share, r.share), r.share)
    half = pl.ds(pl.multiple_of(p.t * (r.share // 2), r.share // 2), r.share // 2)
    pairs = [
        (r.self_query, r.w.at[SELF, p.y, p.c, p.a1, p.a0, p.b]),
        (r.self_key_value, r.w.at[pl.ds(SELF + 1, 2), p.y, p.c, p.a1, p.a0, p.b]),
        (r.cross_query, r.w.at[CROSS, p.y, p.c, p.a1, p.a0, p.b]),
        (r.cross_key_value, r.w.at[pl.ds(CROSS + 1, 2), p.y, p.c, p.a1, p.a0, p.b]),
        (r.self_output, r.w.at[SELF + 3, p.y, p.c, p.a1, p.a0, p.b]),
        (r.cross_output, r.w.at[CROSS + 3, p.y, p.c, p.a1, p.a0, p.b]),
    ]
    down = pl.ds(pl.multiple_of(p.t * 128, 128), 128)
    for j in range(4):
        pairs.append(
            (
                r.ffn_out.at[pl.ds(j * 64, 64), down],
                r.w.at[FEED + 2 * j + 1, p.y, p.c, p.a1, p.a0, p.b],
            )
        )
    up = pl.ds(pl.multiple_of(p.t * 512, 512), 512)
    pairs.append((r.ffn_in.at[:, up], r.own_up))
    weights = len(pairs)
    pairs += [
        (r.stream_hbm.at[:, mine, :], r.stream),
        (r.context_hbm.at[:, mine, :], r.context),
        (r.masks_hbm.at[:, half, :], r.masks),
        (r.encoder, r.big1),
        (r.out_grad, r.cotangent),
    ]
    copies = [
        pltpu.make_async_copy(source, target, r.sems.at[i])
        for i, (source, target) in enumerate(pairs)
    ]
    partners = [p.peer("z", k) for k in range(1, NZ)]
    partners += [p.peer(axis) for axis in ("x", "y", "core", "both")]
    partners.append(p.device(b=1 - p.b, y=1 - p.y))
    barrier = pltpu.get_barrier_semaphore()
    for device in partners:
        pl.semaphore_signal(barrier, inc=1, device_id=device, device_id_type=MESH)
    for copy in copies[:weights]:
        copy.start()
    r.pack[p.a, p.b, 0:3, :64] = r.norm_gain[...].astype(F32)
    r.pack[p.a, p.b, 3:6, :64] = r.norm_bias[...].astype(F32)
    for copy in copies[:weights]:
        copy.wait()
    for j in range(4):
        at = j * 64
        r.w[FEED + 2 * j, p.y, p.c, p.a1, p.a0, p.b] = jnp.concatenate(
            [r.own_up[:, at : at + 64], r.own_up[:, 256 + at : 320 + at]], axis=1
        )
    pl.semaphore_wait(barrier, len(partners))
    for copy in copies[weights:]:
        copy.start()

    chains = {name: Gather(link, p, *spec) for name, spec in GATHERS.items()}
    norms = GatherNorms(link, p)

    def run(phase, step):
        for name, stage in PLAN.get((phase, step), ()):
            if stage < 0:
                chains[name].start(0)
            else:
                chains[name].turn(stage)

    def loop(phase, count, body, needs=None):
        ticks = {}
        for i in range(count):
            names = (needs or {}).get(i, ())
            if PLAN.get((phase, i)) or names:

                def tick(i=i, names=names):
                    run(phase, i)
                    for name in names:
                        chains[name].last()

                ticks[i] = tick
        each(count, functools.partial(body, r), ticks)

    r.sums[...] = jnp.zeros(r.sums.shape, F32)
    run(START, 0)
    norms.start(0)
    run(START, 1)
    for copy in copies[weights:]:
        copy.wait()
    run(START, 2)
    norms.wait(0)
    norms.start(1)
    for name in (Q, K, V):
        chains[name].last()
    loop(SELF_FORWARD, micro, forward_self)
    norms.wait(1)
    r.norms[...] = jnp.concatenate(
        [r.pack[d // NX, d % NX, :, :64] for d in range(NZ * NX)], axis=1
    )
    loop(NORM_FORWARD, micro, first_norm, {0: (O,)})
    loop(CROSS_FORWARD, micro, forward_cross, {0: (C0, C1)})
    loop(FEED_FORWARD, 4 * r.halves, feed, {j * r.halves: (F0 + j,) for j in range(4)})
    for item in link.all:
        item.drain()
    link.all = []
    each(micro, functools.partial(third_norm, r))
    out = [pltpu.make_async_copy(r.d_first, r.block_out, r.sems.at[0])]
    out[0].start()

    sums = {}
    for name, spec in SCATTERS.items():
        boxes = [getattr(r, box_name(name, i)) for i in range(1 + len(spec[2]))]
        sums[name] = Scatter(link, p, *spec, boxes)
        if name >= F0:
            sums[name].share = ShareFfn(link, p, r.all_ffn, 2 * (name - F0), sums[name])
    norm_sums = ScatterNorms(link, p)
    rows = ScatterEncoder(link, p, r.share, micro)
    chains = {SUM + name: item for name, item in sums.items()}
    for m in range(micro):
        chains[ROWS + m] = EncoderPart(rows, m)

    def feed_both(j):
        for i in range(4):
            pl.when(j == i)(functools.partial(run, FEED_BACK, i))
        feed_back(r, j)
        for i in range(4):
            pl.when(j == i)(functools.partial(run, FEED_GRAD, i))
        feed_grad(r, j)
        for i in range(4):
            pl.when(j == i)(functools.partial(sums[F0 + i].start, 0))

    each(4, feed_both)
    run(NORM_BACK, 0)
    each(micro, functools.partial(second_back, r))
    clear_pads(r)
    out[0].wait()

    def cross_back(r, m):
        backward_cross(r, m)
        rows.begin(m)

    loop(CROSS_BACK, micro, cross_back)
    for d in range(NZ * NX):
        r.g_norm[d // NX, d % NX] = jnp.zeros(r.g_norm.shape[2:], F32)
        r.g_norm[d // NX, d % NX, :, :64] = r.sums[:, d * 64 : (d + 1) * 64]
    norm_sums.start(0)

    def grad(kind):
        run(GRAD, kind)
        weight_grad(r, kind)

    def cross_grads(pair):
        for k in (2 * pair, 2 * pair + 1):
            grad(CROSS + k)
        sums[C0 + pair].start(0)

    for pair in range(2 - LATE):
        cross_grads(pair)
    grad(SELF + 3)
    sums[O].start(0)
    norm_sums.step(0)
    loop(SELF_BACK, micro, backward_self)
    out = [
        pltpu.make_async_copy(r.cotangent, r.stream_grad, r.sems.at[0]),
        pltpu.make_async_copy(r.second_low, r.context_grad, r.sems.at[1]),
    ]
    for copy in out:
        copy.start()
    for name, kind in ((V, SELF + 2), (Q, SELF), (K, SELF + 1)):
        grad(kind)
        sums[name].start(0)
    for pair in range(2 - LATE, 2):
        cross_grads(pair)
    run(TAIL, 0)
    norm_sums.step(1)
    run(TAIL, 1)
    norm_sums.step(2)
    rows.finish()
    mine = pl.ds(pl.multiple_of(p.t * r.share, r.share), r.share)
    out.append(pltpu.make_async_copy(r.big1.at[:, mine, :], r.encoder_grad, r.sems.at[2]))
    out[2].start()
    for j in range(4):
        sums[F0 + j].share.wait(0)
    for t in range(NY * NC):
        halves = [
            r.all_ffn[t, 2 * j, :, h * 64 : (h + 1) * 64] for h in range(2) for j in range(4)
        ]
        r.grad_ffn_in[:, t * 512 : (t + 1) * 512] = (
            jnp.concatenate(halves, axis=1).astype(F32) * scale
        )
        for j in range(4):
            r.grad_ffn_out[j * 64 : (j + 1) * 64, t * 128 : (t + 1) * 128] = (
                r.all_ffn[t, 2 * j + 1].astype(F32) * scale
            )
    norm_sums.wait(3)
    total = norm_sums.total() * scale
    r.grad_norm_gain[...] = total[0:3, :64]
    r.grad_norm_bias[...] = total[3:6, :64]
    for name in (C0, C1, O, Q, K, V):
        sums[name].last()
    r.grad_cross_query[...] = sums[C0].total(0) * scale
    r.grad_cross_key_value[0] = sums[C0].total(1) * scale
    r.grad_cross_key_value[1] = sums[C1].total(0) * scale
    r.grad_cross_output[...] = sums[C1].total(1) * scale
    r.grad_self_output[...] = sums[O].total(0) * scale
    r.grad_self_query[...] = sums[Q].total(0) * scale
    r.grad_self_key_value[0] = sums[K].total(0) * scale
    r.grad_self_key_value[1] = sums[V].total(0) * scale
    for item in link.all:
        item.drain()
    for copy in out:
        copy.wait()


def vmem():
    return pl.BlockSpec(memory_space=pltpu.VMEM)


def hbm():
    return pl.BlockSpec(memory_space=pl.ANY)


WEIGHTS = (
    "self_query", "self_key_value", "self_output",
    "cross_query", "cross_key_value", "cross_output",
    "ffn_in", "ffn_out", "norm_gain", "norm_bias",
)


def layer(groups, scale, stream, context, encoder, masks, table, out_grad, weights):
    micro, row, width = stream.shape
    share = out_grad.shape[1]
    enc_len = encoder.shape[1]
    frame, wide = frame_rows(share), window_rows()
    slots, quads = share // SLOT, width // QUAD
    small = ("norm_gain", "norm_bias")
    ins = [
        ("stream_hbm", stream, hbm()),
        ("context_hbm", context, hbm()),
        ("encoder", encoder, hbm()),
        ("masks_hbm", masks, hbm()),
        ("table", table, pl.BlockSpec(memory_space=pltpu.SMEM)),
        ("out_grad", out_grad, hbm()),
    ]
    for name, value in zip(WEIGHTS, weights):
        ins.append((name, value, vmem() if name in small else hbm()))
    part = jax.ShapeDtypeStruct((micro, share, width), BF16)
    outs = [
        ("block_out", part, hbm()),
        ("stream_grad", part, hbm()),
        ("context_grad", part, hbm()),
        ("encoder_grad", part, hbm()),
    ]
    for name, value in zip(WEIGHTS, weights):
        outs.append(("grad_" + name, jax.ShapeDtypeStruct(value.shape, F32), vmem()))
    low = pltpu.VMEM((micro, share, width), BF16)
    high = pltpu.VMEM((micro, share, width), F32)
    window = pltpu.VMEM((micro, frame, width), BF16)
    big = pltpu.VMEM((micro, enc_len, width), BF16)
    norm = pltpu.VMEM((NZ, NX, 8, 128), F32)
    scratch = [
        ("w", pltpu.VMEM((KINDS, NY, NC, NZ // 2, 2, NX, 64, 128), BF16)),
        ("g_ffn", pltpu.VMEM((8, NY, NC, NZ // 2, 2, NX, 64, 128), BF16)),
        ("stream", low),
        ("context", low),
        ("cotangent", low),
        ("masks", pltpu.VMEM((micro, share // 2, 128), jnp.int32)),
        ("q_self", low),
        ("k_self", low),
        ("v_self", low),
        ("mixed_self", low),
        ("first_low", low),
        ("q_cross", low),
        ("k_cross", window),
        ("v_cross", window),
        ("source", window),
        ("mixed_cross", low),
        ("second_low", low),
        ("d_third", low),
        ("d_second", low),
        ("d_first", low),
        ("p_self", pltpu.VMEM((micro, slots, quads, SLOT, QUAD), BF16)),
        ("p_cross", pltpu.VMEM((micro, slots, quads, wide, QUAD), BF16)),
        ("residual", high),
        ("normed1", low),
        ("normed2", low),
        ("factor", pltpu.VMEM((micro, share, 2), F32)),
        ("big1", big),
        ("big2", big),
        ("own_up", pltpu.VMEM((64, 512), BF16)),
        ("norms", pltpu.VMEM((8, width), F32)),
        ("sums", pltpu.VMEM((8, width), F32)),
        ("pack", norm),
        ("g_norm", norm),
        ("n_box0", norm),
        ("n_box1", norm),
        ("n_box2", pltpu.VMEM((NZ, 8, 128), F32)),
        ("n_box3", pltpu.VMEM((NZ - 1, 8, 128), F32)),
        ("e_box1", low),
        ("all_ffn", pltpu.VMEM((NY * NC, 8, 64, 128), BF16)),
        ("sems", pltpu.SemaphoreType.DMA((19,))),
        ("send_sems", pltpu.SemaphoreType.DMA((SEMS,))),
        ("recv_sems", pltpu.SemaphoreType.DMA((SEMS,))),
    ]
    for name, (_, count, order) in SCATTERS.items():
        scratch += scatter_boxes(name, count, order)
    names = [item[0] for item in ins + outs + scratch]
    return pl.pallas_call(
        functools.partial(layer_kernel, names, groups, scale),
        out_shape=[item[1] for item in outs],
        in_specs=[item[2] for item in ins],
        out_specs=[item[2] for item in outs],
        scratch_shapes=[item[1] for item in scratch],
        compiler_params=pltpu.CompilerParams(
            vmem_limit_bytes=VMEM_LIMIT, collective_id=0, has_side_effects=True
        ),
        cost_estimate=pl.CostEstimate(
            flops=30_000_000_000, bytes_accessed=30_000_000, transcendentals=4_000_000
        ),
    )(*[item[1] for item in ins])


def copy_kernel(count, *refs):
    given, results, held = (refs[i * count : (i + 1) * count] for i in range(3))
    sems = refs[3 * count]
    loads = [pltpu.make_async_copy(a, b, sems.at[0, i]) for i, (a, b) in enumerate(zip(given, held))]
    stores = [
        pltpu.make_async_copy(a, b, sems.at[1, i]) for i, (a, b) in enumerate(zip(held, results))
    ]
    for load in loads:
        load.start()
    for load, store in zip(loads, stores):
        load.wait()
        store.start()
    for store in stores:
        store.wait()


def copy_all(values):
    count = len(values)
    return pl.pallas_call(
        functools.partial(copy_kernel, count),
        out_shape=[jax.ShapeDtypeStruct(v.shape, v.dtype) for v in values],
        in_specs=[hbm()] * count,
        out_specs=[hbm()] * count,
        scratch_shapes=[pltpu.VMEM(v.shape, v.dtype) for v in values]
        + [pltpu.SemaphoreType.DMA((2, count))],
        compiler_params=pltpu.CompilerParams(vmem_limit_bytes=VMEM_LIMIT),
    )(*values)


GATHER_DIM = (0, 1, 0, 0, 1, 0, 0, 0, 1, 1)


def per_device(
    query_stream,
    context_stream,
    encoder_out,
    query_masks,
    source_segments,
    out_grad,
    *weights,
):
    micro, row, width = query_stream.shape
    share = out_grad.shape[1]
    slots = share // SLOT
    t = lax.axis_index(TENSOR)
    replicas = lax.axis_size(DP)
    scale = float(micro * row * replicas) ** (-0.5)
    groups = replicas // (NZ * NX)
    weights = [item.T if i in (2, 5) else item for i, item in enumerate(weights)]
    near = [[i * groups + j for j in range(groups)] for i in range(NZ * NX)]
    if groups > 1:
        weights = [
            lax.all_gather(item, DP, axis=dim, tiled=True, axis_index_groups=near)
            for item, dim in zip(weights, GATHER_DIM)
        ]
    bounds = t * slots + jnp.arange(slots + 1, dtype=jnp.int32)
    starts = jnp.sum(
        (source_segments < bounds[None, :, None]).astype(jnp.int32), axis=-1
    )
    table = window_table(starts, share, encoder_out.shape[1])
    results = layer(
        groups, scale, query_stream, context_stream, encoder_out, query_masks, table,
        out_grad, weights,
    )
    results = copy_all(results)
    grads = results[4:]
    if groups > 1:
        grads = [
            lax.psum_scatter(
                item, DP, scatter_dimension=dim, tiled=True, axis_index_groups=near
            )
            for item, dim in zip(grads, GATHER_DIM)
        ]
    grads = [item.T if i in (2, 5) else item for i, item in enumerate(grads)]
    return (*results[:4], *grads)


def solution(mesh):
    in_specs = (
        P(None, DP, None),
        P(None, DP, None),
        P(None, DP, None),
        P(None, DP, None),
        P(None, DP, None),
        P(None, (DP, TENSOR), None),
        P(DP, TENSOR),
        P(None, DP, TENSOR),
        P(TENSOR, DP),
        P(DP, TENSOR),
        P(None, DP, TENSOR),
        P(TENSOR, DP),
        P(DP, None),
        P(DP, None),
        P(None, DP),
        P(None, DP),
    )
    out_specs = (
        P(None, (DP, TENSOR), None),
        P(None, (DP, TENSOR), None),
        P(None, (DP, TENSOR), None),
        P(None, (DP, TENSOR), None),
        P(DP, TENSOR),
        P(None, DP, TENSOR),
        P(TENSOR, DP),
        P(DP, TENSOR),
        P(None, DP, TENSOR),
        P(TENSOR, DP),
        P(DP, None),
        P(DP, None),
        P(None, DP),
        P(None, DP),
    )
    return jax.shard_map(
        per_device, mesh=mesh, in_specs=in_specs, out_specs=out_specs, check_vma=False
    )
```
